32 devices in a mesh: side: 2 (over x), dp: 16 (over z, y, core).
Axes of the slice: x: 2, y: 2, z: 4, core: 2. Of those that a mesh axis runs over, the one named last changes fastest.
Arguments:
- decoder_in: bfloat16 [32, 512, 768], P(('side', 'dp')), may hold values from -6 to 6
- encoder_out: bfloat16 [32, 1024, 768], P(('side', 'dp')), may hold values from -6 to 6
- segment_ids: int32 [32, 512], P(('side', 'dp')), may hold values from 0 to 7, never falling along the last dimension, each value on 1 to 256 neighbouring positions
- cotangent: float32 [32, 512, 768], P(('side', 'dp')), may hold values from -6 to 6
- attn_master: float32 [6144, 768], P(('side', 'dp'))
- ffn_master: float32 [6144, 768], P(('side', 'dp'))
- small_master: float32 [17, 768], replicated
- attn_moment: float32 [6144, 768], P(('side', 'dp')), may hold values from -384 to 384
- ffn_moment: float32 [6144, 768], P(('side', 'dp')), may hold values from -384 to 384
- small_moment: float32 [17, 768], replicated, may hold values from -384 to 384
- attn_average: float32 [6144, 768], P(('side', 'dp')), may hold values from -0.5 to 0.5
- ffn_average: float32 [6144, 768], P(('side', 'dp')), may hold values from -0.5 to 0.5
- small_average: float32 [17, 768], replicated, may hold values from -6 to 6
- rate_matrix: float32 [], replicated, may hold values from 8.457279e-05 to 0.00016914558
- rate_vector: float32 [], replicated, may hold values from 0.00078125 to 0.00234375
Outputs:
- layer_out: float32 [32, 512, 768], P(('side', 'dp'))
- input_grad: float32 [32, 512, 768], P(('side', 'dp'))
- encoder_grad: float32 [32, 1024, 768], P(('side', 'dp'))
- attn_grad: float32 [6144, 768], P(('side', 'dp'))
- ffn_grad: float32 [6144, 768], P(('side', 'dp'))
- small_grad: float32 [17, 768], replicated
- attn_new: float32 [6144, 768], P(('side', 'dp'))
- ffn_new: float32 [6144, 768], P(('side', 'dp'))
- small_new: float32 [17, 768], replicated
- attn_moment_new: float32 [6144, 768], P(('side', 'dp'))
- ffn_moment_new: float32 [6144, 768], P(('side', 'dp'))
- small_moment_new: float32 [17, 768], replicated
- attn_average_new: float32 [6144, 768], P(('side', 'dp'))
- ffn_average_new: float32 [6144, 768], P(('side', 'dp'))
- small_average_new: float32 [17, 768], replicated
The draws below stay inside these ranges and needn't reach their ends.
Inputs may be any that keep to these rules, and one draw needn't show every extreme that they name: `segment_ids`: along each row the ids never fall; each segment holds 1 to 256 positions, one exactly 256.
All inputs are finite; a program needn't handle non-finite values.
Results may differ from the reference program's by a relative error of at most 0.024.
The reference program's roundings to bfloat16 on the way count: a program that leaves them out, or rounds other values in their place, can miss the bound.
Values may be sent and summed in bfloat16 or wider, within the bound.
A program may use at most 192 MiB of HBM per device.

```python
import math
import jax
import jax.numpy as jnp
import numpy as np
from jax import lax

D = 768
HEADS = 12
HEAD_DIM = 64
FF = 3072
LEN = 512
ELEN = 1024
SEGS = 8
SEQS = 32
ALL_TOKENS = 16384
VECS = 17


def draw_attn_master(key, part):
    key = jax.random.fold_in(key, 11)
    base = jax.random.normal(key, (8 * D, D), jnp.float32)
    factors = jnp.array([1.3, 1.3, 1.0, 4.0, 1.3, 1.3, 1.0, 6.0], jnp.float32)
    return base * jnp.repeat(factors, D)[:, None] * D ** (-0.5)


def draw_ffn_master(key, part):
    key = jax.random.fold_in(key, 23)
    base = jax.random.normal(key, (2 * FF, D), jnp.float32)
    row_ids = jnp.arange(2 * FF)
    factor = jnp.where(row_ids < FF, D ** (-0.5), 2.0 * FF ** (-0.5))
    return base * factor[:, None]


def draw_small_master(key, part):
    key = jax.random.fold_in(key, 37)
    base = 0.3 * jax.random.normal(key, (VECS, D), jnp.float32)
    row_ids = jnp.arange(VECS)
    is_gain = (row_ids == 7) | (row_ids == 9) | (row_ids == 11)
    return base * jnp.where(is_gain, 0.33, 1.0)[:, None] + jnp.where(is_gain, 1.0, 0.0)[:, None]


def level_of(own_key, shape, shards, low, high):
    factor_of, own = 1.0, jax.random.fold_in(own_key, 6)
    for dim, shards_of in shards:
        heights = jnp.exp(jax.random.uniform(jax.random.fold_in(own, dim), (shards_of,), jnp.float32, low / len(shards), high / len(shards)))
        factor_of = factor_of * jnp.repeat(heights, shape[dim] // shards_of).reshape([-1 if axis == dim else 1 for axis in range(len(shape))])
    return factor_of


def profile(number_of, total, limit, skew):
    portions = [(1 << 20) // math.isqrt(grade ** skew) + 1 for grade in range(2, number_of + 1)]
    spare, counts = total - limit - (number_of - 1), [1] * (number_of - 1)
    while spare > 0:
        candidates = [i for i in range(number_of - 1) if counts[i] < limit]
        mass, budget = sum([portions[i] for i in candidates]), spare
        for i in candidates:
            addition = min(limit - counts[i], max(1, budget * portions[i] // mass), spare)
            counts[i] = counts[i] + addition
            spare = spare - addition
    return np.array([limit] + counts)


def uneven_parts(key, amount, total, limit, skew):
    if amount == 2:
        one = jax.random.randint(key, (), max(1, total - limit), min(limit, total - 1) + 1)
        return jnp.stack([one, total - one])
    sizes = jnp.asarray(profile(amount, total, limit, skew), jnp.int32)
    pairs = (amount - 1) // 2
    giver, receiver = sizes[1:1 + 2 * pairs:2], sizes[2:2 + 2 * pairs:2]
    room = jnp.minimum(giver - 1, limit - receiver)
    moved = jax.random.randint(jax.random.fold_in(key, 1), (pairs,), 0, 1 << 20) % (room + 1)
    sizes = sizes.at[1:1 + 2 * pairs:2].set(giver - moved).at[2:2 + 2 * pairs:2].set(receiver + moved)
    return sizes[jax.random.permutation(jax.random.fold_in(key, 2), amount)]


def noise(stream_key, shape, scale, reach, split=(), dtype=jnp.bfloat16):
    factor_of = level_of(stream_key, shape, split, -0.22, 0.18) if split else 1.0
    values = jax.random.normal(stream_key, shape, jnp.float32) * scale * factor_of
    return jnp.minimum(jnp.maximum(values, -reach), reach).astype(dtype)


def setup_inputs(seed: int = 0) -> dict:
    keys = jax.random.split(jax.random.key(seed), 16)
    return {
        "decoder_in": noise(keys[0], (SEQS, LEN, D), 1.0, 6.0, ((0, 32),)),
        "encoder_out": noise(keys[1], (SEQS, ELEN, D), 1.0, 6.0, ((0, 32),)),
        "segment_ids": jax.vmap(lambda own: jnp.searchsorted(jnp.cumsum(uneven_parts(own, SEGS, LEN, LEN // 2, 0)), jnp.arange(LEN), side="right"))(jax.random.split(keys[2], SEQS)).reshape((SEQS, LEN)).astype(jnp.int32),
        "cotangent": noise(keys[3], (SEQS, LEN, D), 1.0, 6.0, ((0, 32),), jnp.float32),
        "attn_master": draw_attn_master(jax.random.fold_in(keys[15], 71), 0),
        "ffn_master": draw_ffn_master(jax.random.fold_in(keys[15], 71), 0),
        "small_master": draw_small_master(jax.random.fold_in(keys[15], 71), 0),
        "attn_moment": noise(keys[7], (8 * D, D), (0.5 * ALL_TOKENS ** 0.5), 384.0, ((0, 32),), jnp.float32),
        "ffn_moment": noise(keys[8], (2 * FF, D), (0.5 * ALL_TOKENS ** 0.5), 384.0, ((0, 32),), jnp.float32),
        "small_moment": noise(keys[9], (VECS, D), (0.5 * ALL_TOKENS ** 0.5), 384.0, (), jnp.float32),
        "attn_average": noise(keys[10], (8 * D, D), (D ** -0.5), 0.5, ((0, 32),), jnp.float32),
        "ffn_average": noise(keys[11], (2 * FF, D), (D ** -0.5), 0.5, ((0, 32),), jnp.float32),
        "small_average": noise(keys[12], (VECS, D), 0.5, 6.0, (), jnp.float32),
        "rate_matrix": jnp.clip(jax.random.uniform(keys[13], (), jnp.float32, 8.457279182039201e-05, 0.00016914558), 8.457279182039201e-05, 0.00016914558),
        "rate_vector": jnp.clip(jax.random.uniform(keys[14], (), jnp.float32, 0.00078125, 0.00234375), 0.00078125, 0.00234375),
    }


NEG_FILL = -1e+30
EPSILON = 1e-05
MOMENTUM = 0.5
AVG_DECAY = 0.5

@jax.custom_vjp
def low(v):
    return lax.optimization_barrier(v.astype(jnp.bfloat16)).astype(jnp.float32)

@jax.custom_vjp
def low_back(v):
    return v

def low_keep(v):
    return (low(v), None)

def low_pass(kept, grad):
    return (grad,)

def back_keep(v):
    return (v, None)

def back_low(kept, grad):
    return (low(grad),)
low.defvjp(low_keep, low_pass)
low_back.defvjp(back_keep, back_low)

def precise_dot(left_op, right_op):
    return jnp.dot(left_op, right_op, precision=lax.Precision.HIGHEST)

def layer_norm(residual, norm_gain, norm_shift):
    row_mean = lax.optimization_barrier(jnp.mean(residual, axis=-1, keepdims=True))
    centered = residual - row_mean
    row_var = lax.optimization_barrier(jnp.mean(centered * centered, axis=-1, keepdims=True))
    return centered * lax.rsqrt(row_var + EPSILON) * norm_gain + norm_shift

def attend(queries, keys_in, values_in, allowed):
    q_heads = queries.reshape(queries.shape[0], HEADS, HEAD_DIM)
    k_heads = keys_in.reshape(keys_in.shape[0], HEADS, HEAD_DIM)
    v_heads = values_in.reshape(values_in.shape[0], HEADS, HEAD_DIM)
    scores = low_back(jnp.einsum('qhd,khd->hqk', q_heads, k_heads, precision=lax.Precision.HIGHEST))
    if allowed is not None:
        scores = jnp.where(allowed[None], scores, NEG_FILL)
    row_max = lax.optimization_barrier(jnp.max(scores, axis=-1, keepdims=True))
    exp_scores = jnp.exp(scores - row_max)
    attn_prob = low(exp_scores / lax.optimization_barrier(jnp.sum(exp_scores, axis=-1, keepdims=True)))
    mixed = jnp.einsum('hqk,khd->qhd', attn_prob, v_heads, precision=lax.Precision.HIGHEST)
    return mixed.reshape(queries.shape[0], HEADS * HEAD_DIM)

def decode_row(dec_row, enc_row, seg_row, matrices, ffn_all, vectors):
    model_width = HEADS * HEAD_DIM
    blocks = [matrices[block_index * model_width:(block_index + 1) * model_width] for block_index in range(8)]
    w_query, w_key, w_value, w_proj, c_query, c_key, c_value, c_proj = blocks
    w_in = ffn_all[:FF]
    w_out = ffn_all[FF:]
    scale = 1.0 / math.sqrt(HEAD_DIM)
    positions = jnp.arange(LEN)
    allowed = (positions[None, :] <= positions[:, None]) & (seg_row[None, :] == seg_row[:, None])
    queries = low(low_back((precise_dot(dec_row, w_query) + vectors[0]) * scale))
    keys_self = low(low_back(precise_dot(dec_row, w_key)))
    vals_self = low(low_back(precise_dot(dec_row, w_value) + vectors[1]))
    mixed_self = low(low_back(attend(queries, keys_self, vals_self, allowed)))
    self_out = low_back(precise_dot(mixed_self, w_proj) + vectors[2])
    hidden_one = layer_norm(dec_row + self_out, vectors[7], vectors[8])
    hidden_one_low = low(hidden_one)
    cross_q = low(low_back((precise_dot(hidden_one_low, c_query) + vectors[3]) * scale))
    cross_k = low(low_back(precise_dot(enc_row, c_key)))
    cross_v = low(low_back(precise_dot(enc_row, c_value) + vectors[4]))
    mixed_cross = low(low_back(attend(cross_q, cross_k, cross_v, None)))
    cross_out = low_back(precise_dot(mixed_cross, c_proj) + vectors[5])
    hidden_two = layer_norm(hidden_one + cross_out, vectors[9], vectors[10])
    hidden_two_low = low(hidden_two)
    bias_in = vectors[13:].reshape(FF)
    pre_act = low_back(precise_dot(hidden_two_low, w_in.T) + bias_in)
    act_low = low(jax.nn.gelu(pre_act, approximate=False))
    ffn_out = low_back(precise_dot(act_low, w_out) + vectors[6])
    return layer_norm(hidden_two + ffn_out, vectors[11], vectors[12])

def nesterov(master, moment, average, grad, rate):
    new_moment = MOMENTUM * moment + grad
    new_master = master - rate * (grad + MOMENTUM * new_moment)
    new_average = AVG_DECAY * average + (1.0 - AVG_DECAY) * new_master
    return (new_master, new_moment, new_average)

def reference(decoder_in, encoder_out, segment_ids, cotangent, attn_master, ffn_master, small_master, attn_moment, ffn_moment, small_moment, attn_average, ffn_average, small_average, rate_matrix, rate_vector):
    dec_full = decoder_in.astype(jnp.float32)
    enc_paired = jnp.roll(encoder_out.astype(jnp.float32), SEQS // 2, axis=0)

    def forward(dec_vals, enc_vals, attn_vals, ffn_vals, small_vals):
        matrices = low(attn_vals)
        ffn_all = low(ffn_vals)

        def one_row(row_items):
            return decode_row(row_items[0], row_items[1], row_items[2], matrices, ffn_all, small_vals)
        return lax.map(jax.checkpoint(one_row), (dec_vals, enc_vals, segment_ids))
    layer_out, pull = jax.vjp(forward, dec_full, enc_paired, attn_master, ffn_master, small_master)
    input_grad, enc_grad_paired, attn_grad, ffn_grad, small_grad = pull(cotangent)
    encoder_grad = jnp.roll(enc_grad_paired, SEQS // 2, axis=0)
    attn_new, attn_moment_new, attn_average_new = nesterov(attn_master, attn_moment, attn_average, attn_grad, rate_matrix)
    ffn_new, ffn_moment_new, ffn_average_new = nesterov(ffn_master, ffn_moment, ffn_average, ffn_grad, rate_matrix)
    small_new, small_moment_new, small_average_new = nesterov(small_master, small_moment, small_average, small_grad, rate_vector)
    return (layer_out, input_grad, encoder_grad, attn_grad, ffn_grad, small_grad, attn_new, ffn_new, small_new, attn_moment_new, ffn_moment_new, small_moment_new, attn_average_new, ffn_average_new, small_average_new)
```

```python
import functools
import math

import jax
import jax.numpy as jnp
from jax import lax
from jax.experimental import pallas as pl
from jax.experimental.pallas import tpu as pltpu
from jax.sharding import PartitionSpec as P

HEADS = 12
HEAD_DIM = 64


NEG_FILL = -1e30
EPSILON = 1e-05
MOMENTUM = 0.5
AVG_DECAY = 0.5


MESH_ID = pl.DeviceIdType.MESH
BF = jnp.bfloat16
F32 = jnp.float32
CUT = 512


class Net:
    def __init__(self, send_sems, recv_sems):
        self.s = lax.axis_index("side")
        self.d = lax.axis_index("dp")
        self.z, self.y, self.c = self.d // 4, (self.d // 2) % 2, self.d % 2
        self.depth = lax.axis_size("dp") // 4
        self.send_sems, self.recv_sems = send_sems, recv_sems
        self.sent, self.slots, self.conds = [], {}, []
        self.low = [self.z >= k for k in range(self.depth)]
        self.high = [self.z < self.depth - k for k in range(self.depth)]
        self.here = [self.z == k for k in range(self.depth)]
        self.away = [self.s != k for k in (0, 1)]
        self.home = [self.s == k for k in (0, 1)]

    def at(self, s=None, z=None, y=None, c=None):
        s, z, y, c = (own if got is None else got for got, own in ((s, self.s), (z, self.z), (y, self.y), (c, self.c)))
        return (s, (z * 2 + y) * 2 + c)

    def slot(self, key):
        return self.slots.setdefault(key, len(self.slots))

    def copy(self, src, dst, to, send_slot, recv_slot):
        return pltpu.make_async_remote_copy(
            src_ref=src,
            dst_ref=dst,
            send_sem=self.send_sems.at[send_slot],
            recv_sem=self.recv_sems.at[recv_slot],
            device_id=to,
            device_id_type=MESH_ID,
        )

    def send(self, src, dst, to, key, like):
        send_slot, recv_slot = len(self.sent), self.slot(key)
        self.copy(src, dst, to, send_slot, recv_slot).start()
        peer = (self.s, self.d)
        self.sent.append((lambda: self.copy(like(), like(), peer, send_slot, recv_slot).wait_send(), tuple(self.conds)))

    def recv(self, dst, key):
        self.copy(dst, dst, self.at(c=1 - self.c), 0, self.slot(key)).wait_recv()

    def when(self, cond, body):
        self.conds.append(cond)
        pl.when(cond)(body)
        self.conds.pop()

    def drain(self):
        assert max(len(self.sent), len(self.slots)) <= min(self.send_sems.shape[0], self.recv_sems.shape[0])
        for wait, conds in self.sent:
            for cond in conds:
                wait = functools.partial(pl.when(cond), wait)
            wait()

    def greet(self, others=()):
        barrier = pltpu.get_barrier_semaphore()
        partners = [self.at(s=1 - self.s), self.at(y=1 - self.y), self.at(c=1 - self.c), *others]
        for to in partners:
            pl.semaphore_signal(barrier, inc=1, device_id=to, device_id_type=MESH_ID)
        low, high = self.low[1], self.high[1]

        def signal(to):
            pl.semaphore_signal(barrier, inc=1, device_id=to, device_id_type=MESH_ID)

        pl.when(low)(lambda: signal(self.at(z=self.z - 1)))
        pl.when(high)(lambda: signal(self.at(z=self.z + 1)))
        pl.semaphore_wait(barrier, len(partners) + low.astype(jnp.int32) + high.astype(jnp.int32))


def gather_ticks(net, full, own, tag, placed):
    depth, width = net.depth, full.shape[-1]
    cols = {"A": pl.ds(0, CUT), "B": pl.ds(CUT, width - CUT)}
    coord = {"A": (net.s, net.y), "B": (net.y, net.s)}
    z, c = net.z, net.c

    def part(p, f, z_of, l, core):
        s, y = (f, l) if p == "A" else (l, f)
        return full.at[s, z_of, y, core, :, cols[p]]

    def pair(p, z_of, l, core):
        if p == "A":
            return full.at[:, z_of, l, core, :, cols[p]]
        return full.at[l, z_of, :, core, :, cols[p]]

    def dev(p, f, z_of, l, core):
        s, y = (f, l) if p == "A" else (l, f)
        return net.at(s, z_of, y, core)

    def spread(p, src, dst, ups, rel, f_rel):
        f, l = coord[p]
        like = lambda: full.at[0, 0, 0, 0, :, cols[p]]
        if ups != "down" and 1 - rel < depth:
            net.when(
                net.high[1],
                lambda: net.send(src, dst, dev(p, f, z + 1, l, c), (tag, p, "up", 1 - rel, f_rel), like),
            )
        if ups != "up" and 1 + rel < depth:
            net.when(
                net.low[1],
                lambda: net.send(src, dst, dev(p, f, z - 1, l, c), (tag, p, "down", 1 + rel, f_rel), like),
            )
        net.send(src, dst, dev(p, f, z, 1 - l, c), (tag, p, "l", rel, f_rel), like)

    def to_core(p, rel, l_rel):
        f, l = coord[p]
        l_of = l if l_rel == 0 else 1 - l
        both_f = pair(p, z + rel, l_of, c)
        net.send(both_f, both_f, net.at(c=1 - c), (tag, p, "core", rel, l_rel), lambda: pair(p, 0, 0, 0))

    def first(p):
        f, l = coord[p]
        src, dst = own.at[:, cols[p]], part(p, f, z, l, c)
        net.send(src, dst, dev(p, 1 - f, z, l, c), (tag, p, "f"), lambda: full.at[0, 0, 0, 0, :, cols[p]])
        spread(p, src, dst, "both", 0, 0)

    def second(p):
        f, l = coord[p]
        got = part(p, 1 - f, z, l, c)
        net.recv(got, (tag, p, "f"))
        spread(p, got, got, "both", 0, 1)
        to_core(p, 0, 0)

    def along(p, dist, f_rel, way):
        f, l = coord[p]
        rel = -dist if way == "up" else dist

        def body():
            got = part(p, f if f_rel == 0 else 1 - f, z + rel, l, c)
            net.recv(got, (tag, p, way, dist, f_rel))
            spread(p, got, got, way, rel, f_rel)
            if f_rel == 1:
                to_core(p, rel, 0)

        net.when(net.low[dist] if way == "up" else net.high[dist], body)

    def across(p, rel):
        f, l = coord[p]

        def body():
            for f_rel in (0, 1):
                net.recv(part(p, f if f_rel == 0 else 1 - f, z + rel, 1 - l, c), (tag, p, "l", rel, f_rel))
            to_core(p, rel, 1)

        if rel == 0:
            body()
        else:
            net.when(net.low[-rel] if rel < 0 else net.high[rel], body)

    def from_core(p, rel, l_rel):
        f, l = coord[p]
        body = lambda: net.recv(pair(p, z + rel, l if l_rel == 0 else 1 - l, 1 - c), (tag, p, "core", rel, l_rel))
        if rel == 0:
            body()
        else:
            net.when(net.low[-rel] if rel < 0 else net.high[rel], body)

    def both(fn, *args):
        return lambda: (fn("B", *args), fn("A", *args))

    ticks = [both(first), lambda: (placed(), second("B"), second("A"))]
    for dist in range(1, depth):
        for f_rel in (0, 1):
            ticks.append(lambda dist=dist, f_rel=f_rel: [along(p, dist, f_rel, way) for p in "BA" for way in ("up", "down")])
    for dist in range(depth):
        ticks.append(lambda dist=dist: [across(p, rel) for p in "BA" for rel in sorted({-dist, dist})])
    ticks.append(lambda: [from_core(p, rel, l_rel) for l_rel in (0, 1) for p in "BA" for rel in range(1 - depth, depth)])
    return ticks


def reduce_buffers(depth, rows, width):
    half, rest = rows // 2, width - CUT
    return {
        "rc": (depth, 2, 2, half, width),
        "ya": (depth, 2, half, CUT),
        "xb": (depth, 2, half, rest),
        "da": (depth, 2, half, CUT),
        "ua": (depth, 2, half, CUT),
        "db": (depth, 2, half, rest),
        "ub": (depth, 2, half, rest),
        "xa": (2, half, CUT),
        "yb": (half, rest),
        "xc": (half, rest),
    }


def reduce_ticks(net, part, buf, out, side, tag):
    depth = net.depth
    s, z, y, c = net.s, net.z, net.y, net.c
    rc = buf["rc"]
    a_cols, b_cols = pl.ds(0, CUT), pl.ds(CUT, rc.shape[-1] - CUT)
    x_dev, y_dev, c_dev = net.at(s=1 - s), net.at(y=1 - y), net.at(c=1 - c)

    def start(z1):
        net.send(part.at[z1, :, 1 - c], rc.at[z1], c_dev, (tag, "c", z1), lambda: rc.at[z1])

    def cores(z1):
        net.recv(rc.at[z1], (tag, "c", z1))
        for y1 in (0, 1):
            rc[z1, y1] = rc[z1, y1] + part[z1, y1, c]
        net.send(rc.at[z1, 1 - y, :, :, a_cols], buf["ya"].at[z1], y_dev, (tag, "ya", z1), lambda: buf["ya"].at[z1])
        net.send(rc.at[z1, :, 1 - s, :, b_cols], buf["xb"].at[z1], x_dev, (tag, "xb", z1), lambda: buf["xb"].at[z1])

    def add_a(z1, ref):
        rc[z1, y, :, :, a_cols] = rc[z1, y, :, :, a_cols] + ref[...]

    def add_b(z1, ref):
        for y1 in (0, 1):
            rc[z1, y1, s, :, b_cols] = rc[z1, y1, s, :, b_cols] + ref[y1]

    def planes(z1):
        net.recv(buf["ya"].at[z1], (tag, "ya", z1))
        add_a(z1, buf["ya"].at[z1])
        net.recv(buf["xb"].at[z1], (tag, "xb", z1))
        add_b(z1, buf["xb"].at[z1])

    def wave(k):
        def go(way, z_here, order):
            na, nb, step = ("da", "db", 1) if way == "up" else ("ua", "ub", -1)
            for z1 in order:
                if k > 0:
                    net.recv(buf[na].at[z1], (tag, na, z1))
                    add_a(z1, buf[na].at[z1])
                    net.recv(buf[nb].at[z1], (tag, nb, z1))
                    add_b(z1, buf[nb].at[z1])
                if z1 != z_here:
                    to = net.at(z=z + step)
                    a_like, b_like = (lambda z1=z1: buf[na].at[z1]), (lambda z1=z1: buf[nb].at[z1])
                    net.send(rc.at[z1, y, :, :, a_cols], a_like(), to, (tag, na, z1), a_like)
                    net.send(rc.at[z1, :, s, :, b_cols], b_like(), to, (tag, nb, z1), b_like)

        net.when(net.here[k], lambda: go("up", k, range(depth - 1, k - 1, -1)))
        net.when(net.here[depth - 1 - k], lambda: go("down", depth - 1 - k, range(0, depth - k)))

    def last_one():
        net.send(rc.at[z, 1 - y, s, :, b_cols], buf["yb"], y_dev, (tag, "yb"), lambda: buf["yb"])
        net.when(
            net.away[side],
            lambda: net.send(rc.at[z, y, :, :, a_cols], buf["xa"], x_dev, (tag, "xa"), lambda: buf["xa"]),
        )

    def last_two():
        net.recv(buf["yb"], (tag, "yb"))
        rc[z, y, s, :, b_cols] = rc[z, y, s, :, b_cols] + buf["yb"][...]
        net.when(
            net.away[side],
            lambda: net.send(rc.at[z, y, s, :, b_cols], buf["xc"], x_dev, (tag, "xc"), lambda: buf["xc"]),
        )

    def last_three():
        def body():
            net.recv(buf["xa"], (tag, "xa"))
            out[:, :, a_cols] = rc[z, y, :, :, a_cols].astype(F32) + buf["xa"][...].astype(F32)
            out[s, :, b_cols] = rc[z, y, s, :, b_cols].astype(F32)
            net.recv(buf["xc"], (tag, "xc"))
            out[1 - s, :, b_cols] = buf["xc"][...].astype(F32)

        net.when(net.home[side], body)

    each = range(depth)
    return (
        [functools.partial(start, z1) for z1 in each],
        [functools.partial(cores, z1) for z1 in each],
        [functools.partial(planes, z1) for z1 in each],
        [functools.partial(wave, k) for k in each] + [last_one, last_two, last_three],
    )


def flip_bit(index, bit):
    return index + bit * (1 - 2 * ((index // bit) % 2))


def total_partners(net):
    bits = [2**k for k in range(net_bits(lax.axis_size("dp")))]
    return [(net.s, flip_bit(net.d, bit)) for bit in bits] + [(1 - net.s, net.d)]


def net_bits(number):
    return number.bit_length() - 1


def total_ticks(net, sums, got, tag):
    partners = total_partners(net)

    def start(k):
        net.send(sums.at[k], got.at[k], partners[k], (tag, k), lambda: got.at[k])

    def finish(k):
        net.recv(got.at[k], (tag, k))
        sums[k + 1] = sums[k] + got[k]
        if k + 1 < len(partners):
            start(k + 1)

    return [functools.partial(start, 0)] + [functools.partial(finish, k) for k in range(len(partners))]


def gather_kernel(attn_own, ffn_own, enc, attn_full, ffn_full, enc_got, send_sems, recv_sems, local_sems):
    net = Net(send_sems, recv_sems)
    s, z, y, c = net.s, net.z, net.y, net.c
    net.greet()
    moves = [
        pltpu.make_async_copy(own, full.at[s, z, y, c], local_sems.at[k])
        for k, (own, full) in enumerate(((attn_own, attn_full), (ffn_own, ffn_full)))
    ]
    for move in moves:
        move.start()
    attn = gather_ticks(net, attn_full, attn_own, "attn", moves[0].wait)
    ffn = gather_ticks(net, ffn_full, ffn_own, "ffn", moves[1].wait)
    quarter = enc.shape[0] // 4
    attn[0]()
    ffn[0]()
    for k in range(4):
        rows = pl.ds(k * quarter, quarter)
        net.send(enc.at[rows], enc_got.at[rows], net.at(s=1 - s), ("enc", k), lambda rows=rows: enc_got.at[rows])
    for one, two in zip(attn[1:], ffn[1:]):
        one()
        two()
    for k in range(4):
        net.recv(enc_got.at[pl.ds(k * quarter, quarter)], ("enc", k))
    net.drain()


def gather_call(attn_own, ffn_own, enc):
    rows, width = attn_own.shape
    depth = lax.axis_size("dp") // 4
    full = jax.ShapeDtypeStruct((2, depth, 2, 2, rows, width), BF)
    anywhere = pl.BlockSpec(memory_space=pl.ANY)
    inside = pl.BlockSpec(memory_space=pltpu.VMEM)
    return pl.pallas_call(
        gather_kernel,
        out_shape=(full, full, jax.ShapeDtypeStruct(enc.shape, enc.dtype)),
        in_specs=[inside, inside, anywhere],
        out_specs=(anywhere, anywhere, anywhere),
        scratch_shapes=[
            pltpu.SemaphoreType.DMA((192,)),
            pltpu.SemaphoreType.DMA((192,)),
            pltpu.SemaphoreType.DMA((2,)),
        ],
        compiler_params=pltpu.CompilerParams(collective_id=0, has_side_effects=True),
        name="gather_all",
    )(attn_own, ffn_own, enc)


NAMES = ("rc", "ya", "xb", "da", "ua", "db", "ub", "xa", "yb", "xc")


def reduce_kernel(attn_part, ffn_part, small, attn_out, ffn_out, small_out, send_sems, recv_sems, sums, got, *bufs):
    net = Net(send_sems, recv_sems)
    net.greet([to for to in total_partners(net)[2:-1]])
    count = len(NAMES)
    plans = []
    for k, (part, out, side) in enumerate(((ffn_part, ffn_out, 1), (ffn_part, ffn_out, 0), (attn_part, attn_out, 1), (attn_part, attn_out, 0))):
        buf = dict(zip(NAMES, bufs[k * count : (k + 1) * count]))
        plans.append(reduce_ticks(net, part.at[side], buf, out, side, k))
    sums[0] = small[...]
    total = total_ticks(net, sums, got, "small")
    for plan in plans:
        for tick in plan[0]:
            tick()
    for plan in plans:
        for tick in plan[1]:
            tick()
    total[0]()
    total = total[1:]
    count = len(plans)
    for t in range(count + 1):
        if t < count:
            for tick in plans[t][2]:
                tick()
            plans[t][3][0]()
            plans[t][3][1]()
        if t > 0:
            plans[t - 1][3][2]()
            for tick in plans[t - 1][3][3:-3]:
                tick()
            plans[t - 1][3][-3]()
        if t < len(total):
            total[t]()
        if t > 0:
            plans[t - 1][3][-2]()
            plans[t - 1][3][-1]()
    for tick in total[count + 1:]:
        tick()
    small_out[...] = sums[sums.shape[0] - 1]
    net.drain()


def reduce_call(attn_part, ffn_part, small):
    width = attn_part.shape[-1]
    devices = lax.axis_size("dp") * 2
    depth = lax.axis_size("dp") // 4
    rows = attn_part.shape[0] // devices
    shape = (2, depth, 2, 2, 2, rows // 2, width)
    inside = pl.BlockSpec(memory_space=pltpu.VMEM)
    shapes = reduce_buffers(depth, rows, width)
    steps = net_bits(devices)
    out = jax.ShapeDtypeStruct((2, rows // 2, width), F32)
    return pl.pallas_call(
        reduce_kernel,
        out_shape=(out, out, jax.ShapeDtypeStruct(small.shape, F32)),
        in_specs=[inside] * 3,
        out_specs=(inside,) * 3,
        scratch_shapes=[
            pltpu.SemaphoreType.DMA((192,)),
            pltpu.SemaphoreType.DMA((192,)),
            pltpu.VMEM((steps + 1, *small.shape), F32),
            pltpu.VMEM((steps, *small.shape), F32),
            *[pltpu.VMEM(shapes[name], BF) for k in range(4) for name in NAMES],
        ],
        compiler_params=pltpu.CompilerParams(collective_id=1, has_side_effects=True, vmem_limit_bytes=60 << 20),
        name="reduce_all",
    )(attn_part.reshape(shape), ffn_part.reshape(shape), small)


def partner(value, axis, apart):
    mask = 2**apart
    pairs = [(source, source ^ mask) for source in range(lax.axis_size(axis))]
    return lax.ppermute(value, axis, pairs)


def matmul(left_op, right_op):
    return jnp.dot(left_op, right_op, preferred_element_type=jnp.float32)


def contract_rows(left_op, right_op):
    return lax.dot_general(
        left_op, right_op, (((0,), (0,)), ((), ())), preferred_element_type=jnp.float32
    )


def contract_cols(left_op, right_op):
    return lax.dot_general(
        left_op, right_op, (((1,), (1,)), ((), ())), preferred_element_type=jnp.float32
    )


def gelu_exact(pre_value):
    return jax.nn.gelu(pre_value, approximate=False)


def split_heads(matrix):
    return matrix.reshape(matrix.shape[0], HEADS, HEAD_DIM)


def merge_heads(tensor):
    return tensor.reshape(tensor.shape[0], HEADS * HEAD_DIM)


def column_sum(grad_low):
    return jnp.sum(grad_low.astype(jnp.float32), axis=0)


def norm_forward(residual, norm_gain, norm_shift):
    row_mean = jnp.mean(residual, axis=-1, keepdims=True)
    centered = residual - row_mean
    row_var = jnp.mean(centered * centered, axis=-1, keepdims=True)
    inv_std = lax.rsqrt(row_var + EPSILON)
    normed = centered * inv_std
    return (normed * norm_gain + norm_shift, normed, inv_std)


def norm_backward(grad_out, normed, inv_std, norm_gain):
    grad_norm = grad_out * norm_gain
    centered_grad = grad_norm - jnp.mean(grad_norm, axis=-1, keepdims=True)
    grad_res = inv_std * (
        centered_grad - normed * jnp.mean(grad_norm * normed, axis=-1, keepdims=True)
    )
    return (grad_res, jnp.sum(grad_out * normed, axis=0), jnp.sum(grad_out, axis=0))


def block_scores(q_block, keys_in, seg_row, first_row):
    scores = jnp.einsum("qhd,khd->hqk", q_block, keys_in, preferred_element_type=jnp.float32)
    if seg_row is None:
        return scores
    block_len = q_block.shape[0]
    query_pos = first_row + jnp.arange(block_len)
    key_pos = jnp.arange(seg_row.shape[0])
    allowed = (key_pos[None, :] <= query_pos[:, None]) & (seg_row[:, None] == seg_row[None, :])
    return jnp.where(allowed[None], scores, NEG_FILL)


def attend_forward(queries, keys_in, values_in, seg_row):
    scores = block_scores(queries, keys_in, seg_row, 0)
    row_max = jnp.max(scores, axis=-1, keepdims=True)
    exp_scores = jnp.exp(scores - row_max)
    totals = jnp.sum(exp_scores, axis=-1, keepdims=True)
    attn_prob = (exp_scores / totals).astype(jnp.bfloat16)
    outputs = jnp.einsum("hqk,khd->qhd", attn_prob, values_in, preferred_element_type=jnp.float32)
    lse_list = [row_max + jnp.log(totals)]
    return (outputs, lse_list)


def attend_backward(queries, keys_in, values_in, seg_row, lse_list, grad_mixed):
    query_len = queries.shape[0]
    block_len = min(512, query_len)
    grad_queries = []
    grad_keys = jnp.zeros(keys_in.shape, jnp.float32)
    grad_values = jnp.zeros(values_in.shape, jnp.float32)
    for block_index, first_row in enumerate(range(0, query_len, block_len)):
        scores = block_scores(queries, keys_in, seg_row, first_row)
        attn_prob = jnp.exp(scores - lse_list[block_index])
        grad_values = jnp.einsum(
            "hqk,qhd->khd",
            attn_prob.astype(jnp.bfloat16),
            grad_mixed,
            preferred_element_type=jnp.float32,
        )
        grad_prob = jnp.einsum(
            "qhd,khd->hqk", grad_mixed, values_in, preferred_element_type=jnp.float32
        )
        grad_scores = attn_prob * (
            grad_prob - jnp.sum(grad_prob * attn_prob, axis=-1, keepdims=True)
        )
        grad_low = grad_scores.astype(jnp.bfloat16)
        grad_queries.append(
            jnp.einsum("hqk,khd->qhd", grad_low, keys_in, preferred_element_type=jnp.float32)
        )
        grad_keys = jnp.einsum(
            "hqk,qhd->khd", grad_low, queries, preferred_element_type=jnp.float32
        )
    grad_q_all = grad_queries[0].astype(jnp.bfloat16)
    return (grad_q_all, grad_keys.astype(jnp.bfloat16), grad_values.astype(jnp.bfloat16))


def layer_row(dec_row, enc_row, seg_row, cot_row, blocks, w_in, w_out, vectors):
    w_query, w_key, w_value, w_proj, c_query, c_key, c_value, c_proj = blocks
    scale = 1.0 / math.sqrt(HEAD_DIM)
    bias_in = vectors[13:].reshape(-1)
    dec_full = dec_row.astype(jnp.float32)
    queries = ((matmul(dec_row, w_query) + vectors[0]) * scale).astype(jnp.bfloat16)
    keys_self = matmul(dec_row, w_key).astype(jnp.bfloat16)
    vals_self = (matmul(dec_row, w_value) + vectors[1]).astype(jnp.bfloat16)
    mixed_self, lse_self = attend_forward(
        split_heads(queries), split_heads(keys_self), split_heads(vals_self), seg_row
    )
    self_flat = merge_heads(mixed_self).astype(jnp.bfloat16)
    self_out = matmul(self_flat, w_proj) + vectors[2]
    hidden_one, normed_one, inv_one = norm_forward(dec_full + self_out, vectors[7], vectors[8])
    hidden_one_low = hidden_one.astype(jnp.bfloat16)
    cross_q = ((matmul(hidden_one_low, c_query) + vectors[3]) * scale).astype(jnp.bfloat16)
    cross_k = matmul(enc_row, c_key).astype(jnp.bfloat16)
    cross_v = (matmul(enc_row, c_value) + vectors[4]).astype(jnp.bfloat16)
    mixed_cross, lse_cross = attend_forward(
        split_heads(cross_q), split_heads(cross_k), split_heads(cross_v), None
    )
    cross_flat = merge_heads(mixed_cross).astype(jnp.bfloat16)
    cross_out = matmul(cross_flat, c_proj) + vectors[5]
    hidden_two, normed_two, inv_two = norm_forward(hidden_one + cross_out, vectors[9], vectors[10])
    hidden_two_low = hidden_two.astype(jnp.bfloat16)
    pre_act = contract_cols(hidden_two_low, w_in) + bias_in
    act_full, act_pull = jax.vjp(gelu_exact, pre_act)
    act_low = act_full.astype(jnp.bfloat16)
    ffn_out = matmul(act_low, w_out) + vectors[6]
    result, normed_three, inv_three = norm_forward(hidden_two + ffn_out, vectors[11], vectors[12])
    grad_r3, grad_g3, grad_e3 = norm_backward(cot_row, normed_three, inv_three, vectors[11])
    grad_y = grad_r3.astype(jnp.bfloat16)
    grad_w_out = contract_rows(act_low, grad_y)
    grad_act = contract_cols(grad_y, w_out)
    grad_pre = act_pull(grad_act)[0].astype(jnp.bfloat16)
    grad_w_in = contract_rows(grad_pre, hidden_two_low)
    grad_h2 = grad_r3 + matmul(grad_pre, w_in)
    grad_r2, grad_g2, grad_e2 = norm_backward(grad_h2, normed_two, inv_two, vectors[9])
    grad_co = grad_r2.astype(jnp.bfloat16)
    grad_c_proj = contract_rows(cross_flat, grad_co)
    grad_mix_c = contract_cols(grad_co, c_proj).astype(jnp.bfloat16)
    grad_q_c, grad_k_c, grad_v_c = attend_backward(
        split_heads(cross_q),
        split_heads(cross_k),
        split_heads(cross_v),
        None,
        lse_cross,
        split_heads(grad_mix_c),
    )
    grad_cq = merge_heads(grad_q_c) * scale
    grad_ck = merge_heads(grad_k_c)
    grad_cv = merge_heads(grad_v_c)
    grad_c_query = contract_rows(hidden_one_low, grad_cq)
    grad_h1 = grad_r2 + contract_cols(grad_cq, c_query)
    grad_r1, grad_g1, grad_e1 = norm_backward(grad_h1, normed_one, inv_one, vectors[7])
    grad_so = grad_r1.astype(jnp.bfloat16)
    grad_w_proj = contract_rows(self_flat, grad_so)
    grad_mix_s = contract_cols(grad_so, w_proj).astype(jnp.bfloat16)
    grad_q_s, grad_k_s, grad_v_s = attend_backward(
        split_heads(queries),
        split_heads(keys_self),
        split_heads(vals_self),
        seg_row,
        lse_self,
        split_heads(grad_mix_s),
    )
    grad_sq = merge_heads(grad_q_s) * scale
    grad_sk = merge_heads(grad_k_s)
    grad_sv = merge_heads(grad_v_s)
    grad_w_query = contract_rows(dec_row, grad_sq)
    grad_w_key = contract_rows(dec_row, grad_sk)
    grad_w_value = contract_rows(dec_row, grad_sv)
    grad_input = (
        grad_r1
        + contract_cols(grad_sq, w_query)
        + contract_cols(grad_sk, w_key)
        + contract_cols(grad_sv, w_value)
    )
    vec_rows = jnp.stack(
        [
            column_sum(grad_sq),
            column_sum(grad_sv),
            column_sum(grad_so),
            column_sum(grad_cq),
            column_sum(grad_cv),
            column_sum(grad_co),
            column_sum(grad_y),
            grad_g1,
            grad_e1,
            grad_g2,
            grad_e2,
            grad_g3,
            grad_e3,
        ]
    )
    vec_grad = jnp.concatenate([vec_rows, column_sum(grad_pre).reshape(-1, vectors.shape[1])], 0)
    row_mats = (grad_w_query, grad_w_key, grad_w_value, grad_w_proj, grad_c_query, grad_c_proj)
    return (result, grad_input, grad_ck, grad_cv, row_mats, grad_w_in, grad_w_out, vec_grad)


def nesterov(master, moment, average, grad, rate):
    new_moment = MOMENTUM * moment + grad
    new_master = master - rate * (grad + MOMENTUM * new_moment)
    new_average = AVG_DECAY * average + (1.0 - AVG_DECAY) * new_master
    return (new_master, new_moment, new_average)


def local(
    decoder_in,
    encoder_out,
    segment_ids,
    cotangent,
    attn_master,
    ffn_master,
    small_master,
    attn_moment,
    ffn_moment,
    small_moment,
    attn_average,
    ffn_average,
    small_average,
    rate_matrix,
    rate_vector,
):
    own_kernels = attn_master.shape[0] % 32 == 0 and lax.axis_size("dp") % 4 == 0
    attn_own, ffn_own = attn_master.astype(BF), ffn_master.astype(BF)
    if own_kernels:
        attn_full, ffn_full, enc_got = gather_call(attn_own, ffn_own, encoder_out[0])
        matrices, ffn_all = (full.reshape(-1, attn_own.shape[-1]) for full in (attn_full, ffn_full))
        partner_enc = enc_got[None]
    else:
        matrices, ffn_all = (
            lax.all_gather(own, ("side", "dp"), axis=0, tiled=True) for own in (attn_own, ffn_own)
        )
        partner_enc = partner(encoder_out, "side", 0)
    model_width = matrices.shape[1]
    hidden_units = ffn_all.shape[0] // 2
    blocks = [
        matrices[block_index * model_width : (block_index + 1) * model_width]
        for block_index in range(8)
    ]
    w_in = ffn_all[:hidden_units]
    w_out = ffn_all[hidden_units:]
    mat_grads = [jnp.zeros((model_width, model_width), jnp.float32) for block_index in range(8)]
    slots = (0, 1, 2, 3, 4, 7)
    row_index = 0
    outcome = layer_row(
        decoder_in[row_index],
        partner_enc[row_index],
        segment_ids[row_index],
        cotangent[row_index],
        blocks,
        w_in,
        w_out,
        small_master,
    )
    result, grad_input, grad_ck, grad_cv, row_mats, grad_w_in, grad_w_out, vec_grad = outcome
    results = [result]
    input_grads = [grad_input]
    key_grads = [grad_ck]
    value_grads = [grad_cv]
    for slot_index, slot_grad in zip(slots, row_mats):
        mat_grads[slot_index] = slot_grad
    mat_grads[5] = contract_rows(partner_enc[0], key_grads[0])
    mat_grads[6] = contract_rows(partner_enc[0], value_grads[0])
    enc_term = contract_cols(key_grads[0], blocks[5]) + contract_cols(value_grads[0], blocks[6])
    encoder_grad = partner(enc_term.astype(BF)[None], "side", 0).astype(F32)
    if own_kernels:
        attn_part = jnp.concatenate([grad.astype(BF) for grad in mat_grads], 0)
        ffn_part = jnp.concatenate([grad_w_in.astype(BF), grad_w_out.astype(BF)], 0)
        padded = jnp.pad(vec_grad, ((0, -vec_grad.shape[0] % 8), (0, 0)))
        attn_grad, ffn_grad, small_grad = reduce_call(attn_part, ffn_part, padded)
        attn_grad, ffn_grad = attn_grad.reshape(attn_master.shape), ffn_grad.reshape(ffn_master.shape)
        small_grad = small_grad[: vec_grad.shape[0]]
    else:
        attn_total = jnp.concatenate(mat_grads, 0)
        ffn_total = jnp.concatenate([grad_w_in, grad_w_out], 0)
        attn_grad, ffn_grad = (
            lax.psum_scatter(total, ("side", "dp"), scatter_dimension=0, tiled=True)
            for total in (attn_total, ffn_total)
        )
        small_grad = lax.psum(vec_grad, ("side", "dp"))
    attn_new, attn_moment_new, attn_average_new = nesterov(
        attn_master, attn_moment, attn_average, attn_grad, rate_matrix
    )
    ffn_new, ffn_moment_new, ffn_average_new = nesterov(
        ffn_master, ffn_moment, ffn_average, ffn_grad, rate_matrix
    )
    small_new, small_moment_new, small_average_new = nesterov(
        small_master, small_moment, small_average, small_grad, rate_vector
    )
    layer_out = jnp.stack(results)
    input_grad = jnp.stack(input_grads)
    return (
        layer_out,
        input_grad,
        encoder_grad,
        attn_grad,
        ffn_grad,
        small_grad,
        attn_new,
        ffn_new,
        small_new,
        attn_moment_new,
        ffn_moment_new,
        small_moment_new,
        attn_average_new,
        ffn_average_new,
        small_average_new,
    )


def solution(mesh):
    placed = (
        P(("side", "dp"), None, None),
        P(("side", "dp"), None, None),
        P(("side", "dp"), None),
        P(("side", "dp"), None, None),
        P(("side", "dp"), None),
        P(("side", "dp"), None),
        P(),
        P(("side", "dp"), None),
        P(("side", "dp"), None),
        P(),
        P(("side", "dp"), None),
        P(("side", "dp"), None),
        P(),
        P(),
        P(),
    )
    return jax.shard_map(
        local,
        mesh=mesh,
        in_specs=placed,
        out_specs=(
            P(("side", "dp"), None, None),
            P(("side", "dp"), None, None),
            P(("side", "dp"), None, None),
            P(("side", "dp"), None),
            P(("side", "dp"), None),
            P(),
            P(("side", "dp"), None),
            P(("side", "dp"), None),
            P(),
            P(("side", "dp"), None),
            P(("side", "dp"), None),
            P(),
            P(("side", "dp"), None),
            P(("side", "dp"), None),
            P(),
        ),
        check_vma=False,
    )
```

```python
import functools
import math

import jax
import jax.numpy as jnp
from jax import lax
from jax.experimental import pallas as pl
from jax.experimental.pallas import tpu as pltpu
from jax.sharding import PartitionSpec as P

HEADS = 12
HEAD_DIM = 64


NEG_FILL = -1e30
EPSILON = 1e-05
MOMENTUM = 0.5
AVG_DECAY = 0.5


MESH_ID = pl.DeviceIdType.MESH
BF = jnp.bfloat16
F32 = jnp.float32
CUT = 512


def run_when(cond, body):
    @pl.when(cond)
    def _():
        body()


class Net:
    def __init__(self, send_sems, recv_sems):
        self.s = lax.axis_index("side")
        self.d = lax.axis_index("dp")
        self.z, self.y, self.c = self.d // 4, (self.d // 2) % 2, self.d % 2
        self.depth = lax.axis_size("dp") // 4
        self.send_sems, self.recv_sems = send_sems, recv_sems
        self.sent, self.slots, self.conds = [], {}, []
        self.low = [self.z >= k for k in range(self.depth)]
        self.high = [self.z < self.depth - k for k in range(self.depth)]
        self.here = [self.z == k for k in range(self.depth)]
        self.away = [self.s != k for k in (0, 1)]
        self.home = [self.s == k for k in (0, 1)]

    def at(self, s=None, z=None, y=None, c=None):
        s, z, y, c = (own if got is None else got for got, own in ((s, self.s), (z, self.z), (y, self.y), (c, self.c)))
        return (s, (z * 2 + y) * 2 + c)

    def slot(self, key):
        return self.slots.setdefault(key, len(self.slots))

    def copy(self, src, dst, to, send_slot, recv_slot):
        return pltpu.make_async_remote_copy(
            src_ref=src,
            dst_ref=dst,
            send_sem=self.send_sems.at[send_slot],
            recv_sem=self.recv_sems.at[recv_slot],
            device_id=to,
            device_id_type=MESH_ID,
        )

    def send(self, src, dst, to, key, like):
        send_slot, recv_slot = len(self.sent), self.slot(key)
        self.copy(src, dst, to, send_slot, recv_slot).start()
        peer = (self.s, self.d)
        self.sent.append((lambda: self.copy(like(), like(), peer, send_slot, recv_slot).wait_send(), tuple(self.conds)))

    def recv(self, dst, key):
        self.copy(dst, dst, self.at(c=1 - self.c), 0, self.slot(key)).wait_recv()

    def when(self, cond, body):
        self.conds.append(cond)
        run_when(cond, body)
        self.conds.pop()

    def drain(self):
        assert max(len(self.sent), len(self.slots)) <= min(self.send_sems.shape[0], self.recv_sems.shape[0])
        for wait, conds in self.sent:
            for cond in conds:
                wait = functools.partial(pl.when(cond), wait)
            wait()

    def greet(self, others=()):
        barrier = pltpu.get_barrier_semaphore()
        partners = [self.at(s=1 - self.s), self.at(y=1 - self.y), self.at(c=1 - self.c), *others]
        for to in partners:
            pl.semaphore_signal(barrier, inc=1, device_id=to, device_id_type=MESH_ID)
        low, high = self.low[1], self.high[1]

        def signal(to):
            pl.semaphore_signal(barrier, inc=1, device_id=to, device_id_type=MESH_ID)

        pl.when(low)(lambda: signal(self.at(z=self.z - 1)))
        pl.when(high)(lambda: signal(self.at(z=self.z + 1)))
        pl.semaphore_wait(barrier, len(partners) + low.astype(jnp.int32) + high.astype(jnp.int32))


def gather_ticks(net, full, own, tag):
    depth, width = net.depth, full.shape[-1]
    cols = {"A": pl.ds(0, CUT), "B": pl.ds(CUT, width - CUT)}
    coord = {"A": (net.s, net.y), "B": (net.y, net.s)}
    z, c = net.z, net.c

    def part(p, f, z_of, l, core):
        s, y = (f, l) if p == "A" else (l, f)
        return full.at[s, z_of, y, core, :, cols[p]]

    def pair(p, z_of, l, core):
        if p == "A":
            return full.at[:, z_of, l, core, :, cols[p]]
        return full.at[l, z_of, :, core, :, cols[p]]

    def dev(p, f, z_of, l, core):
        s, y = (f, l) if p == "A" else (l, f)
        return net.at(s, z_of, y, core)

    def spread(p, src, dst, ups, rel, f_rel):
        f, l = coord[p]
        like = lambda: full.at[0, 0, 0, 0, :, cols[p]]
        if ups != "down" and 1 - rel < depth:
            net.when(
                net.high[1],
                lambda: net.send(src, dst, dev(p, f, z + 1, l, c), (tag, p, "up", 1 - rel, f_rel), like),
            )
        if ups != "up" and 1 + rel < depth:
            net.when(
                net.low[1],
                lambda: net.send(src, dst, dev(p, f, z - 1, l, c), (tag, p, "down", 1 + rel, f_rel), like),
            )
        net.send(src, dst, dev(p, f, z, 1 - l, c), (tag, p, "l", rel, f_rel), like)

    def to_core(p, rel, l_rel):
        f, l = coord[p]
        l_of = l if l_rel == 0 else 1 - l
        both_f = pair(p, z + rel, l_of, c)
        net.send(both_f, both_f, net.at(c=1 - c), (tag, p, "core", rel, l_rel), lambda: pair(p, 0, 0, 0))

    def first(p):
        f, l = coord[p]
        src, dst = own.at[:, cols[p]], part(p, f, z, l, c)
        net.send(src, dst, dev(p, 1 - f, z, l, c), (tag, p, "f"), lambda: full.at[0, 0, 0, 0, :, cols[p]])
        spread(p, src, dst, "both", 0, 0)

    def second(p):
        f, l = coord[p]
        got = part(p, 1 - f, z, l, c)
        net.recv(got, (tag, p, "f"))
        spread(p, got, got, "both", 0, 1)
        to_core(p, 0, 0)

    def along(p, dist, f_rel, way):
        f, l = coord[p]
        rel = -dist if way == "up" else dist

        def body():
            got = part(p, f if f_rel == 0 else 1 - f, z + rel, l, c)
            net.recv(got, (tag, p, way, dist, f_rel))
            spread(p, got, got, way, rel, f_rel)
            if f_rel == 1:
                to_core(p, rel, 0)

        net.when(net.low[dist] if way == "up" else net.high[dist], body)

    def across(p, rel):
        f, l = coord[p]

        def body():
            for f_rel in (0, 1):
                net.recv(part(p, f if f_rel == 0 else 1 - f, z + rel, 1 - l, c), (tag, p, "l", rel, f_rel))
            to_core(p, rel, 1)

        if rel == 0:
            body()
        else:
            net.when(net.low[-rel] if rel < 0 else net.high[rel], body)

    def from_core(p, rel, l_rel):
        f, l = coord[p]
        body = lambda: net.recv(pair(p, z + rel, l if l_rel == 0 else 1 - l, 1 - c), (tag, p, "core", rel, l_rel))
        if rel == 0:
            body()
        else:
            net.when(net.low[-rel] if rel < 0 else net.high[rel], body)

    def both(fn, *args):
        return lambda: (fn("B", *args), fn("A", *args))

    ticks = [both(first), both(second)]
    for dist in range(1, depth):
        for f_rel in (0, 1):
            ticks.append(lambda dist=dist, f_rel=f_rel: [along(p, dist, f_rel, way) for p in "BA" for way in ("up", "down")])
    for dist in range(depth):
        ticks.append(lambda dist=dist: [across(p, rel) for p in "BA" for rel in sorted({-dist, dist})])
    ticks.append(lambda: [from_core(p, rel, l_rel) for l_rel in (0, 1) for p in "BA" for rel in range(1 - depth, depth)])
    return ticks


def reduce_buffers(depth, rows, width):
    half, rest = rows // 2, width - CUT
    return {
        "rc": (depth, 2, 2, half, width),
        "ya": (depth, 2, half, CUT),
        "xb": (depth, 2, half, rest),
        "za": (depth + 1, 2, half, CUT),
        "zb": (depth + 1, 2, half, rest),
        "xa": (2, half, CUT),
        "yb": (half, rest),
        "xc": (half, rest),
    }


def reduce_ticks(net, part, own, buf, out, side, tag):
    depth = net.depth
    s, z, y, c = net.s, net.z, net.y, net.c
    rc = buf["rc"]
    a_cols, b_cols = pl.ds(0, CUT), pl.ds(CUT, rc.shape[-1] - CUT)
    x_dev, y_dev, c_dev = net.at(s=1 - s), net.at(y=1 - y), net.at(c=1 - c)

    def start(z1):
        net.send(part.at[z1, :, 1 - c], rc.at[z1], c_dev, (tag, "c", z1), lambda: rc.at[z1])

    def cores(z1):
        net.recv(rc.at[z1], (tag, "c", z1))
        for y1 in (0, 1):
            rc[z1, y1] = rc[z1, y1] + own(z1, y1)
        net.send(rc.at[z1, 1 - y, :, :, a_cols], buf["ya"].at[z1], y_dev, (tag, "ya", z1), lambda: buf["ya"].at[z1])
        net.send(rc.at[z1, :, 1 - s, :, b_cols], buf["xb"].at[z1], x_dev, (tag, "xb", z1), lambda: buf["xb"].at[z1])

    def add_a(z1, ref):
        rc[z1, y, :, :, a_cols] = rc[z1, y, :, :, a_cols] + ref[...]

    def add_b(z1, ref):
        for y1 in (0, 1):
            rc[z1, y1, s, :, b_cols] = rc[z1, y1, s, :, b_cols] + ref[y1]

    def planes(z1):
        net.recv(buf["ya"].at[z1], (tag, "ya", z1))
        add_a(z1, buf["ya"].at[z1])
        net.recv(buf["xb"].at[z1], (tag, "xb", z1))
        add_b(z1, buf["xb"].at[z1])

    def wave(k):
        def go(way, z_here, order):
            step = 1 if way == "up" else -1
            for z1 in order:
                place = z1 + 1 if way == "up" else z1
                a_like = lambda place=place: buf["za"].at[place]
                b_like = lambda place=place: buf["zb"].at[place]
                if k > 0:
                    net.recv(a_like(), (tag, "za", place))
                    add_a(z1, a_like())
                    net.recv(b_like(), (tag, "zb", place))
                    add_b(z1, b_like())
                if z1 != z_here:
                    to = net.at(z=z + step)
                    net.send(rc.at[z1, y, :, :, a_cols], a_like(), to, (tag, "za", place), a_like)
                    net.send(rc.at[z1, :, s, :, b_cols], b_like(), to, (tag, "zb", place), b_like)

        net.when(net.here[k], lambda: go("up", k, range(depth - 1, k - 1, -1)))
        net.when(net.here[depth - 1 - k], lambda: go("down", depth - 1 - k, range(0, depth - k)))

    def last_one():
        net.send(rc.at[z, 1 - y, s, :, b_cols], buf["yb"], y_dev, (tag, "yb"), lambda: buf["yb"])
        net.when(
            net.away[side],
            lambda: net.send(rc.at[z, y, :, :, a_cols], buf["xa"], x_dev, (tag, "xa"), lambda: buf["xa"]),
        )

    def last_two():
        net.recv(buf["yb"], (tag, "yb"))
        rc[z, y, s, :, b_cols] = rc[z, y, s, :, b_cols] + buf["yb"][...]
        net.when(
            net.away[side],
            lambda: net.send(rc.at[z, y, s, :, b_cols], buf["xc"], x_dev, (tag, "xc"), lambda: buf["xc"]),
        )

    def last_three():
        def body():
            net.recv(buf["xa"], (tag, "xa"))
            out[:, :, a_cols] = rc[z, y, :, :, a_cols].astype(F32) + buf["xa"][...].astype(F32)
            out[s, :, b_cols] = rc[z, y, s, :, b_cols].astype(F32)
            net.recv(buf["xc"], (tag, "xc"))
            out[1 - s, :, b_cols] = buf["xc"][...].astype(F32)

        net.when(net.home[side], body)

    each = range(depth)
    return (
        [functools.partial(start, z1) for z1 in each],
        [functools.partial(cores, z1) for z1 in each],
        [functools.partial(planes, z1) for z1 in each],
        [functools.partial(wave, k) for k in each] + [last_one, last_two, last_three],
    )


def flip_bit(index, bit):
    return index + bit * (1 - 2 * ((index // bit) % 2))


def total_partners(net):
    bits = [2**k for k in range(net_bits(lax.axis_size("dp")))]
    return [(net.s, flip_bit(net.d, bit)) for bit in bits] + [(1 - net.s, net.d)]


def net_bits(number):
    return number.bit_length() - 1


def total_ticks(net, sums, got, tag):
    partners = total_partners(net)

    def start(k):
        net.send(sums.at[k], got.at[k], partners[k], (tag, k), lambda: got.at[k])

    def finish(k):
        net.recv(got.at[k], (tag, k))
        sums[k + 1] = sums[k] + got[k]
        if k + 1 < len(partners):
            start(k + 1)

    return [functools.partial(start, 0)] + [functools.partial(finish, k) for k in range(len(partners))]


PAIR = 2 * HEAD_DIM


def dg(left, right, left_dim, right_dim):
    return lax.dot_general(
        left, right, (((left_dim,), (right_dim,)), ((), ())), preferred_element_type=F32
    )


def lane_ids(rows):
    return lax.broadcasted_iota(jnp.int32, (rows, PAIR), 1)


def head_lanes(h):
    lane = lane_ids(1)
    return jnp.where((lane >= h * HEAD_DIM) & (lane < (h + 1) * HEAD_DIM), 1.0, 0.0).astype(BF)


def spare_lanes(h):
    lane, first = lane_ids(1), (1 - h) * HEAD_DIM
    return jnp.where((lane >= first) & (lane < first + 3), 1.0, 0.0).astype(BF)


def with_constant(values, constant, h):
    high = constant.astype(BF).astype(F32)
    mid = (constant - high).astype(BF).astype(F32)
    low = constant - high - mid
    lane, first = lane_ids(values.shape[0]), (1 - h) * HEAD_DIM
    own = (lane >= h * HEAD_DIM) & (lane < (h + 1) * HEAD_DIM)
    out = jnp.where(own, values, 0.0)
    for k, term in enumerate((high, mid, low)):
        out = jnp.where(lane == first + k, term, out)
    return out.astype(BF)


def pair_lanes(p):
    return pl.ds(pl.multiple_of(p * PAIR, PAIR), PAIR)


def norm_rows(r, gain, shift):
    mean = jnp.mean(r, axis=-1, keepdims=True)
    centered = r - mean
    var = jnp.mean(centered * centered, axis=-1, keepdims=True)
    inv = lax.rsqrt(var + EPSILON)
    normed = centered * inv
    return normed * gain + shift, normed, inv


def norm_rows_back(grad, normed, inv, gain):
    dn = grad * gain
    out = inv * (
        dn
        - jnp.mean(dn, axis=-1, keepdims=True)
        - normed * jnp.mean(dn * normed, axis=-1, keepdims=True)
    )
    return out


def rowsum(values):
    return jnp.sum(values, axis=0, keepdims=True)


def by_rows(length, body, step=64):
    def go(k, carry):
        body(pl.ds(pl.multiple_of(k * step, step), step))
        return carry

    lax.fori_loop(0, length // step, go, 0)


def allowed_bias(bias, seg_row, seg_col):
    length = bias.shape[0]

    def body(span):
        shape = (span.size, length)
        query = lax.broadcasted_iota(jnp.int32, shape, 0) + span.start
        key = lax.broadcasted_iota(jnp.int32, shape, 1)
        ok = (key <= query) & (seg_col[span, :] == seg_row[...])
        bias[span, :] = jnp.where(ok, 0.0, NEG_FILL)

    by_rows(length, body)


def attend_pair(p, q, k, v, q_aug, out, bias):
    lanes = pair_lanes(p)
    half = q.shape[0] // 2
    blocks = [(0, half, k.shape[0]), (half, half, k.shape[0])]
    if bias is not None:
        blocks = [(0, half, half), (half, half, 2 * half)]
    for first, rows, keys in blocks:
        span = pl.ds(first, rows)
        q_rows = q[span, lanes]
        k_rows, v_rows = k[pl.ds(0, keys), lanes], v[pl.ds(0, keys), lanes]
        outs = []
        for h in (0, 1):
            scores = dg(q_rows * head_lanes(h), k_rows, 1, 1)
            if bias is not None:
                scores = scores + bias[span, pl.ds(0, keys)]
            top = jnp.max(scores, axis=-1, keepdims=True)
            weight = jnp.exp(scores - top)
            total = jnp.sum(weight, axis=-1, keepdims=True)
            prob = (weight * (1.0 / total)).astype(BF)
            outs.append(dg(prob, v_rows, 1, 0))
            q_aug[2 * p + h, span, :] = with_constant(q_rows.astype(F32), -(top + jnp.log(total)), h)
        out[span, lanes] = jnp.where(lane_ids(rows) < HEAD_DIM, outs[0], outs[1]).astype(BF)


def whole(ref):
    return ref[...].reshape(-1, ref.shape[-1])


class Local:
    def __init__(self, sems):
        self.sems, self.count, self.open = sems, 0, []

    def copy(self, src, dst):
        move = pltpu.make_async_copy(src, dst, self.sems.at[self.count])
        self.count += 1
        move.start()
        return move

    def save(self, src, dst):
        self.open.append(self.copy(src, dst))

    def drain(self):
        for move in self.open:
            move.wait()


FWD_SAVED = ("qa", "k", "v", "a", "h1", "n1", "inv1", "qb", "k2", "v2", "a2", "enc", "dr2", "vec")


def forward_kernel(names, *refs):
    r = dict(zip(names, refs))
    net = Net(r["send_sems"], r["recv_sems"])
    s, z, y, c = net.s, net.z, net.y, net.c
    small, attn_full, ffn_full = r["small"], r["attn_full"], r["ffn_full"]
    local = Local(r["local_sems"])
    depth = net.depth
    scale = 1.0 / math.sqrt(HEAD_DIM)
    pairs = r["x"].shape[1] // PAIR

    attn_full[s, z, y, c] = r["attn_own"][...].astype(BF)
    ffn_full[s, z, y, c] = r["ffn_own"][...].astype(BF)
    net.greet()
    attn = gather_ticks(net, attn_full, attn_full.at[s, z, y, c], "attn")
    ffn = gather_ticks(net, ffn_full, ffn_full.at[s, z, y, c], "ffn")
    attn.pop(0)()
    attn.pop(0)()
    quarter = r["enc_own"].shape[0] // 4
    for k in range(4):
        rows = pl.ds(k * quarter, quarter)
        net.send(r["enc_own"].at[rows], r["enc"].at[rows], net.at(s=1 - s), ("enc", k), lambda rows=rows: r["enc"].at[rows])
    allowed_bias(r["bias"], r["seg_row"], r["seg_col"])
    attn.pop(0)()
    attn.pop(0)()
    ffn.pop(0)()
    while attn:
        attn.pop(0)()
        if len(attn) in (7, 6):
            ffn.pop(0)()

    def block(k):
        return whole(attn_full.at[k // depth, k % depth])

    def tick(p, at):
        if ffn:
            run_when(p == at, ffn.pop(0))

    def into_heads(dst, left, right, bias, factor):
        half = left.shape[0] // 2
        for k in (0, 1):
            span = pl.ds(k * half, half)
            value = dg(left[span, :], right, 1, 0)
            if bias is not None:
                value = value + bias
            if factor is not None:
                value = value * factor
            dst[span, :] = value.astype(BF)

    t, length = r["t"], r["x"].shape[0]
    into_heads(r["q"], r["x"], block(0), small[0:1], scale)
    into_heads(r["k"], r["x"], block(1), None, None)
    into_heads(r["v"], r["x"], block(2), small[1:2], None)
    local.save(attn_full, r["attn_out"])

    def self_body(p, carry):
        attend_pair(p, r["q"], r["k"], r["v"], r["qa"], r["a"], r["bias"])
        tick(p, 1)
        tick(p, 3)
        return carry

    lax.fori_loop(0, pairs, self_body, 0)
    t[...] = dg(r["a"][...], block(3), 1, 0)

    def norm_one(span):
        res = r["x"][span, :].astype(F32) + t[span, :] + small[2:3]
        hidden, normed, inv = norm_rows(res, small[7:8], small[8:9])
        r["h1f"][span, :] = hidden
        r["h1"][span, :] = hidden.astype(BF)
        r["n1"][span, :] = normed
        r["inv1"][span, :] = jnp.broadcast_to(inv, (span.size, PAIR))

    by_rows(length, norm_one)
    into_heads(r["q"], r["h1"], block(4), small[3:4], scale)
    for k in range(4):
        net.recv(r["enc"].at[pl.ds(k * quarter, quarter)], ("enc", k))
    if ffn:
        ffn.pop(0)()
    into_heads(r["k2"], r["enc"], block(5), None, None)
    into_heads(r["v2"], r["enc"], block(6), small[4:5], None)

    def cross_body(p, carry):
        attend_pair(p, r["q"], r["k2"], r["v2"], r["qb"], r["a2"], None)
        for at in range(pairs):
            tick(p, at)
        return carry

    for name in ("qa", "k", "v", "a", "h1", "n1", "inv1", "k2", "v2", "enc"):
        local.save(r[name], r[name + "_out"])
    lax.fori_loop(0, pairs, cross_body, 0)
    for name in ("qb", "a2"):
        local.save(r[name], r[name + "_out"])
    t[...] = dg(r["a2"][...], block(7), 1, 0)

    def norm_two(span):
        res = r["h1f"][span, :] + t[span, :] + small[5:6]
        hidden, normed, inv = norm_rows(res, small[9:10], small[10:11])
        r["h1f"][span, :] = hidden
        r["h2"][span, :] = hidden.astype(BF)
        r["n2"][span, :] = normed
        r["inv2"][span, :] = jnp.broadcast_to(inv, (span.size, PAIR))

    by_rows(length, norm_two)
    while ffn:
        ffn.pop(0)()

    vec, acc = r["vec"], r["h1f"]
    vec[...] = jnp.zeros_like(vec)
    root = math.sqrt(0.5)
    for k in range(depth):
        t[...] = dg(r["h2"][...], whole(ffn_full.at[0, k]), 1, 1)

        def gelu(span, k=k):
            u = t[span, :] + small[13 + k : 14 + k]
            below = 0.5 + 0.5 * lax.erf(u * root)
            r["g"][k, span, :] = (u * below).astype(BF)
            r["gp"][k, span, :] = below + u * (jnp.exp(-0.5 * u * u) * (1.0 / math.sqrt(2.0 * math.pi)))

        by_rows(length, gelu)
        acc[...] += dg(r["g"][k], whole(ffn_full.at[1, k]), 1, 0)

    def norm_three(span):
        hidden, normed, inv = norm_rows(acc[span, :] + small[6:7], small[11:12], small[12:13])
        r["out"][span, :] = hidden
        cot = r["cot"][span, :]
        dr3 = norm_rows_back(cot, normed, inv, small[11:12])
        vec[11:12] += rowsum(cot * normed)
        vec[12:13] += rowsum(cot)
        acc[span, :] = dr3
        low = dr3.astype(BF)
        r["dy"][span, :] = low
        vec[6:7] += rowsum(low.astype(F32))

    by_rows(length, norm_three)
    local.save(r["out"], r["layer_out"])
    slots = r["slots"]
    held = [None] * slots.shape[0]
    used = 0

    def put(left, right, dst):
        nonlocal used
        slot = used % len(held)
        used += 1
        if held[slot] is not None:
            held[slot].wait()
        slots[slot] = dg(left, right, 0, 0).astype(BF).reshape(slots.shape[1:])
        held[slot] = local.copy(slots.at[slot], dst)

    for k in range(depth):
        put(r["g"][k], r["dy"][...], r["g_ffn"].at[1, k])
        t[...] = dg(r["dy"][...], whole(ffn_full.at[1, k]), 1, 1)

        def through(span, k=k):
            du = (t[span, :] * r["gp"][k, span, :]).astype(BF)
            r["g"][k, span, :] = du
            vec[13 + k : 14 + k] += rowsum(du.astype(F32))

        by_rows(length, through)
    for k in range(depth):
        put(r["g"][k], r["h2"][...], r["g_ffn"].at[0, k])
        acc[...] += dg(r["g"][k], whole(ffn_full.at[0, k]), 1, 0)

    def norm_two_back(span):
        grad, normed = acc[span, :], r["n2"][span, :]
        vec[9:10] += rowsum(grad * normed)
        vec[10:11] += rowsum(grad)
        r["dr2"][span, :] = norm_rows_back(grad, normed, r["inv2"][span, 0:1], small[9:10])

    by_rows(length, norm_two_back)
    for name in ("dr2", "vec"):
        local.save(r[name], r[name + "_out"])
    for move in held:
        move.wait()
    local.drain()
    net.drain()


def forward_call(x, enc, seg, cot, attn_own, ffn_own, small):
    rows, width = attn_own.shape
    depth = lax.axis_size("dp") // 4
    length, enc_length = x.shape[0], enc.shape[0]
    heads = width // HEAD_DIM
    act, enc_act = ((length, width), BF), ((enc_length, width), BF)
    wide, aug, stack = ((length, width), F32), ((heads, length, PAIR), BF), ((2, depth, 2, 2, rows, width), BF)
    col = ((length, PAIR), F32)
    grads = ((2, depth, 2, 2, 2, rows // 2, width), BF)
    vec = ((-(-small.shape[0] // 8) * 8, width), F32)
    kept = dict(qa=aug, k=act, v=act, a=act, h1=act, n1=wide, inv1=col, qb=aug, k2=enc_act, v2=enc_act, a2=act, enc=enc_act, dr2=wide, vec=vec)
    outs = {"layer_out": wide, "attn_out": stack, "g_ffn": grads, **{name + "_out": kept[name] for name in FWD_SAVED}}
    inner = dict(kept, attn_full=stack, ffn_full=stack, q=act, bias=((length, length), F32), h1f=wide, t=wide, h2=act, n2=wide, inv2=col, g=((depth, length, width), BF), gp=((depth, length, width), F32), out=wide, dy=act, slots=((2, 2, 2, 2, rows // 2, width), BF))
    inside, anywhere = pl.BlockSpec(memory_space=pltpu.VMEM), pl.BlockSpec(memory_space=pl.ANY)
    args = dict(x=x, enc_own=enc, seg_row=seg, seg_col=seg.reshape(-1, 1), cot=cot, attn_own=attn_own, ffn_own=ffn_own, small=small)
    names = (*args, *outs, *inner, "send_sems", "recv_sems", "local_sems")
    got = pl.pallas_call(
        functools.partial(forward_kernel, names),
        out_shape=tuple(jax.ShapeDtypeStruct(*outs[name]) for name in outs),
        in_specs=[anywhere if name == "enc_own" else inside for name in args],
        out_specs=(anywhere,) * len(outs),
        scratch_shapes=[
            *[pltpu.VMEM(*inner[name]) for name in inner],
            pltpu.SemaphoreType.DMA((192,)),
            pltpu.SemaphoreType.DMA((192,)),
            pltpu.SemaphoreType.DMA((32,)),
        ],
        compiler_params=pltpu.CompilerParams(collective_id=0, has_side_effects=True, vmem_limit_bytes=62 << 20),
        name="gather_and_forward",
    )(*args.values())
    return dict(zip(outs, got))


def attend_pair_back(p, q_aug, k, v, a, da, dq, dk, dv, bias):
    lanes = pair_lanes(p)
    length, keys_all = da.shape[0], k.shape[0]
    half = length // 2
    blocks = [(half, half, keys_all), (0, half, keys_all)]
    if bias is not None:
        keys_all = length
        blocks = [(half, half, length), (0, half, half)]
    sums = None
    for first, rows, keys in blocks:
        span = pl.ds(first, rows)
        k_rows, v_rows = k[pl.ds(0, keys), lanes], v[pl.ds(0, keys), lanes]
        grad = da[span, lanes]
        grad_wide = grad.astype(F32)
        prod = grad_wide * a[span, lanes].astype(F32)
        q0, q1 = q_aug[2 * p, span, :], q_aug[2 * p + 1, span, :]
        q_t = (q0 * head_lanes(0) + q1 * head_lanes(1)).T
        grad_t = grad.T
        dqs, dks, dvs = [], [], []
        for h, q_h in ((0, q0), (1, q1)):
            lane = lane_ids(rows)
            own = (lane >= h * HEAD_DIM) & (lane < (h + 1) * HEAD_DIM)
            dot = jnp.sum(jnp.where(own, prod, 0.0), axis=-1, keepdims=True)
            spare = spare_lanes(h)
            keep = 1 - spare
            scores = dg(q_h, k_rows * keep + spare, 1, 1)
            if bias is not None:
                scores = scores + bias[span, pl.ds(0, keys)]
            prob = jnp.exp(scores)
            d_prob = dg(with_constant(grad_wide, -dot, h), v_rows * keep + spare, 1, 1)
            d_score = (prob * d_prob).astype(BF)
            own_rows = slice(h * HEAD_DIM, (h + 1) * HEAD_DIM)
            dqs.append(dg(d_score, k_rows, 1, 0))
            dvs.append(dg(grad_t[own_rows], prob.astype(BF), 1, 0))
            dks.append(dg(q_t[own_rows], d_score, 1, 0))
        d_q = jnp.where(lane_ids(rows) < HEAD_DIM, dqs[0], dqs[1]).astype(BF)
        dq[span, lanes] = (d_q.astype(F32) * (1.0 / math.sqrt(HEAD_DIM))).astype(BF)
        new = [jnp.concatenate(parts, 0) for parts in (dks, dvs)]
        if sums is None:
            sums = new
        else:
            sums = [
                old + term if keys == keys_all else jnp.concatenate([old[:, :keys] + term, old[:, keys:]], 1)
                for old, term in zip(sums, new)
            ]
    for ref, value in zip((dk, dv), sums):
        ref[pl.ds(0, keys_all), lanes] = value.astype(BF).T


def backward_kernel(names, *refs):
    r = dict(zip(names, refs))
    net = Net(r["send_sems"], r["recv_sems"])
    s, z, y, c = net.s, net.z, net.y, net.c
    local = Local(r["local_sems"])
    depth = net.depth
    small, vec, stack = r["small"], r["vec"], r["g_attn"]
    pairs = r["x"].shape[1] // PAIR
    length = r["x"].shape[0]
    net.greet([to for to in total_partners(net)[2:-1]])

    bufs = [{name: r[name + str(k)] for name in reduce_buffers(1, 2, 2 * CUT)} for k in range(4)]
    held = [None] * depth

    def load_own(side, z1):
        held[z1] = local.count
        local.copy(r["g_ffn"].at[side, z1, :, c], r["own"].at[z1])

    def own_ffn(z1, y1):
        return r["own"][z1, y1]

    f1 = reduce_ticks(net, r["g_ffn"].at[1], own_ffn, bufs[0], r["ffn_grad"], 1, "f1")
    f0 = reduce_ticks(net, r["g_ffn"].at[0], own_ffn, bufs[1], r["ffn_grad"], 0, "f0")
    cross = reduce_ticks(net, stack.at[1], lambda z1, y1: stack[1, z1, y1, c], bufs[2], r["attn_grad"], 1, "cross")
    self_ = reduce_ticks(net, stack.at[0], lambda z1, y1: stack[0, z1, y1, c], bufs[3], r["attn_grad"], 0, "self")

    loads = {}

    def load(key, src, dst):
        loads[key] = local.copy(src, dst)

    def load_weight(k, slot):
        load(("w", k), r["w"].at[k // depth, k % depth], r["slots"].at[slot])

    def weight(k, slot):
        loads[("w", k)].wait()
        return whole(r["slots"].at[slot])

    for z1 in range(depth):
        f1[0][z1]()
    load("dr2", r["dr2_in"], r["dr2"])
    load("a2", r["a2_in"], r["a"])
    load_weight(7, 0)
    for name in ("qb", "k2", "v2"):
        load(name, r[name + "_in"], r[name[0] + "s"])
    load("enc", r["enc_in"], r["enc"])
    load("h1", r["h1_in"], r["h1"])
    load_weight(5, 1)
    load_weight(6, 2)
    for z1 in range(depth):
        load_own(1, z1)
    for z1 in range(depth):
        f0[0][z1]()

    vec[...] = r["vec_in"][...]

    def cores_ffn(batch, z1, then):
        like = r["g_ffn"].at[0, z1, :, 0], r["own"].at[z1]
        pltpu.make_async_copy(*like, local.sems.at[held[z1]]).wait()
        batch[1][z1]()
        if then:
            load_own(0, z1)

    queue = [functools.partial(cores_ffn, f1, z1, True) for z1 in range(depth)]
    queue += [functools.partial(cores_ffn, f0, z1, False) for z1 in range(depth)]

    def several(*steps):
        return lambda: [step() for step in steps]

    queue = [several(*queue[:depth]), several(*queue[depth:])]
    queue += [several(*f1[2], f1[3][0]), f1[3][1], f1[3][2], several(*f0[2], f0[3][0])]

    def tick(p, at):
        if queue:
            run_when(p == at, queue.pop(0))

    def put(value, side, z1):
        stack[side, z1] = value.astype(BF).reshape(stack.shape[2:])

    def colsum(ref):
        return rowsum(ref.astype(F32))

    def low_dot(dst, left, right):
        half = left.shape[0] // 2
        for k in (0, 1):
            span = pl.ds(k * half, half)
            dst[span, :] = dg(left[span, :], right, 1, 1).astype(BF)

    def colsum_into(row, ref, rows):
        vec[row : row + 1] = jnp.zeros_like(vec[row : row + 1])

        def body(span):
            vec[row : row + 1] += colsum(ref[span, :])

        by_rows(rows, body)

    loads["dr2"].wait()

    def round_dr2(span):
        r["do"][span, :] = r["dr2"][span, :].astype(BF)

    by_rows(length, round_dr2)
    colsum_into(5, r["do"], length)
    loads["a2"].wait()
    low_dot(r["da"], r["do"], weight(7, 0))
    put(dg(r["a"][...], r["do"][...], 0, 0), 1, 3)
    cross[0][3]()
    load_weight(4, 0)
    for name in ("qb", "k2", "v2"):
        loads[name].wait()

    def cross_body(p, carry):
        for at in range(pairs):
            tick(p, at)
        attend_pair_back(p, r["qs"], r["ks"], r["vs"], r["a"], r["da"], r["dq"], r["dk"], r["dv"], None)
        return carry

    lax.fori_loop(0, pairs, cross_body, 0)
    load("qa", r["qa_in"], r["qs"])
    load("k", r["k_in"], r["ks"].at[pl.ds(0, length)])
    load("v", r["v_in"], r["vs"].at[pl.ds(0, length)])
    load("a", r["a_in"], r["a"])
    loads["h1"].wait()
    loads["enc"].wait()
    put(dg(r["h1"][...], r["dq"][...], 0, 0), 1, 0)
    cross[0][0]()
    put(dg(r["enc"][...], r["dk"][...], 0, 0), 1, 1)
    cross[0][1]()
    put(dg(r["enc"][...], r["dv"][...], 0, 0), 1, 2)
    cross[0][2]()
    load("n1", r["n1_in"], r["n1"])
    load("inv1", r["inv1_in"], r["inv1"])
    from_keys, from_values = weight(5, 1), weight(6, 2)
    quarter = r["enc"].shape[0] // 4
    for k in range(4):
        span = pl.ds(k * quarter, quarter)
        r["enc"][span, :] = (dg(r["dk"][span, :], from_keys, 1, 1) + dg(r["dv"][span, :], from_values, 1, 1)).astype(BF)
    for k in range(4):
        rows = pl.ds(k * quarter, quarter)
        net.send(r["enc"].at[rows], r["enc_got"].at[rows], net.at(s=1 - s), ("enc", k), lambda rows=rows: r["enc"].at[rows])
    load_weight(3, 1)
    colsum_into(3, r["dq"], length)
    colsum_into(4, r["dv"], r["dv"].shape[0])
    r["dr2"][...] += dg(r["dq"][...], weight(4, 0), 1, 1)
    load_weight(0, 2)
    load_weight(1, 0)
    for tick_ in cross[1]:
        tick_()
    loads["n1"].wait()
    loads["inv1"].wait()
    vec[7:8] = jnp.zeros_like(vec[7:8])
    vec[8:9] = jnp.zeros_like(vec[8:9])
    vec[2:3] = jnp.zeros_like(vec[2:3])

    def norm_one_back(span):
        grad, normed = r["dr2"][span, :], r["n1"][span, :]
        vec[7:8] += rowsum(grad * normed)
        vec[8:9] += rowsum(grad)
        grad = norm_rows_back(grad, normed, r["inv1"][span, 0:1], small[7:8])
        r["dr2"][span, :] = grad
        low = grad.astype(BF)
        r["do"][span, :] = low
        vec[2:3] += rowsum(low.astype(F32))

    by_rows(length, norm_one_back)
    low_dot(r["da"], r["do"], weight(3, 1))
    load_weight(2, 1)
    loads["a"].wait()
    put(dg(r["a"][...], r["do"][...], 0, 0), 0, 3)
    self_[0][3]()
    allowed_bias(r["bias"], r["seg_row"], r["seg_col"])
    for name in ("qa", "k", "v"):
        loads[name].wait()

    queue += [f1[3][3], f0[3][1], several(*f1[3][4:]), several(*cross[2], cross[3][0]), f0[3][2]]

    def self_body(p, carry):
        for at in range(pairs):
            tick(p, at)
        attend_pair_back(p, r["qs"], r["ks"], r["vs"], r["a"], r["da"], r["dq"], r["dk"], r["dv"], r["bias"])
        return carry

    lax.fori_loop(0, pairs, self_body, 0)
    x = r["x"]
    near = pl.ds(0, length)
    put(dg(x[...], r["dq"][...], 0, 0), 0, 0)
    self_[0][0]()
    put(dg(x[...], r["dk"][near, :], 0, 0), 0, 1)
    self_[0][1]()
    put(dg(x[...], r["dv"][near, :], 0, 0), 0, 2)
    self_[0][2]()
    colsum_into(0, r["dq"], length)
    colsum_into(1, r["dv"], length)
    r["sums"][0] = vec[...]
    total = total_ticks(net, r["sums"], r["sum_got"], "small")
    total.pop(0)()
    while queue:
        queue.pop(0)()
    r["dr2"][...] += dg(r["dq"][...], weight(0, 2), 1, 1)
    for tick_ in self_[1]:
        tick_()
    r["dr2"][...] += dg(r["dk"][near, :], weight(1, 0), 1, 1)
    cross[3][1]()
    r["dr2"][...] += dg(r["dv"][near, :], weight(2, 1), 1, 1)
    local.save(r["dr2"], r["input_grad"])
    total.pop(0)()
    f0[3][3]()
    cross[3][2]()
    total.pop(0)()
    for tick_ in f0[3][4:]:
        tick_()
    cross[3][3]()
    for tick_ in self_[2]:
        tick_()
    self_[3][0]()
    total.pop(0)()
    self_[3][1]()
    for tick_ in cross[3][4:]:
        tick_()
    self_[3][2]()
    total.pop(0)()
    for k in range(4):
        net.recv(r["enc_got"].at[pl.ds(k * quarter, quarter)], ("enc", k))

    for k in (0, 1):

        def widen(span, k=k):
            r["n1"][span, :] = r["enc_got"][pl.ds(span.start + k * length, span.size), :].astype(F32)

        by_rows(length, widen)
        local.copy(r["n1"], r["enc_grad"].at[pl.ds(k * length, length)]).wait()
    while total:
        total.pop(0)()
    for tick_ in self_[3][3:]:
        tick_()
    r["small_grad"][...] = r["sums"][r["sums"].shape[0] - 1]
    local.drain()
    net.drain()


def backward_call(x, seg, small, kept, rows):
    width = x.shape[1]
    depth = lax.axis_size("dp") // 4
    devices = lax.axis_size("dp") * 2
    length, enc_length = x.shape[0], kept["enc_out"].shape[0]
    heads = width // HEAD_DIM
    steps = net_bits(devices)
    act, enc_act, wide = ((length, width), BF), ((enc_length, width), BF), ((length, width), F32)
    own_rows = ((2, rows // 2, width), F32)
    vec = (kept["vec_out"].shape, F32)
    outs = dict(input_grad=wide, enc_grad=((enc_length, width), F32), attn_grad=own_rows, ffn_grad=own_rows, small_grad=vec)
    inner = dict(
        g_attn=((2, depth, 2, 2, 2, rows // 2, width), BF),
        own=((depth, 2, 2, rows // 2, width), BF),
        slots=((3, 2, 2, rows, width), BF),
        qs=((heads, length, PAIR), BF),
        ks=enc_act, vs=enc_act, enc=enc_act, enc_got=enc_act, a=act, h1=act, da=act, do=act, dq=act, dk=enc_act, dv=enc_act,
        dr2=wide, n1=wide, inv1=((length, PAIR), F32), bias=((length, length), F32), vec=vec,
        sums=((steps + 1, *vec[0]), F32), sum_got=((steps, *vec[0]), F32),
    )
    for k in range(4):
        inner.update({name + str(k): (shape, BF) for name, shape in reduce_buffers(depth, rows, width).items()})
    inside, anywhere = pl.BlockSpec(memory_space=pltpu.VMEM), pl.BlockSpec(memory_space=pl.ANY)
    args = dict(x=x, seg_row=seg, seg_col=seg.reshape(-1, 1), small=small, vec_in=kept["vec_out"])
    far = {name + "_in": kept[name + "_out"] for name in ("dr2", "a2", "qb", "k2", "v2", "enc", "h1", "qa", "k", "v", "a", "n1", "inv1")}
    far.update(w=kept["attn_out"], g_ffn=kept["g_ffn"])
    names = (*args, *far, *outs, *inner, "send_sems", "recv_sems", "local_sems")
    got = pl.pallas_call(
        functools.partial(backward_kernel, names),
        out_shape=tuple(jax.ShapeDtypeStruct(*outs[name]) for name in outs),
        in_specs=[inside] * len(args) + [anywhere] * len(far),
        out_specs=tuple(anywhere if name in ("input_grad", "enc_grad") else inside for name in outs),
        scratch_shapes=[
            *[pltpu.VMEM(*inner[name]) for name in inner],
            pltpu.SemaphoreType.DMA((192,)),
            pltpu.SemaphoreType.DMA((192,)),
            pltpu.SemaphoreType.DMA((48,)),
        ],
        compiler_params=pltpu.CompilerParams(collective_id=1, has_side_effects=True, vmem_limit_bytes=63 << 20),
        name="backward_and_sum",
    )(*args.values(), *far.values())
    return dict(zip(outs, got))


def partner(value, axis, apart):
    mask = 2**apart
    pairs = [(source, source ^ mask) for source in range(lax.axis_size(axis))]
    return lax.ppermute(value, axis, pairs)


def matmul(left_op, right_op):
    return jnp.dot(left_op, right_op, preferred_element_type=jnp.float32)


def contract_rows(left_op, right_op):
    return lax.dot_general(
        left_op, right_op, (((0,), (0,)), ((), ())), preferred_element_type=jnp.float32
    )


def contract_cols(left_op, right_op):
    return lax.dot_general(
        left_op, right_op, (((1,), (1,)), ((), ())), preferred_element_type=jnp.float32
    )


def gelu_exact(pre_value):
    return jax.nn.gelu(pre_value, approximate=False)


def split_heads(matrix):
    return matrix.reshape(matrix.shape[0], HEADS, HEAD_DIM)


def merge_heads(tensor):
    return tensor.reshape(tensor.shape[0], HEADS * HEAD_DIM)


def column_sum(grad_low):
    return jnp.sum(grad_low.astype(jnp.float32), axis=0)


def norm_forward(residual, norm_gain, norm_shift):
    row_mean = jnp.mean(residual, axis=-1, keepdims=True)
    centered = residual - row_mean
    row_var = jnp.mean(centered * centered, axis=-1, keepdims=True)
    inv_std = lax.rsqrt(row_var + EPSILON)
    normed = centered * inv_std
    return (normed * norm_gain + norm_shift, normed, inv_std)


def norm_backward(grad_out, normed, inv_std, norm_gain):
    grad_norm = grad_out * norm_gain
    centered_grad = grad_norm - jnp.mean(grad_norm, axis=-1, keepdims=True)
    grad_res = inv_std * (
        centered_grad - normed * jnp.mean(grad_norm * normed, axis=-1, keepdims=True)
    )
    return (grad_res, jnp.sum(grad_out * normed, axis=0), jnp.sum(grad_out, axis=0))


def block_scores(q_block, keys_in, seg_row, first_row):
    scores = jnp.einsum("qhd,khd->hqk", q_block, keys_in, preferred_element_type=jnp.float32)
    if seg_row is None:
        return scores
    block_len = q_block.shape[0]
    query_pos = first_row + jnp.arange(block_len)
    key_pos = jnp.arange(seg_row.shape[0])
    allowed = (key_pos[None, :] <= query_pos[:, None]) & (seg_row[:, None] == seg_row[None, :])
    return jnp.where(allowed[None], scores, NEG_FILL)


def attend_forward(queries, keys_in, values_in, seg_row):
    scores = block_scores(queries, keys_in, seg_row, 0)
    row_max = jnp.max(scores, axis=-1, keepdims=True)
    exp_scores = jnp.exp(scores - row_max)
    totals = jnp.sum(exp_scores, axis=-1, keepdims=True)
    attn_prob = (exp_scores / totals).astype(jnp.bfloat16)
    outputs = jnp.einsum("hqk,khd->qhd", attn_prob, values_in, preferred_element_type=jnp.float32)
    lse_list = [row_max + jnp.log(totals)]
    return (outputs, lse_list)


def attend_backward(queries, keys_in, values_in, seg_row, lse_list, grad_mixed):
    query_len = queries.shape[0]
    block_len = min(512, query_len)
    grad_queries = []
    grad_keys = jnp.zeros(keys_in.shape, jnp.float32)
    grad_values = jnp.zeros(values_in.shape, jnp.float32)
    for block_index, first_row in enumerate(range(0, query_len, block_len)):
        scores = block_scores(queries, keys_in, seg_row, first_row)
        attn_prob = jnp.exp(scores - lse_list[block_index])
        grad_values = jnp.einsum(
            "hqk,qhd->khd",
            attn_prob.astype(jnp.bfloat16),
            grad_mixed,
            preferred_element_type=jnp.float32,
        )
        grad_prob = jnp.einsum(
            "qhd,khd->hqk", grad_mixed, values_in, preferred_element_type=jnp.float32
        )
        grad_scores = attn_prob * (
            grad_prob - jnp.sum(grad_prob * attn_prob, axis=-1, keepdims=True)
        )
        grad_low = grad_scores.astype(jnp.bfloat16)
        grad_queries.append(
            jnp.einsum("hqk,khd->qhd", grad_low, keys_in, preferred_element_type=jnp.float32)
        )
        grad_keys = jnp.einsum(
            "hqk,qhd->khd", grad_low, queries, preferred_element_type=jnp.float32
        )
    grad_q_all = grad_queries[0].astype(jnp.bfloat16)
    return (grad_q_all, grad_keys.astype(jnp.bfloat16), grad_values.astype(jnp.bfloat16))


def layer_row(dec_row, enc_row, seg_row, cot_row, blocks, w_in, w_out, vectors):
    w_query, w_key, w_value, w_proj, c_query, c_key, c_value, c_proj = blocks
    scale = 1.0 / math.sqrt(HEAD_DIM)
    bias_in = vectors[13:].reshape(-1)
    dec_full = dec_row.astype(jnp.float32)
    queries = ((matmul(dec_row, w_query) + vectors[0]) * scale).astype(jnp.bfloat16)
    keys_self = matmul(dec_row, w_key).astype(jnp.bfloat16)
    vals_self = (matmul(dec_row, w_value) + vectors[1]).astype(jnp.bfloat16)
    mixed_self, lse_self = attend_forward(
        split_heads(queries), split_heads(keys_self), split_heads(vals_self), seg_row
    )
    self_flat = merge_heads(mixed_self).astype(jnp.bfloat16)
    self_out = matmul(self_flat, w_proj) + vectors[2]
    hidden_one, normed_one, inv_one = norm_forward(dec_full + self_out, vectors[7], vectors[8])
    hidden_one_low = hidden_one.astype(jnp.bfloat16)
    cross_q = ((matmul(hidden_one_low, c_query) + vectors[3]) * scale).astype(jnp.bfloat16)
    cross_k = matmul(enc_row, c_key).astype(jnp.bfloat16)
    cross_v = (matmul(enc_row, c_value) + vectors[4]).astype(jnp.bfloat16)
    mixed_cross, lse_cross = attend_forward(
        split_heads(cross_q), split_heads(cross_k), split_heads(cross_v), None
    )
    cross_flat = merge_heads(mixed_cross).astype(jnp.bfloat16)
    cross_out = matmul(cross_flat, c_proj) + vectors[5]
    hidden_two, normed_two, inv_two = norm_forward(hidden_one + cross_out, vectors[9], vectors[10])
    hidden_two_low = hidden_two.astype(jnp.bfloat16)
    pre_act = contract_cols(hidden_two_low, w_in) + bias_in
    act_full, act_pull = jax.vjp(gelu_exact, pre_act)
    act_low = act_full.astype(jnp.bfloat16)
    ffn_out = matmul(act_low, w_out) + vectors[6]
    result, normed_three, inv_three = norm_forward(hidden_two + ffn_out, vectors[11], vectors[12])
    grad_r3, grad_g3, grad_e3 = norm_backward(cot_row, normed_three, inv_three, vectors[11])
    grad_y = grad_r3.astype(jnp.bfloat16)
    grad_w_out = contract_rows(act_low, grad_y)
    grad_act = contract_cols(grad_y, w_out)
    grad_pre = act_pull(grad_act)[0].astype(jnp.bfloat16)
    grad_w_in = contract_rows(grad_pre, hidden_two_low)
    grad_h2 = grad_r3 + matmul(grad_pre, w_in)
    grad_r2, grad_g2, grad_e2 = norm_backward(grad_h2, normed_two, inv_two, vectors[9])
    grad_co = grad_r2.astype(jnp.bfloat16)
    grad_c_proj = contract_rows(cross_flat, grad_co)
    grad_mix_c = contract_cols(grad_co, c_proj).astype(jnp.bfloat16)
    grad_q_c, grad_k_c, grad_v_c = attend_backward(
        split_heads(cross_q),
        split_heads(cross_k),
        split_heads(cross_v),
        None,
        lse_cross,
        split_heads(grad_mix_c),
    )
    grad_cq = merge_heads(grad_q_c) * scale
    grad_ck = merge_heads(grad_k_c)
    grad_cv = merge_heads(grad_v_c)
    grad_c_query = contract_rows(hidden_one_low, grad_cq)
    grad_h1 = grad_r2 + contract_cols(grad_cq, c_query)
    grad_r1, grad_g1, grad_e1 = norm_backward(grad_h1, normed_one, inv_one, vectors[7])
    grad_so = grad_r1.astype(jnp.bfloat16)
    grad_w_proj = contract_rows(self_flat, grad_so)
    grad_mix_s = contract_cols(grad_so, w_proj).astype(jnp.bfloat16)
    grad_q_s, grad_k_s, grad_v_s = attend_backward(
        split_heads(queries),
        split_heads(keys_self),
        split_heads(vals_self),
        seg_row,
        lse_self,
        split_heads(grad_mix_s),
    )
    grad_sq = merge_heads(grad_q_s) * scale
    grad_sk = merge_heads(grad_k_s)
    grad_sv = merge_heads(grad_v_s)
    grad_w_query = contract_rows(dec_row, grad_sq)
    grad_w_key = contract_rows(dec_row, grad_sk)
    grad_w_value = contract_rows(dec_row, grad_sv)
    grad_input = (
        grad_r1
        + contract_cols(grad_sq, w_query)
        + contract_cols(grad_sk, w_key)
        + contract_cols(grad_sv, w_value)
    )
    vec_rows = jnp.stack(
        [
            column_sum(grad_sq),
            column_sum(grad_sv),
            column_sum(grad_so),
            column_sum(grad_cq),
            column_sum(grad_cv),
            column_sum(grad_co),
            column_sum(grad_y),
            grad_g1,
            grad_e1,
            grad_g2,
            grad_e2,
            grad_g3,
            grad_e3,
        ]
    )
    vec_grad = jnp.concatenate([vec_rows, column_sum(grad_pre).reshape(-1, vectors.shape[1])], 0)
    row_mats = (grad_w_query, grad_w_key, grad_w_value, grad_w_proj, grad_c_query, grad_c_proj)
    return (result, grad_input, grad_ck, grad_cv, row_mats, grad_w_in, grad_w_out, vec_grad)


def nesterov(master, moment, average, grad, rate):
    new_moment = MOMENTUM * moment + grad
    new_master = master - rate * (grad + MOMENTUM * new_moment)
    new_average = AVG_DECAY * average + (1.0 - AVG_DECAY) * new_master
    return (new_master, new_moment, new_average)


def local(
    decoder_in,
    encoder_out,
    segment_ids,
    cotangent,
    attn_master,
    ffn_master,
    small_master,
    attn_moment,
    ffn_moment,
    small_moment,
    attn_average,
    ffn_average,
    small_average,
    rate_matrix,
    rate_vector,
):
    if attn_master.shape[0] % 32 == 0 and lax.axis_size("dp") % 4 == 0 and decoder_in.shape[0] == 1:
        kept = forward_call(
            decoder_in[0], encoder_out[0], segment_ids, cotangent[0], attn_master, ffn_master, small_master
        )
        got = backward_call(decoder_in[0], segment_ids, small_master, kept, attn_master.shape[0])
        layer_out, input_grad, encoder_grad = kept["layer_out"][None], got["input_grad"][None], got["enc_grad"][None]
        attn_grad, ffn_grad = (got[name].reshape(attn_master.shape) for name in ("attn_grad", "ffn_grad"))
        small_grad = got["small_grad"][: small_master.shape[0]]
    else:
        matrices, ffn_all = (
            lax.all_gather(attn_master.astype(jnp.bfloat16), ("side", "dp"), axis=0, tiled=True),
            lax.all_gather(ffn_master.astype(jnp.bfloat16), ("side", "dp"), axis=0, tiled=True),
        )
        model_width = matrices.shape[1]
        hidden_units = ffn_all.shape[0] // 2
        blocks = [
            matrices[block_index * model_width : (block_index + 1) * model_width]
            for block_index in range(8)
        ]
        w_in = ffn_all[:hidden_units]
        w_out = ffn_all[hidden_units:]
        partner_enc = partner(encoder_out, "side", 0)
        mat_grads = [jnp.zeros((model_width, model_width), jnp.float32) for block_index in range(8)]
        slots = (0, 1, 2, 3, 4, 7)
        row_index = 0
        outcome = layer_row(
            decoder_in[row_index],
            partner_enc[row_index],
            segment_ids[row_index],
            cotangent[row_index],
            blocks,
            w_in,
            w_out,
            small_master,
        )
        result, grad_input, grad_ck, grad_cv, row_mats, grad_w_in, grad_w_out, vec_grad = outcome
        layer_out = result[None]
        input_grad = grad_input[None]
        key_grads = [grad_ck]
        value_grads = [grad_cv]
        for slot_index, slot_grad in zip(slots, row_mats):
            mat_grads[slot_index] = slot_grad
        returned = partner(jnp.stack([jnp.stack(key_grads), jnp.stack(value_grads)]), "side", 0)
        row_index = 0
        own_rows = encoder_out[row_index]
        mat_grads[5] = contract_rows(own_rows, returned[0, row_index])
        mat_grads[6] = contract_rows(own_rows, returned[1, row_index])
        enc_grads = [
            contract_cols(returned[0, row_index], blocks[5])
            + contract_cols(returned[1, row_index], blocks[6])
        ]
        encoder_grad = jnp.stack(enc_grads)
        attn_total = jnp.concatenate(mat_grads, 0)
        ffn_total = jnp.concatenate([grad_w_in, grad_w_out], 0)
        attn_grad, ffn_grad = (
            lax.psum_scatter(attn_total, ("side", "dp"), scatter_dimension=0, tiled=True),
            lax.psum_scatter(ffn_total, ("side", "dp"), scatter_dimension=0, tiled=True),
        )
        small_grad = lax.psum(vec_grad, ("side", "dp"))
    attn_new, attn_moment_new, attn_average_new = nesterov(
        attn_master, attn_moment, attn_average, attn_grad, rate_matrix
    )
    ffn_new, ffn_moment_new, ffn_average_new = nesterov(
        ffn_master, ffn_moment, ffn_average, ffn_grad, rate_matrix
    )
    small_new, small_moment_new, small_average_new = nesterov(
        small_master, small_moment, small_average, small_grad, rate_vector
    )
    return (
        layer_out,
        input_grad,
        encoder_grad,
        attn_grad,
        ffn_grad,
        small_grad,
        attn_new,
        ffn_new,
        small_new,
        attn_moment_new,
        ffn_moment_new,
        small_moment_new,
        attn_average_new,
        ffn_average_new,
        small_average_new,
    )


def solution(mesh):
    placed = (
        P(("side", "dp"), None, None),
        P(("side", "dp"), None, None),
        P(("side", "dp"), None),
        P(("side", "dp"), None, None),
        P(("side", "dp"), None),
        P(("side", "dp"), None),
        P(),
        P(("side", "dp"), None),
        P(("side", "dp"), None),
        P(),
        P(("side", "dp"), None),
        P(("side", "dp"), None),
        P(),
        P(),
        P(),
    )
    return jax.shard_map(
        local,
        mesh=mesh,
        in_specs=placed,
        out_specs=(
            P(("side", "dp"), None, None),
            P(("side", "dp"), None, None),
            P(("side", "dp"), None, None),
            P(("side", "dp"), None),
            P(("side", "dp"), None),
            P(),
            P(("side", "dp"), None),
            P(("side", "dp"), None),
            P(),
            P(("side", "dp"), None),
            P(("side", "dp"), None),
            P(),
            P(("side", "dp"), None),
            P(("side", "dp"), None),
            P(),
        ),
        check_vma=False,
    )
```

```python
import functools
import math
import types

import jax
import jax.numpy as jnp
from jax import lax
from jax.experimental import pallas as pl
from jax.experimental.pallas import tpu as pltpu
from jax.sharding import PartitionSpec as P

HEADS = 12
HEAD_DIM = 64


NEG_FILL = -1e30
EPSILON = 1e-05
MOMENTUM = 0.5
AVG_DECAY = 0.5


SIDE = "side"
DP = "dp"
ROUTE_A = "A"
ROUTE_B = "B"
UP = "up"
DOWN = "down"
L = "l"
CORE = "core"
F = "f"
FIRST = "first"
NEAR = "near"
ALONG = "along"
ACROSS = "across"
XA = "xa"
EA = "ea"
EB = "eb"
YB = "yb"
XC = "xc"
C = "c"
SLOT = "slot"
YA = "ya"
XB = "xb"
ZA = "za"
ZB = "zb"
START = "start"
CORES = "cores"
PLANES = "planes"
WAVE = "wave"
LAST = "last"
STEP = "step"
BEGIN = "begin"
SEG = "seg"
SEND = "send"
ATTN = "attn"
FFN = "ffn"
X = "x"
COT = "cot"
RECV = "recv"
WEIGHTS = "weights"
SELF = "self"
NORM1 = "norm1"
KEYS = "keys"
VALUES = "values"
CROSS = "cross"
NORM2 = "norm2"
FFN_DONE = "ffn_done"
NORM3 = "norm3"
LO = "lo"
DW2 = "dw2"
F1 = "f1"
DW1 = "dw1"
F0 = "f0"
NORM2_BACK = "norm2_back"
CROSS_BACK = "cross_back"
CR = "cr"
DCQ = "dcq"
DCK = "dck"
DCV = "dcv"
DWO = "dwo"
SELF_BACK = "self_back"
SL = "sl"
SR = "sr"
VEC = "vec"
SM = "sm"
DX = "dx"
IG = "ig"
LOADS = "loads"
ENC = "enc"
END = "end"
END2 = "end2"
END3 = "end3"
FFN_GRAD = "ffn_grad"
ATTN_GRAD = "attn_grad"
_MORE = "_more"
ENC_GRAD = "enc_grad"
QHD_KHD_HQK = "qhd,khd->hqk"
HQK_KHD_QHD = "hqk,khd->qhd"
HQK_QHD_KHD = "hqk,qhd->khd"

MESH_ID = pl.DeviceIdType.MESH
BF = jnp.bfloat16
F32 = jnp.float32
CUT = 512


def run_when(cond, body):
    @pl.when(cond)
    def _():
        body()


class Net:
    def __init__(self, send_sems, recv_sems):
        self.s = lax.axis_index(SIDE)
        self.d = lax.axis_index(DP)
        self.z, self.y, self.c = self.d // 4, (self.d // 2) % 2, self.d % 2
        self.depth = lax.axis_size(DP) // 4
        self.send_sems, self.recv_sems = send_sems, recv_sems
        self.sent, self.slots, self.conds = [], {}, []
        self.low = [self.z >= k for k in range(self.depth)]
        self.high = [self.z < self.depth - k for k in range(self.depth)]
        self.here = [self.z == k for k in range(self.depth)]
        self.away = [self.s != k for k in (0, 1)]
        self.away_y = [self.y != k for k in (0, 1)]
        self.home = [self.s == k for k in (0, 1)]

    def at(self, s=None, z=None, y=None, c=None):
        s, z, y, c = (own if got is None else got for got, own in ((s, self.s), (z, self.z), (y, self.y), (c, self.c)))
        return (s, (z * 2 + y) * 2 + c)

    def slot(self, key):
        return self.slots.setdefault(key, len(self.slots))

    def copy(self, src, dst, to, send_slot, recv_slot):
        return pltpu.make_async_remote_copy(
            src_ref=src,
            dst_ref=dst,
            send_sem=self.send_sems.at[send_slot],
            recv_sem=self.recv_sems.at[recv_slot],
            device_id=to,
            device_id_type=MESH_ID,
        )

    def send(self, src, dst, to, key, like, group=None):
        send_slot, recv_slot = len(self.sent), self.slot(key)
        self.copy(src, dst, to, send_slot, recv_slot).start()
        peer = (self.s, self.d)
        wait = lambda: self.copy(like(), like(), peer, send_slot, recv_slot).wait_send()
        self.sent.append((wait, tuple(self.conds), group))

    def recv(self, dst, key):
        self.copy(dst, dst, self.at(c=1 - self.c), 0, self.slot(key)).wait_recv()

    def when(self, cond, body):
        self.conds.append(cond)
        run_when(cond, body)
        self.conds.pop()

    def drain(self):
        assert max(len(self.sent), len(self.slots)) <= min(self.send_sems.shape[0], self.recv_sems.shape[0])
        for k, entry in enumerate(self.sent):
            if entry is not None:
                wait, conds, _ = entry
                for cond in conds:
                    wait = functools.partial(run_when, cond, wait)
                wait()
                self.sent[k] = None

    def drain_one(self, group):
        for k, entry in enumerate(self.sent):
            if entry is not None and entry[2] == group:
                entry[0]()
                self.sent[k] = None

    def greet(self, others=()):
        barrier = pltpu.get_barrier_semaphore()
        partners = [self.at(s=1 - self.s), self.at(y=1 - self.y), self.at(c=1 - self.c), *others]
        for to in partners:
            pl.semaphore_signal(barrier, inc=1, device_id=to, device_id_type=MESH_ID)
        low, high = self.low[1], self.high[1]

        def signal(to):
            pl.semaphore_signal(barrier, inc=1, device_id=to, device_id_type=MESH_ID)

        pl.when(low)(lambda: signal(self.at(z=self.z - 1)))
        pl.when(high)(lambda: signal(self.at(z=self.z + 1)))
        pl.semaphore_wait(barrier, len(partners) + low.astype(jnp.int32) + high.astype(jnp.int32))


def gather_ticks(net, full, tag):
    depth, width = net.depth, full.shape[-1]
    cols = {ROUTE_A: pl.ds(0, CUT), ROUTE_B: pl.ds(CUT, width - CUT)}
    coord = {ROUTE_A: (net.s, net.y), ROUTE_B: (net.y, net.s)}
    other = {ROUTE_A: net.away, ROUTE_B: net.away_y}
    z, c = net.z, net.c

    def part(p, f, z_of, l, core):
        s, y = (f, l) if p == ROUTE_A else (l, f)
        return full.at[s, z_of, y, core, :, cols[p]]

    def dev(p, f, z_of, l, core):
        s, y = (f, l) if p == ROUTE_A else (l, f)
        return net.at(s, z_of, y, core)

    def like(p):
        return lambda: full.at[0, 0, 0, 0, :, cols[p]]

    def spread(p, f_of, rel, ways):
        f, l = coord[p]
        got = part(p, f_of, z + rel, l, c)
        if UP in ways and 1 - rel < depth:
            key = (tag, p, UP, 1 - rel, f_of)
            net.when(net.high[1], lambda: net.send(got, got, dev(p, f, z + 1, l, c), key, like(p)))
        if DOWN in ways and 1 + rel < depth:
            key = (tag, p, DOWN, 1 + rel, f_of)
            net.when(net.low[1], lambda: net.send(got, got, dev(p, f, z - 1, l, c), key, like(p)))
        net.send(got, got, dev(p, f, z, 1 - l, c), (tag, p, L, rel, f_of), like(p))

    def exists(rel, body):
        if rel == 0:
            body()
        else:
            net.when(net.low[-rel] if rel < 0 else net.high[rel], body)

    def to_core(p, rel, f_of, l_rel):
        f, l = coord[p]
        got = part(p, f_of, z + rel, l if l_rel == 0 else 1 - l, c)
        net.send(got, got, net.at(c=1 - c), (tag, p, CORE, rel, f_of, l_rel), like(p))

    def first(p):
        f, l = coord[p]
        got = part(p, f, z, l, c)
        net.send(got, got, dev(p, 1 - f, z, l, c), (tag, p, F), like(p))

    def near(p, f_of):
        f, l = coord[p]
        net.when(other[p][f_of], lambda: net.recv(part(p, f_of, z, l, c), (tag, p, F)))
        spread(p, f_of, 0, (UP, DOWN))
        to_core(p, 0, f_of, 0)

    def along(p, dist, f_of):
        f, l = coord[p]
        for way, rel in ((UP, -dist), (DOWN, dist)):

            def body(way=way, rel=rel):
                net.recv(part(p, f_of, z + rel, l, c), (tag, p, way, dist, f_of))
                spread(p, f_of, rel, (way,))
                to_core(p, rel, f_of, 0)

            exists(rel, body)

    def across(p, dist, f_of):
        f, l = coord[p]
        for rel in sorted({-dist, dist}):

            def body(rel=rel):
                net.recv(part(p, f_of, z + rel, 1 - l, c), (tag, p, L, rel, f_of))
                to_core(p, rel, f_of, 1)

            exists(rel, body)

    def from_core(p, f_of, side):
        f, l = coord[p]

        def body(l_rel):
            for rel in range(1 - depth, depth):
                got = lambda rel=rel: part(p, f_of, z + rel, l if l_rel == 0 else 1 - l, 1 - c)
                exists(rel, lambda rel=rel: net.recv(got(), (tag, p, CORE, rel, f_of, l_rel)))

        if p == ROUTE_A:
            body(0)
            body(1)
        else:
            net.when(net.home[side], lambda: body(0))
            net.when(net.away[side], lambda: body(1))

    ticks = {}
    for p in "AB":
        ticks[FIRST, p] = functools.partial(first, p)
        for f_of in (0, 1):
            ticks[NEAR, p, f_of] = functools.partial(near, p, f_of)
            for dist in range(1, depth):
                ticks[ALONG, p, dist, f_of] = functools.partial(along, p, dist, f_of)
            for dist in range(depth):
                ticks[ACROSS, p, dist, f_of] = functools.partial(across, p, dist, f_of)
            for side in (0, 1):
                if p == ROUTE_B or side == f_of:
                    ticks[CORE, p, f_of, side] = functools.partial(from_core, p, f_of, side)
    return ticks


def reduce_extra(rows, cut, rest):
    half = rows // 2
    return {XA: (rows, cut), EA: (rows, cut), EB: (2, half, rest), YB: (half, rest), XC: (half, rest)}


def reduce_ticks(net, slots, own, room, extra, out, side, tag, columns):
    depth, rows = net.depth, room.shape[-2]
    first, cut, rest = columns
    half = rows // 2
    s, z, y, c = net.s, net.z, net.y, net.c
    a_cols, b_cols, cols = pl.ds(first, cut), pl.ds(first + cut, rest), pl.ds(first, cut + rest)
    x_dev, y_dev, c_dev = net.at(s=1 - s), net.at(y=1 - y), net.at(c=1 - c)

    def part_of(which):
        return pl.ds(pl.multiple_of(which * half, half), half)

    mine, theirs = part_of(s), part_of(1 - s)
    rc = room.at[:, :, 0]
    ya = lambda z1: room.at[z1, 0, 1, :, a_cols]
    xb = lambda z1: room.at[z1, :, 1, pl.ds(0, half), b_cols]
    za = lambda place: room.at[place, 1, 1, :, a_cols] if place < depth else extra[EA]
    zb = lambda place: room.at[place, :, 1, pl.ds(half, half), b_cols] if place < depth else extra[EB]

    def start(z1, slot):
        like = lambda: rc.at[z1, :, :, cols]
        net.send(slots.at[slot, :, 1 - c, :, cols], like(), c_dev, (tag, C, z1), like, (SLOT, slot))

    def cores(z1):
        net.recv(rc.at[z1, :, :, cols], (tag, C, z1))
        for y1 in (0, 1):
            rc[z1, y1, :, cols] = rc[z1, y1, :, cols] + own[z1, y1, :, cols]
        net.send(rc.at[z1, 1 - y, :, a_cols], ya(z1), y_dev, (tag, YA, z1), lambda: ya(z1))
        net.send(rc.at[z1, :, theirs, b_cols], xb(z1), x_dev, (tag, XB, z1), lambda: xb(z1))

    def add_a(z1, ref):
        rc[z1, y, :, a_cols] = rc[z1, y, :, a_cols] + ref[...]

    def add_b(z1, ref):
        for y1 in (0, 1):
            rc[z1, y1, mine, b_cols] = rc[z1, y1, mine, b_cols] + ref[y1]

    def planes(z1):
        net.recv(ya(z1), (tag, YA, z1))
        add_a(z1, ya(z1))
        net.recv(xb(z1), (tag, XB, z1))
        add_b(z1, xb(z1))

    def wave(k, j):
        def go(way, z_here, z1):
            step = 1 if way == UP else -1
            place = z1 + 1 if way == UP else z1
            if k > 0:
                net.recv(za(place), (tag, ZA, place))
                add_a(z1, za(place))
                net.recv(zb(place), (tag, ZB, place))
                add_b(z1, zb(place))
            if z1 != z_here:
                to = net.at(z=z + step)
                net.send(rc.at[z1, y, :, a_cols], za(place), to, (tag, ZA, place), lambda: za(place))
                net.send(rc.at[z1, :, mine, b_cols], zb(place), to, (tag, ZB, place), lambda: zb(place))

        net.when(net.here[k], lambda: go(UP, k, depth - 1 - j))
        net.when(net.here[depth - 1 - k], lambda: go(DOWN, depth - 1 - k, j))

    def last_one():
        net.send(rc.at[z, 1 - y, mine, b_cols], extra[YB], y_dev, (tag, YB), lambda: extra[YB])
        net.when(
            net.away[side],
            lambda: net.send(rc.at[z, y, :, a_cols], extra[XA], x_dev, (tag, XA), lambda: extra[XA]),
        )

    def last_two():
        net.recv(extra[YB], (tag, YB))
        rc[z, y, mine, b_cols] = rc[z, y, mine, b_cols] + extra[YB][...]
        net.when(
            net.away[side],
            lambda: net.send(rc.at[z, y, mine, b_cols], extra[XC], x_dev, (tag, XC), lambda: extra[XC]),
        )

    def last_three():
        def body():
            net.recv(extra[XA], (tag, XA))
            total, more = out
            total[:, a_cols], more[:, a_cols] = rc[z, y, :, a_cols], extra[XA][...]
            total[mine, b_cols] = rc[z, y, mine, b_cols]
            net.recv(extra[XC], (tag, XC))
            total[theirs, b_cols] = extra[XC][...]
            more[:, b_cols] = jnp.zeros((rows, rest), BF)

        net.when(net.home[side], body)

    ticks = {}
    for z1 in range(depth):
        ticks[START, z1] = functools.partial(start, z1)
        ticks[CORES, z1] = functools.partial(cores, z1)
        ticks[PLANES, z1] = functools.partial(planes, z1)
        for j in range(depth - z1):
            ticks[WAVE, z1, j] = functools.partial(wave, z1, j)
    ticks[LAST, 1], ticks[LAST, 2], ticks[LAST, 3] = last_one, last_two, last_three
    return ticks


def flip_bit(index, bit):
    return index + bit * (1 - 2 * ((index // bit) % 2))


def total_partners(net):
    bits = [2**k for k in range(net_bits(lax.axis_size(DP)))]
    return [(net.s, flip_bit(net.d, bit)) for bit in bits] + [(1 - net.s, net.d)]


def net_bits(number):
    return number.bit_length() - 1


def total_ticks(net, sums, got, tag):
    partners = total_partners(net)

    def start(k):
        net.send(sums.at[k], got.at[k], partners[k], (tag, k), lambda: got.at[k])

    def finish(k):
        net.recv(got.at[k], (tag, k))
        sums[k + 1] = sums[k] + got[k]
        if k + 1 < len(partners):
            start(k + 1)

    ticks = {(START, 0): functools.partial(start, 0)}
    for k in range(len(partners)):
        ticks[STEP, k] = functools.partial(finish, k)
    return ticks


PAIR = 2 * HEAD_DIM


def dg(left, right, left_dim, right_dim):
    return lax.dot_general(
        left, right, (((left_dim,), (right_dim,)), ((), ())), preferred_element_type=F32
    )


def lane_ids(rows):
    return lax.broadcasted_iota(jnp.int32, (rows, PAIR), 1)


def head_lanes(h):
    lane = lane_ids(1)
    return jnp.where((lane >= h * HEAD_DIM) & (lane < (h + 1) * HEAD_DIM), 1.0, 0.0).astype(BF)


def spare_lanes(h):
    lane, first = lane_ids(1), (1 - h) * HEAD_DIM
    return jnp.where((lane >= first) & (lane < first + 3), 1.0, 0.0).astype(BF)


def with_constant(values, constant, h):
    high = constant.astype(BF).astype(F32)
    mid = (constant - high).astype(BF).astype(F32)
    low = constant - high - mid
    lane, first = lane_ids(values.shape[0]), (1 - h) * HEAD_DIM
    own = (lane >= h * HEAD_DIM) & (lane < (h + 1) * HEAD_DIM)
    out = jnp.where(own, values, 0.0)
    for k, term in enumerate((high, mid, low)):
        out = jnp.where(lane == first + k, term, out)
    return out.astype(BF)


def pair_lanes(p):
    return pl.ds(pl.multiple_of(p * PAIR, PAIR), PAIR)


def norm_rows(r, gain, shift):
    mean = jnp.mean(r, axis=-1, keepdims=True)
    centered = r - mean
    var = jnp.mean(centered * centered, axis=-1, keepdims=True)
    inv = lax.rsqrt(var + EPSILON)
    normed = centered * inv
    return normed * gain + shift, normed, inv


def norm_rows_back(grad, normed, inv, gain):
    dn = grad * gain
    out = inv * (
        dn
        - jnp.mean(dn, axis=-1, keepdims=True)
        - normed * jnp.mean(dn * normed, axis=-1, keepdims=True)
    )
    return out


def rowsum(values):
    return jnp.sum(values, axis=0, keepdims=True)


def by_rows(length, body, step=64):
    def go(k, carry):
        body(pl.ds(pl.multiple_of(k * step, step), step))
        return carry

    lax.fori_loop(0, length // step, go, 0)


def allowed_bias(bias, seg_row, seg_col):
    length = bias.shape[0]

    def body(span):
        shape = (span.size, length)
        query = lax.broadcasted_iota(jnp.int32, shape, 0) + span.start
        key = lax.broadcasted_iota(jnp.int32, shape, 1)
        ok = (key <= query) & (seg_col[span, 0:1] == seg_row[0:1, :].astype(F32))
        bias[span, :] = jnp.where(ok, 0.0, NEG_FILL)

    by_rows(length, body)


def attend_pair(p, q, k, v, q_aug, out, bias):
    lanes = pair_lanes(p)
    half = q.shape[0] // 2
    blocks = [(0, half, k.shape[0]), (half, half, k.shape[0])]
    if bias is not None:
        blocks = [(0, half, half), (half, half, 2 * half)]
    for first, rows, keys in blocks:
        span = pl.ds(first, rows)
        q_rows = q[span, lanes]
        k_rows, v_rows = k[pl.ds(0, keys), lanes], v[pl.ds(0, keys), lanes]
        outs = []
        for h in (0, 1):
            scores = dg(q_rows * head_lanes(h), k_rows, 1, 1)
            if bias is not None:
                scores = scores + bias[span, pl.ds(0, keys)]
            top = jnp.max(scores, axis=-1, keepdims=True)
            weight = jnp.exp(scores - top)
            total = jnp.sum(weight, axis=-1, keepdims=True)
            prob = (weight * (1.0 / total)).astype(BF)
            outs.append(dg(prob, v_rows, 1, 0))
            q_aug[2 * p + h, span, :] = with_constant(q_rows.astype(F32), -(top + jnp.log(total)), h)
        out[span, lanes] = jnp.where(lane_ids(rows) < HEAD_DIM, outs[0], outs[1]).astype(BF)


def whole(ref):
    return ref[...].reshape(-1, ref.shape[-1])


class Local:
    def __init__(self, sems):
        self.sems, self.count, self.open = sems, 0, []

    def copy(self, src, dst):
        move = pltpu.make_async_copy(src, dst, self.sems.at[self.count])
        self.count += 1
        move.start()
        return move

    def save(self, src, dst):
        self.open.append(self.copy(src, dst))

    def drain(self):
        for move in self.open:
            move.wait()


def attend_pair_back(p, q_aug, k, v, a, da, dq, dk, dv, bias):
    lanes = pair_lanes(p)
    length, keys_all = da.shape[0], k.shape[0]
    part = dk[0].shape[0]
    half = length // 2
    blocks = [(half, half, keys_all), (0, half, keys_all)]
    if bias is not None:
        keys_all = length
        blocks = [(half, half, length), (0, half, half)]
    sums = None
    for first, rows, keys in blocks:
        span = pl.ds(first, rows)
        k_rows, v_rows = k[pl.ds(0, keys), lanes], v[pl.ds(0, keys), lanes]
        grad = da[span, lanes]
        grad_wide = grad.astype(F32)
        prod = grad_wide * a[span, lanes].astype(F32)
        q0, q1 = q_aug[2 * p, span, :], q_aug[2 * p + 1, span, :]
        q_t = (q0 * head_lanes(0) + q1 * head_lanes(1)).T
        grad_t = grad.T
        dqs, dks, dvs = [], [], []
        for h, q_h in ((0, q0), (1, q1)):
            lane = lane_ids(rows)
            own = (lane >= h * HEAD_DIM) & (lane < (h + 1) * HEAD_DIM)
            dot = jnp.sum(jnp.where(own, prod, 0.0), axis=-1, keepdims=True)
            spare = spare_lanes(h)
            keep = 1 - spare
            scores = dg(q_h, k_rows * keep + spare, 1, 1)
            if bias is not None:
                scores = scores + bias[span, pl.ds(0, keys)]
            prob = jnp.exp(scores)
            d_prob = dg(with_constant(grad_wide, -dot, h), v_rows * keep + spare, 1, 1)
            d_score = (prob * d_prob).astype(BF)
            own_rows = slice(h * HEAD_DIM, (h + 1) * HEAD_DIM)
            dqs.append(dg(d_score, k_rows, 1, 0))
            dvs.append(dg(grad_t[own_rows], prob.astype(BF), 1, 0))
            dks.append(dg(q_t[own_rows], d_score, 1, 0))
        d_q = jnp.where(lane_ids(rows) < HEAD_DIM, dqs[0], dqs[1]).astype(BF)
        dq[span, lanes] = (d_q.astype(F32) * (1.0 / math.sqrt(HEAD_DIM))).astype(BF)
        new = [jnp.concatenate(parts, 0) for parts in (dks, dvs)]
        if sums is None:
            sums = new
        else:
            sums = [
                old + term if keys == keys_all else jnp.concatenate([old[:, :keys] + term, old[:, keys:]], 1)
                for old, term in zip(sums, new)
            ]
    for refs, value in zip((dk, dv), sums):
        low = value.astype(BF)
        for j in range(keys_all // part):
            refs[j][:, lanes] = low[:, j * part : (j + 1) * part].T


PLAN = {
    BEGIN: (
        (SEG, SEND, 0), (ATTN, FIRST, ROUTE_A), (ATTN, FIRST, ROUTE_B), (ATTN, NEAR, ROUTE_B, 0),
        (FFN, FIRST, ROUTE_B), (FFN, NEAR, ROUTE_B, 0), (X, SEND, 1), (ATTN, NEAR, ROUTE_B, 1),
        (ATTN, NEAR, ROUTE_A, 0), (ATTN, ALONG, ROUTE_B, 1, 0), (ATTN, ALONG, ROUTE_A, 1, 0),
        (ATTN, ALONG, ROUTE_B, 2, 0), (ATTN, ALONG, ROUTE_A, 2, 0), (FFN, FIRST, ROUTE_A),
        (ATTN, ALONG, ROUTE_B, 3, 0),
    ),
    COT: (
        (SEG, RECV, 0), (X, SEND, 0), (ATTN, NEAR, ROUTE_A, 1), (ATTN, ACROSS, ROUTE_B, 1, 0),
        (ATTN, ACROSS, ROUTE_B, 2, 0), (ATTN, ALONG, ROUTE_A, 1, 1), (ATTN, ALONG, ROUTE_A, 3, 0),
        (ATTN, ACROSS, ROUTE_B, 3, 0), (ATTN, ACROSS, ROUTE_A, 0, 0), (ATTN, ACROSS, ROUTE_B, 0, 0),
        (ATTN, ACROSS, ROUTE_A, 2, 0), (ATTN, ALONG, ROUTE_B, 1, 1), (ATTN, ACROSS, ROUTE_A, 1, 0),
    ),
    WEIGHTS: (
        (X, RECV, 1), (FFN, NEAR, ROUTE_A, 1), (ATTN, ALONG, ROUTE_B, 2, 1), (FFN, NEAR, ROUTE_A, 0),
        (FFN, ALONG, ROUTE_B, 1, 0), (ATTN, ALONG, ROUTE_A, 2, 1), (ATTN, ACROSS, ROUTE_A, 3, 0), (X, RECV, 0),
        (ATTN, CORE, ROUTE_A, 0, 0), (ATTN, CORE, ROUTE_B, 0, 0), (ATTN, CORE, ROUTE_B, 0, 1),
        (ATTN, ALONG, ROUTE_B, 3, 1), (ATTN, ACROSS, ROUTE_B, 0, 1), (ATTN, ACROSS, ROUTE_B, 1, 1),
        (ATTN, ACROSS, ROUTE_B, 2, 1), (ATTN, ACROSS, ROUTE_B, 3, 1), (ATTN, CORE, ROUTE_B, 1, 0),
    ),
    (SELF, 0): (
        (FFN, NEAR, ROUTE_B, 1),
    ),
    (SELF, 1): (
        (FFN, ALONG, ROUTE_A, 1, 1),
    ),
    (SELF, 2): (
        (ATTN, ACROSS, ROUTE_A, 1, 1), (ATTN, ALONG, ROUTE_A, 3, 1),
    ),
    (SELF, 3): (
        (FFN, ACROSS, ROUTE_B, 0, 1), (COT, SEND, 0),
    ),
    (SELF, 4): (
        (ATTN, ACROSS, ROUTE_A, 0, 1), (FFN, ALONG, ROUTE_B, 1, 1),
    ),
    (SELF, 5): (
        (FFN, ACROSS, ROUTE_B, 0, 0), (FFN, ALONG, ROUTE_A, 2, 1),
    ),
    NORM1: (
        (ATTN, ACROSS, ROUTE_A, 2, 1), (ATTN, ACROSS, ROUTE_A, 3, 1), (ATTN, CORE, ROUTE_A, 1, 1),
        (ATTN, CORE, ROUTE_B, 1, 1),
    ),
    KEYS: (
        (FFN, ALONG, ROUTE_A, 1, 0),
    ),
    VALUES: (
        (FFN, ALONG, ROUTE_B, 2, 1), (FFN, ALONG, ROUTE_B, 2, 0),
    ),
    (CROSS, 0): (
        (FFN, ALONG, ROUTE_A, 3, 1),
    ),
    (CROSS, 1): (
        (FFN, ACROSS, ROUTE_B, 2, 1), (FFN, ACROSS, ROUTE_A, 1, 1),
    ),
    (CROSS, 2): (
        (FFN, ALONG, ROUTE_A, 2, 0), (FFN, ALONG, ROUTE_B, 3, 1), (FFN, ACROSS, ROUTE_A, 2, 1),
        (FFN, ALONG, ROUTE_B, 3, 0),
    ),
    (CROSS, 3): (
        (FFN, ALONG, ROUTE_A, 3, 0),
    ),
    (CROSS, 4): (
        (FFN, ACROSS, ROUTE_B, 1, 1), (FFN, ACROSS, ROUTE_B, 3, 1), (FFN, ACROSS, ROUTE_B, 3, 0),
        (FFN, ACROSS, ROUTE_A, 1, 0), (COT, SEND, 1), (FFN, ACROSS, ROUTE_A, 3, 1), (FFN, ACROSS, ROUTE_A, 0, 1),
        (FFN, ACROSS, ROUTE_B, 2, 0),
    ),
    (CROSS, 5): (
        (FFN, ACROSS, ROUTE_B, 1, 0), (FFN, ACROSS, ROUTE_A, 2, 0),
    ),
    NORM2: (
        (FFN, ACROSS, ROUTE_A, 3, 0), (FFN, ACROSS, ROUTE_A, 0, 0),
    ),
    (FFN, 0): (
        (FFN, CORE, ROUTE_B, 1, 1), (FFN, CORE, ROUTE_B, 1, 0), (FFN, CORE, ROUTE_A, 1, 1),
        (FFN, CORE, ROUTE_B, 0, 0), (FFN, CORE, ROUTE_B, 0, 1), (FFN, CORE, ROUTE_A, 0, 0),
    ),
    FFN_DONE: (
        (COT, RECV, 1), (COT, RECV, 0),
    ),
    NORM3: (
        (LO, SEND, 0), (LO, SEND, 1),
    ),
    (DW2, 1): (
        (F1, CORES, 0),
    ),
    (DW2, 3): (
        (F1, CORES, 1),
    ),
    (DW1, 1): (
        (F1, CORES, 2),
    ),
    (DW1, 2): (
        (F1, CORES, 3),
    ),
    (DW1, 3): (
        (F0, CORES, 1),
    ),
    NORM2_BACK: (
        (F0, CORES, 3),
    ),
    (CROSS_BACK, 0): (
        (F0, CORES, 2), (F1, PLANES, 2), (F1, PLANES, 1), (F1, WAVE, 0, 1),
    ),
    (CROSS_BACK, 1): (
        (F1, WAVE, 0, 2), (CR, CORES, 3), (F1, PLANES, 3),
    ),
    (CROSS_BACK, 2): (
        (F0, PLANES, 1), (F0, PLANES, 2), (F0, WAVE, 0, 1), (F1, PLANES, 0), (F1, WAVE, 0, 0),
    ),
    (CROSS_BACK, 4): (
        (F1, WAVE, 1, 1), (F0, CORES, 0),
    ),
    DCQ: (
        (F1, WAVE, 1, 2),
    ),
    DCK: (
        (CR, CORES, 0), (F0, WAVE, 0, 2),
    ),
    DCV: (
        (CR, PLANES, 3),
    ),
    DWO: (
        (CR, PLANES, 0), (CR, WAVE, 0, 0), (CR, CORES, 2),
    ),
    (SELF_BACK, 0): (
        (F0, PLANES, 3),
    ),
    (SELF_BACK, 1): (
        (F1, WAVE, 1, 0),
    ),
    (SL, 0): (
        (CR, CORES, 1),
    ),
    (SL, 1): (
        (F0, PLANES, 0), (F0, WAVE, 0, 0), (F1, WAVE, 2, 1),
    ),
    (SL, 2): (
        (F0, WAVE, 1, 1),
    ),
    (SELF_BACK, 3): (
        (SL, CORES, 0),
    ),
    (SELF_BACK, 5): (
        (SL, CORES, 3),
    ),
    (SR, 0): (
        (CR, PLANES, 2), (CR, PLANES, 1), (CR, WAVE, 0, 2), (SR, CORES, 3), (SR, CORES, 0),
        (SL, CORES, 1),
    ),
    (SR, 2): (
        (CR, WAVE, 1, 0),
    ),
    VEC: (
        (SM, START, 0), (SL, CORES, 2),
    ),
    (DX, 0): (
        (IG, SEND, 0), (F0, WAVE, 1, 0), (SR, PLANES, 3), (SR, PLANES, 0), (SR, WAVE, 0, 0),
        (SL, PLANES, 0), (SL, PLANES, 3), (SL, WAVE, 0, 3),
    ),
    (DX, 1): (
        (IG, SEND, 1), (F1, WAVE, 2, 0), (SR, CORES, 1), (SL, WAVE, 0, 0),
    ),
    LOADS: (
        (CR, WAVE, 1, 2),
    ),
    (ENC, 1): (
        (F0, WAVE, 2, 1),
    ),
    (ENC, 3): (
        (SM, STEP, 0), (SR, WAVE, 1, 0), (SL, PLANES, 1), (SL, PLANES, 2), (SL, WAVE, 0, 1),
    ),
    END: (
        (LO, RECV, 1), (IG, RECV, 0), (CR, WAVE, 2, 0), (F0, WAVE, 1, 2), (CR, WAVE, 0, 1),
        (LO, RECV, 0), (F1, WAVE, 3, 0),
    ),
    END2: (
        (SL, WAVE, 0, 2),
    ),
    END3: (
        (SL, WAVE, 1, 0), (CR, WAVE, 0, 3), (F0, WAVE, 2, 0), (SR, CORES, 2), (SL, WAVE, 1, 1),
        (SR, PLANES, 1), (SR, PLANES, 2), (SR, WAVE, 0, 1), (F0, WAVE, 0, 3), (SR, WAVE, 2, 0),
        (SL, WAVE, 2, 1), (SR, WAVE, 0, 2), (SR, WAVE, 0, 3), (SL, WAVE, 2, 0), (SM, STEP, 1),
        (CR, WAVE, 1, 1), (IG, RECV, 1), (F0, WAVE, 3, 0), (F0, LAST, 1), (F0, LAST, 2),
        (F1, WAVE, 0, 3), (F1, LAST, 1), (F1, LAST, 2), (SR, WAVE, 1, 1), (CR, WAVE, 2, 1),
        (CR, WAVE, 3, 0), (SL, WAVE, 1, 2), (SL, WAVE, 3, 0), (SR, WAVE, 1, 2), (SR, WAVE, 2, 1),
        (SR, WAVE, 3, 0), (CR, LAST, 1), (SL, LAST, 1), (SR, LAST, 1), (SM, STEP, 2),
        (CR, LAST, 2), (SL, LAST, 2), (SR, LAST, 2), (SM, STEP, 3), (F1, LAST, 3),
        (F0, LAST, 3), (CR, LAST, 3), (SL, LAST, 3), (SR, LAST, 3), (SM, STEP, 4),
    ),
}


def transfer_plan(depth):
    assert depth == 4
    return PLAN


def once(loop_index, at, body):
    run_when(loop_index == at, body)


SUMS = {
    F1: (0, FFN_GRAD, 1, (0, 512, 256)),
    F0: (1, FFN_GRAD, 0, (0, 512, 256)),
    CR: (3, ATTN_GRAD, 1, (0, 512, 256)),
    SL: (2, ATTN_GRAD, 0, (0, 256, 128)),
    SR: (2, ATTN_GRAD, 0, (384, 256, 128)),
}


def mega_kernel(names, plan, *refs):
    r = types.SimpleNamespace(**dict(zip(names, refs)))
    net = Net(r.send_sems, r.recv_sems)
    s, z, y, c, depth = net.s, net.z, net.y, net.c, net.depth
    small, vec, attn_full, ffn_full = r.small, r.vec, r.attn_full, r.ffn_full
    local = Local(r.local_sems)
    scale = 1.0 / math.sqrt(HEAD_DIM)
    length, width = r.x.shape
    enc_length = r.enc.shape[0]
    pairs = width // PAIR
    partner_dev = net.at(s=1 - s)
    t, acc, bias = r.t, r.acc, r.t.at[:, pl.ds(0, length)]
    g, own, slots = r.g, r.own, r.slots

    ticks = {}
    for tag, full in ((ATTN, attn_full), (FFN, ffn_full)):
        ticks.update({(tag, *key): tick for key, tick in gather_ticks(net, full, tag).items()})
    for tag, (place, out, side, columns) in SUMS.items():
        extra = {name: getattr(r, name + tag) for name in reduce_extra(2, 1, 1)}
        room = (attn_full, ffn_full)[place // 2].at[place % 2]
        terms = (getattr(r, out), getattr(r, out + _MORE))
        steps = reduce_ticks(net, slots, own, room, extra, terms, side, tag, columns)
        ticks.update({(tag, *key): step for key, step in steps.items()})

    def exchange(name, src, dst, parts):
        rows = src.shape[0] // parts

        def send(k):
            span = pl.ds(k * rows, rows)
            net.send(src.at[span], dst.at[span], partner_dev, (name, k), lambda: dst.at[span], name)

        def recv(k):
            net.recv(dst.at[pl.ds(k * rows, rows)], (name, k))

        for k in range(parts):
            ticks[name, SEND, k] = functools.partial(send, k)
            ticks[name, RECV, k] = functools.partial(recv, k)

    exchange(SEG, r.seg_mine, r.seg, 1)
    exchange(X, r.x_own, r.x, 2)
    exchange(COT, g.at[0], r.cot, 2)
    exchange(LO, r.cot, r.lo_got, 2)
    exchange(IG, r.h1, r.ig_got, 2)
    ticks.update({(SM, *key): step for key, step in total_ticks(net, r.sums, r.sum_got, SM).items()})
    done = set()

    def at(point, p=None, turns=range(pairs)):
        if p is None:
            for key in plan.get(point, ()):
                assert key not in done, key
                done.add(key)
                ticks[key]()
            return
        for k in turns:
            if plan.get((point, k)):
                once(p, k, lambda k=k: at((point, k)))

    def signal_room(sem):
        for to in neighbours:
            pl.semaphore_signal(sem, inc=1, device_id=to, device_id_type=MESH_ID)
        run_when(net.low[1], lambda: pl.semaphore_signal(sem, inc=1, device_id=net.at(z=z - 1), device_id_type=MESH_ID))
        run_when(net.high[1], lambda: pl.semaphore_signal(sem, inc=1, device_id=net.at(z=z + 1), device_id_type=MESH_ID))

    def wait_room(sem):
        pl.semaphore_wait(sem, len(neighbours) + net.low[1].astype(jnp.int32) + net.high[1].astype(jnp.int32))

    neighbours = [net.at(s=1 - s), net.at(y=1 - y), net.at(c=1 - c)]

    r.seg_mine[...] = jnp.broadcast_to(r.seg_own[...], r.seg_mine.shape)
    attn_full[s, z, y, c] = r.attn_own[...].astype(BF)
    ffn_full[s, z, y, c] = r.ffn_own[...].astype(BF)
    net.greet([to for to in total_partners(net)[2:-1]])
    at(BEGIN)
    enc_load = local.copy(r.enc_own, r.enc)
    local.copy(r.cot_own, acc).wait()

    def low_cot(span):
        g[0, span, :] = acc[span, :].astype(BF)

    by_rows(length, low_cot)
    at(COT)
    r.seg_col[...] = r.seg[...].astype(F32).T
    allowed_bias(bias, r.seg, r.seg_col)
    at(WEIGHTS)

    def block(k):
        return whole(attn_full.at[k // depth, k % depth])

    def into_heads(dst, left, right, shift, factor):
        half = left.shape[0] // 2
        for k in (0, 1):
            span = pl.ds(k * half, half)
            value = dg(left[span, :], right, 1, 0)
            if shift is not None:
                value = value + shift
            if factor is not None:
                value = value * factor
            dst[span, :] = value.astype(BF)

    into_heads(r.q, r.x, block(0), small[0:1], scale)
    into_heads(r.k, r.x, block(1), None, None)
    into_heads(r.v, r.x, block(2), small[1:2], None)
    at("qkv")

    def self_body(p, carry):
        attend_pair(p, r.q, r.k, r.v, r.qa, r.a, bias)
        at(SELF, p)
        return carry

    lax.fori_loop(0, pairs, self_body, 0)
    t[...] = dg(r.a[...], block(3), 1, 0)

    def norm_one(span):
        res = r.x[span, :].astype(F32) + t[span, :] + small[2:3]
        hidden, normed, inv = norm_rows(res, small[7:8], small[8:9])
        acc[span, :] = hidden
        r.h1[span, :] = hidden.astype(BF)
        r.n1[span, :] = normed
        r.inv[span, :] = jnp.broadcast_to(inv, (span.size, PAIR))

    by_rows(length, norm_one)
    at(NORM1)
    weights_saved = local.copy(attn_full, r.attn_out)

    into_heads(r.q, r.h1, block(4), small[3:4], scale)
    enc_load.wait()
    into_heads(r.k2, r.enc, block(5), None, None)
    at(KEYS)
    into_heads(r.v2, r.enc, block(6), small[4:5], None)
    at(VALUES)

    def cross_body(p, carry):
        attend_pair(p, r.q, r.k2, r.v2, r.qb, r.a2, None)
        at(CROSS, p)
        return carry

    lax.fori_loop(0, pairs, cross_body, 0)
    t[...] = dg(r.a2[...], block(7), 1, 0)

    def norm_two(span):
        res = acc[span, :] + t[span, :] + small[5:6]
        hidden, normed, inv = norm_rows(res, small[9:10], small[10:11])
        acc[span, :] = hidden
        r.h2[span, :] = hidden.astype(BF)
        r.n2[span, :] = normed
        r.inv[span, :] = jnp.where(lane_ids(span.size) < HEAD_DIM, r.inv[span, :], inv)

    by_rows(length, norm_two)
    at(NORM2)

    vec[...] = jnp.zeros_like(vec)
    root = math.sqrt(0.5)
    weights_saved.wait()
    net.drain_one(COT)
    for k in range(depth):
        at((FFN, k))
        t[...] = dg(r.h2[...], whole(ffn_full.at[0, k]), 1, 1)

        def gelu(span, k=k):
            u = t[span, :] + small[13 + k : 14 + k]
            below = 0.5 + 0.5 * lax.erf(u * root)
            g[k, span, :] = (u * below).astype(BF)
            r.gp[pl.ds(span.start + k * length, span.size), :] = (below + u * (jnp.exp(-0.5 * u * u) * (1.0 / math.sqrt(2.0 * math.pi)))).astype(BF)

        by_rows(length, gelu)
        acc[...] += dg(g[k], whole(ffn_full.at[1, k]), 1, 0)
    net.drain()
    signal_room(r.room_a)
    at(FFN_DONE)

    def norm_three(span):
        hidden, normed, inv = norm_rows(acc[span, :] + small[6:7], small[11:12], small[12:13])
        cot = r.cot[span, :].astype(F32)
        r.cot[span, :] = hidden.astype(BF)
        dr3 = norm_rows_back(cot, normed, inv, small[11:12])
        vec[11:12] += rowsum(cot * normed)
        vec[12:13] += rowsum(cot)
        acc[span, :] = dr3
        low = dr3.astype(BF)
        r.dy[span, :] = low
        vec[6:7] += rowsum(low.astype(F32))

    by_rows(length, norm_three)
    at(NORM3)

    used = [0]

    def put(left, right, tags, z1, first=0):
        cols = pl.ds(first, right.shape[-1])
        slot = used[0] % slots.shape[0]
        used[0] += 1
        if used[0] > slots.shape[0]:
            net.drain_one((SLOT, slot))
        slots[slot, :, :, :, cols] = dg(left, right, 0, 0).astype(BF).reshape(*slots.shape[1:4], -1)
        for y1 in (0, 1):
            own[z1, y1, :, cols] = slots[slot, y1, c, :, cols]
        for tag in tags:
            ticks[tag, START, z1](slot)

    wait_room(r.room_a)
    for k in range(depth):
        put(g[k], r.dy[...], (F1,), k)
        at((DW2, k))
        t[...] = dg(r.dy[...], whole(ffn_full.at[1, k]), 1, 1)

        def through(span, k=k):
            du = (t[span, :] * r.gp[pl.ds(span.start + k * length, span.size), :].astype(F32)).astype(BF)
            g[k, span, :] = du
            vec[13 + k : 14 + k] += rowsum(du.astype(F32))

        by_rows(length, through)
        at(("du", k))
    for k in range(depth):
        acc[...] += dg(g[k], whole(ffn_full.at[0, k]), 1, 0)
        at(("dh", k))
        put(g[k], r.h2[...], (F0,), k)
        at((DW1, k))
    signal_room(r.room_f)

    loads = {}

    def load_weight(k, slot):
        block_rows = attn_full.shape[-2]
        loads[k] = [
            local.copy(
                r.attn_out.at[k // depth, k % depth, j // 2, j % 2],
                r.gp.at[pl.ds(slot * width + j * block_rows, block_rows)],
            )
            for j in range(4)
        ]

    def weight(k, slot):
        for move in loads[k]:
            move.wait()
        return r.gp[pl.ds(slot * width, width), :]

    load_weight(7, 0)
    do, da, dq = r.dy, r.h2, r.q
    dk, dv = [g.at[0], g.at[1]], [g.at[2], g.at[3]]

    def norm_two_back(span):
        grad, normed = acc[span, :], r.n2[span, :]
        vec[9:10] += rowsum(grad * normed)
        vec[10:11] += rowsum(grad)
        grad = norm_rows_back(grad, normed, r.inv[span, HEAD_DIM : HEAD_DIM + 1], small[9:10])
        acc[span, :] = grad
        low = grad.astype(BF)
        do[span, :] = low
        vec[5:6] += rowsum(low.astype(F32))

    by_rows(length, norm_two_back)
    at(NORM2_BACK)

    def low_dot(dst, left, right):
        half = left.shape[0] // 2
        for k in (0, 1):
            span = pl.ds(k * half, half)
            dst[span, :] = dg(left[span, :], right, 1, 1).astype(BF)

    low_dot(da, do, weight(7, 0))
    load_weight(4, 0)
    wait_room(r.room_f)
    put(r.a2[...], do[...], (CR,), 3)
    at("dco")

    def cross_back(p, carry):
        attend_pair_back(p, r.qb, r.k2, r.v2, r.a2, da, dq, dk, dv, None)
        at(CROSS_BACK, p)
        return carry

    lax.fori_loop(0, pairs, cross_back, 0)
    put(r.h1[...], dq[...], (CR,), 0)
    at(DCQ)
    acc[...] += dg(dq[...], weight(4, 0), 1, 1)
    put(r.enc[...], g[0:2].reshape(enc_length, width), (CR,), 1)
    at(DCK)
    put(r.enc[...], g[2:4].reshape(enc_length, width), (CR,), 2)
    at(DCV)

    def colsum_into(row, ref):
        def body(span):
            vec[row : row + 1] += rowsum(ref[span, :].astype(F32))

        by_rows(ref.shape[0], body)

    colsum_into(3, dq)
    colsum_into(4, dv[0])
    colsum_into(4, dv[1])
    load_weight(3, 0)

    def norm_one_back(span):
        grad, normed = acc[span, :], r.n1[span, :]
        vec[7:8] += rowsum(grad * normed)
        vec[8:9] += rowsum(grad)
        grad = norm_rows_back(grad, normed, r.inv[span, 0:1], small[7:8])
        acc[span, :] = grad
        low = grad.astype(BF)
        do[span, :] = low
        vec[2:3] += rowsum(low.astype(F32))

    by_rows(length, norm_one_back)
    load_weight(0, 1)
    load_weight(1, 2)

    low_dot(da, do, weight(3, 0))
    load_weight(2, 0)
    put(r.a[...], do[...], (SL, SR), 3)
    at(DWO)
    allowed_bias(bias, r.seg, r.seg_col)
    ek, ev = r.k2.at[pl.ds(0, length)], r.v2.at[pl.ds(0, length)]
    edge = SUMS[SR][3][0]
    turns = edge // PAIR

    def self_back(some, p, carry):
        attend_pair_back(p, r.qa, r.k, r.v, r.a, da, dq, [ek], [ev], bias)
        at(SELF_BACK, p, some)
        return carry

    for tag, first, some in ((SL, 0, range(turns)), (SR, edge, range(turns, pairs))):
        lax.fori_loop(some.start, some.stop, functools.partial(self_back, some), 0)
        cols = pl.ds(first, len(some) * PAIR)
        for z1, ref in ((0, dq), (1, ek), (2, ev)):
            put(r.x[...], ref[:, cols], (tag,), z1, first)
            at((tag, z1))
    colsum_into(0, dq)
    colsum_into(1, ev)
    r.sums[0] = vec[...]
    at(VEC)
    from_q, from_k, from_v = weight(0, 1), weight(1, 2), weight(2, 0)
    half = length // 2
    for k in (0, 1):
        span = pl.ds(k * half, half)
        grad = acc[span, :] + dg(dq[span, :], from_q, 1, 1)
        grad = grad + dg(ek[span, :], from_k, 1, 1) + dg(ev[span, :], from_v, 1, 1)
        r.h1[span, :] = grad.astype(BF)
        at((DX, k))
    load_weight(5, 1)
    load_weight(6, 2)
    at(LOADS)
    from_keys, from_values = weight(5, 1), weight(6, 2)
    moves = [None, None]
    for k in range(4):
        span, rows = pl.ds((k % 2) * half, half), pl.ds((k % 2) * half, half)
        if moves[k % 2] is not None:
            moves[k % 2].wait()
        t[span, :] = dg(dk[k // 2][rows, :], from_keys, 1, 1) + dg(dv[k // 2][rows, :], from_values, 1, 1)
        moves[k % 2] = local.copy(t.at[span], r.enc_grad.at[pl.ds(k * half, half)])
        at((ENC, k))
    for move in moves:
        move.wait()
    at(END)

    at(END2)
    at(END3)
    r.small_grad[...] = r.sums[r.sums.shape[0] - 1]
    local.drain()
    net.drain()
    missing = [key for key in ticks if key not in done and key[1] != START]
    assert not missing, missing


def mega_call(x, enc, seg, cot, attn_own, ffn_own, small):
    rows, width = attn_own.shape
    depth = lax.axis_size(DP) // 4
    devices = lax.axis_size(DP) * 2
    length, enc_length = x.shape[0], enc.shape[0]
    heads = width // HEAD_DIM
    steps = net_bits(devices)
    act, enc_act, wide = ((length, width), BF), ((enc_length, width), BF), ((length, width), F32)
    aug, stack, col = ((heads, length, PAIR), BF), ((2, depth, 2, 2, rows, width), BF), ((length, PAIR), F32)
    many = ((depth, length, width), BF)
    vec = ((-(-small.shape[0] // 8) * 8, width), F32)
    own_rows = ((rows, width), BF)
    outs = dict(lo_got=act, ig_got=act, enc_grad=((enc_length, width), F32), attn_grad=own_rows, ffn_grad=own_rows, attn_grad_more=own_rows, ffn_grad_more=own_rows, small_grad=vec, attn_out=stack)
    inner = dict(
        attn_full=stack, ffn_full=stack, x=act, cot=act, enc=enc_act, seg=((8, length), jnp.int32), seg_mine=((8, length), jnp.int32), seg_col=((length, 8), F32),
        qa=aug, qb=aug, q=act, k=act, v=act, a=act, h1=act, k2=enc_act, v2=enc_act, a2=act, n1=wide, inv=col, acc=wide, t=wide,
        h2=act, n2=wide, g=many, gp=((max(depth * length, 3 * width), width), BF), dy=act, vec=vec,
        slots=((2, 2, 2, rows, width), BF), own=((depth, 2, rows, width), BF),
        sums=((steps + 1, *vec[0]), F32), sum_got=((steps, *vec[0]), F32),
    )
    for tag, (_, _, _, columns) in SUMS.items():
        inner.update({name + tag: (shape, BF) for name, shape in reduce_extra(rows, *columns[1:]).items()})
    inside, anywhere = pl.BlockSpec(memory_space=pltpu.VMEM), pl.BlockSpec(memory_space=pl.ANY)
    args = dict(x_own=x, enc_own=enc, seg_own=seg, cot_own=cot, attn_own=attn_own, ffn_own=ffn_own, small=small)
    names = (*args, *outs, *inner, "send_sems", "recv_sems", "local_sems", "room_a", "room_f")
    got = pl.pallas_call(
        functools.partial(mega_kernel, names, transfer_plan(depth)),
        out_shape=tuple(jax.ShapeDtypeStruct(*outs[name]) for name in outs),
        in_specs=[anywhere if name in ("x_own", "enc_own", "cot_own") else inside for name in args],
        out_specs=tuple(inside if "_grad" in name and name != ENC_GRAD else anywhere for name in outs),
        scratch_shapes=[
            *[pltpu.VMEM(*inner[name]) for name in inner],
            pltpu.SemaphoreType.DMA((440,)),
            pltpu.SemaphoreType.DMA((440,)),
            pltpu.SemaphoreType.DMA((64,)),
            pltpu.SemaphoreType.REGULAR,
            pltpu.SemaphoreType.REGULAR,
        ],
        compiler_params=pltpu.CompilerParams(collective_id=0, has_side_effects=True, vmem_limit_bytes=255 << 18),
        name="layer",
    )(*args.values())
    return dict(zip(outs, got))


def partner(value, axis, apart):
    mask = 2**apart
    pairs = [(source, source ^ mask) for source in range(lax.axis_size(axis))]
    return lax.ppermute(value, axis, pairs)


def matmul(left_op, right_op):
    return jnp.dot(left_op, right_op, preferred_element_type=jnp.float32)


def contract_rows(left_op, right_op):
    return lax.dot_general(
        left_op, right_op, (((0,), (0,)), ((), ())), preferred_element_type=jnp.float32
    )


def contract_cols(left_op, right_op):
    return lax.dot_general(
        left_op, right_op, (((1,), (1,)), ((), ())), preferred_element_type=jnp.float32
    )


def gelu_exact(pre_value):
    return jax.nn.gelu(pre_value, approximate=False)


def split_heads(matrix):
    return matrix.reshape(matrix.shape[0], HEADS, HEAD_DIM)


def merge_heads(tensor):
    return tensor.reshape(tensor.shape[0], HEADS * HEAD_DIM)


def column_sum(grad_low):
    return jnp.sum(grad_low.astype(jnp.float32), axis=0)


def norm_forward(residual, norm_gain, norm_shift):
    row_mean = jnp.mean(residual, axis=-1, keepdims=True)
    centered = residual - row_mean
    row_var = jnp.mean(centered * centered, axis=-1, keepdims=True)
    inv_std = lax.rsqrt(row_var + EPSILON)
    normed = centered * inv_std
    return (normed * norm_gain + norm_shift, normed, inv_std)


def norm_backward(grad_out, normed, inv_std, norm_gain):
    grad_norm = grad_out * norm_gain
    centered_grad = grad_norm - jnp.mean(grad_norm, axis=-1, keepdims=True)
    grad_res = inv_std * (
        centered_grad - normed * jnp.mean(grad_norm * normed, axis=-1, keepdims=True)
    )
    return (grad_res, jnp.sum(grad_out * normed, axis=0), jnp.sum(grad_out, axis=0))


def block_scores(q_block, keys_in, seg_row, first_row):
    scores = jnp.einsum(QHD_KHD_HQK, q_block, keys_in, preferred_element_type=jnp.float32)
    if seg_row is None:
        return scores
    block_len = q_block.shape[0]
    query_pos = first_row + jnp.arange(block_len)
    key_pos = jnp.arange(seg_row.shape[0])
    allowed = (key_pos[None, :] <= query_pos[:, None]) & (seg_row[:, None] == seg_row[None, :])
    return jnp.where(allowed[None], scores, NEG_FILL)


def attend_forward(queries, keys_in, values_in, seg_row):
    scores = block_scores(queries, keys_in, seg_row, 0)
    row_max = jnp.max(scores, axis=-1, keepdims=True)
    exp_scores = jnp.exp(scores - row_max)
    totals = jnp.sum(exp_scores, axis=-1, keepdims=True)
    attn_prob = (exp_scores / totals).astype(jnp.bfloat16)
    outputs = jnp.einsum(HQK_KHD_QHD, attn_prob, values_in, preferred_element_type=jnp.float32)
    lse_list = [row_max + jnp.log(totals)]
    return (outputs, lse_list)


def attend_backward(queries, keys_in, values_in, seg_row, lse_list, grad_mixed):
    query_len = queries.shape[0]
    block_len = min(512, query_len)
    grad_queries = []
    grad_keys = jnp.zeros(keys_in.shape, jnp.float32)
    grad_values = jnp.zeros(values_in.shape, jnp.float32)
    for block_index, first_row in enumerate(range(0, query_len, block_len)):
        scores = block_scores(queries, keys_in, seg_row, first_row)
        attn_prob = jnp.exp(scores - lse_list[block_index])
        grad_values = jnp.einsum(
            HQK_QHD_KHD,
            attn_prob.astype(jnp.bfloat16),
            grad_mixed,
            preferred_element_type=jnp.float32,
        )
        grad_prob = jnp.einsum(
            QHD_KHD_HQK, grad_mixed, values_in, preferred_element_type=jnp.float32
        )
        grad_scores = attn_prob * (
            grad_prob - jnp.sum(grad_prob * attn_prob, axis=-1, keepdims=True)
        )
        grad_low = grad_scores.astype(jnp.bfloat16)
        grad_queries.append(
            jnp.einsum(HQK_KHD_QHD, grad_low, keys_in, preferred_element_type=jnp.float32)
        )
        grad_keys = jnp.einsum(
            HQK_QHD_KHD, grad_low, queries, preferred_element_type=jnp.float32
        )
    grad_q_all = grad_queries[0].astype(jnp.bfloat16)
    return (grad_q_all, grad_keys.astype(jnp.bfloat16), grad_values.astype(jnp.bfloat16))


def layer_row(dec_row, enc_row, seg_row, cot_row, blocks, w_in, w_out, vectors):
    w_query, w_key, w_value, w_proj, c_query, c_key, c_value, c_proj = blocks
    scale = 1.0 / math.sqrt(HEAD_DIM)
    bias_in = vectors[13:].reshape(-1)
    dec_full = dec_row.astype(jnp.float32)
    queries = ((matmul(dec_row, w_query) + vectors[0]) * scale).astype(jnp.bfloat16)
    keys_self = matmul(dec_row, w_key).astype(jnp.bfloat16)
    vals_self = (matmul(dec_row, w_value) + vectors[1]).astype(jnp.bfloat16)
    mixed_self, lse_self = attend_forward(
        split_heads(queries), split_heads(keys_self), split_heads(vals_self), seg_row
    )
    self_flat = merge_heads(mixed_self).astype(jnp.bfloat16)
    self_out = matmul(self_flat, w_proj) + vectors[2]
    hidden_one, normed_one, inv_one = norm_forward(dec_full + self_out, vectors[7], vectors[8])
    hidden_one_low = hidden_one.astype(jnp.bfloat16)
    cross_q = ((matmul(hidden_one_low, c_query) + vectors[3]) * scale).astype(jnp.bfloat16)
    cross_k = matmul(enc_row, c_key).astype(jnp.bfloat16)
    cross_v = (matmul(enc_row, c_value) + vectors[4]).astype(jnp.bfloat16)
    mixed_cross, lse_cross = attend_forward(
        split_heads(cross_q), split_heads(cross_k), split_heads(cross_v), None
    )
    cross_flat = merge_heads(mixed_cross).astype(jnp.bfloat16)
    cross_out = matmul(cross_flat, c_proj) + vectors[5]
    hidden_two, normed_two, inv_two = norm_forward(hidden_one + cross_out, vectors[9], vectors[10])
    hidden_two_low = hidden_two.astype(jnp.bfloat16)
    pre_act = contract_cols(hidden_two_low, w_in) + bias_in
    act_full, act_pull = jax.vjp(gelu_exact, pre_act)
    act_low = act_full.astype(jnp.bfloat16)
    ffn_out = matmul(act_low, w_out) + vectors[6]
    result, normed_three, inv_three = norm_forward(hidden_two + ffn_out, vectors[11], vectors[12])
    grad_r3, grad_g3, grad_e3 = norm_backward(cot_row, normed_three, inv_three, vectors[11])
    grad_y = grad_r3.astype(jnp.bfloat16)
    grad_w_out = contract_rows(act_low, grad_y)
    grad_act = contract_cols(grad_y, w_out)
    grad_pre = act_pull(grad_act)[0].astype(jnp.bfloat16)
    grad_w_in = contract_rows(grad_pre, hidden_two_low)
    grad_h2 = grad_r3 + matmul(grad_pre, w_in)
    grad_r2, grad_g2, grad_e2 = norm_backward(grad_h2, normed_two, inv_two, vectors[9])
    grad_co = grad_r2.astype(jnp.bfloat16)
    grad_c_proj = contract_rows(cross_flat, grad_co)
    grad_mix_c = contract_cols(grad_co, c_proj).astype(jnp.bfloat16)
    grad_q_c, grad_k_c, grad_v_c = attend_backward(
        split_heads(cross_q),
        split_heads(cross_k),
        split_heads(cross_v),
        None,
        lse_cross,
        split_heads(grad_mix_c),
    )
    grad_cq = merge_heads(grad_q_c) * scale
    grad_ck = merge_heads(grad_k_c)
    grad_cv = merge_heads(grad_v_c)
    grad_c_query = contract_rows(hidden_one_low, grad_cq)
    grad_h1 = grad_r2 + contract_cols(grad_cq, c_query)
    grad_r1, grad_g1, grad_e1 = norm_backward(grad_h1, normed_one, inv_one, vectors[7])
    grad_so = grad_r1.astype(jnp.bfloat16)
    grad_w_proj = contract_rows(self_flat, grad_so)
    grad_mix_s = contract_cols(grad_so, w_proj).astype(jnp.bfloat16)
    grad_q_s, grad_k_s, grad_v_s = attend_backward(
        split_heads(queries),
        split_heads(keys_self),
        split_heads(vals_self),
        seg_row,
        lse_self,
        split_heads(grad_mix_s),
    )
    grad_sq = merge_heads(grad_q_s) * scale
    grad_sk = merge_heads(grad_k_s)
    grad_sv = merge_heads(grad_v_s)
    grad_w_query = contract_rows(dec_row, grad_sq)
    grad_w_key = contract_rows(dec_row, grad_sk)
    grad_w_value = contract_rows(dec_row, grad_sv)
    grad_input = (
        grad_r1
        + contract_cols(grad_sq, w_query)
        + contract_cols(grad_sk, w_key)
        + contract_cols(grad_sv, w_value)
    )
    vec_rows = jnp.stack(
        [
            column_sum(grad_sq),
            column_sum(grad_sv),
            column_sum(grad_so),
            column_sum(grad_cq),
            column_sum(grad_cv),
            column_sum(grad_co),
            column_sum(grad_y),
            grad_g1,
            grad_e1,
            grad_g2,
            grad_e2,
            grad_g3,
            grad_e3,
        ]
    )
    vec_grad = jnp.concatenate([vec_rows, column_sum(grad_pre).reshape(-1, vectors.shape[1])], 0)
    row_mats = (grad_w_query, grad_w_key, grad_w_value, grad_w_proj, grad_c_query, grad_c_proj)
    return (result, grad_input, grad_ck, grad_cv, row_mats, grad_w_in, grad_w_out, vec_grad)


def nesterov(master, moment, average, grad, rate):
    new_moment = MOMENTUM * moment + grad
    new_master = master - rate * (grad + MOMENTUM * new_moment)
    new_average = AVG_DECAY * average + (1.0 - AVG_DECAY) * new_master
    return (new_master, new_moment, new_average)


def local(
    decoder_in,
    encoder_out,
    segment_ids,
    cotangent,
    attn_master,
    ffn_master,
    small_master,
    attn_moment,
    ffn_moment,
    small_moment,
    attn_average,
    ffn_average,
    small_average,
    rate_matrix,
    rate_vector,
):
    if (
        lax.axis_size(DP) == 16
        and attn_master.shape[0] % 32 == 0
        and decoder_in.shape[0] == 1
        and encoder_out.shape[1] == 2 * decoder_in.shape[1]
    ):
        got = mega_call(
            decoder_in[0], encoder_out[0], segment_ids, cotangent[0], attn_master, ffn_master, small_master
        )
        layer_out, input_grad = (got[name][None].astype(F32) for name in ("lo_got", "ig_got"))
        encoder_grad = got[ENC_GRAD][None]
        attn_grad, ffn_grad = (
            got[name].astype(F32) + got[name + _MORE].astype(F32) for name in (ATTN_GRAD, FFN_GRAD)
        )
        small_grad = got["small_grad"][: small_master.shape[0]]
    else:
        matrices, ffn_all = (
            lax.all_gather(attn_master.astype(jnp.bfloat16), (SIDE, DP), axis=0, tiled=True),
            lax.all_gather(ffn_master.astype(jnp.bfloat16), (SIDE, DP), axis=0, tiled=True),
        )
        model_width = matrices.shape[1]
        hidden_units = ffn_all.shape[0] // 2
        blocks = [
            matrices[block_index * model_width : (block_index + 1) * model_width]
            for block_index in range(8)
        ]
        w_in = ffn_all[:hidden_units]
        w_out = ffn_all[hidden_units:]
        partner_enc = partner(encoder_out, SIDE, 0)
        mat_grads = [jnp.zeros((model_width, model_width), jnp.float32) for block_index in range(8)]
        slots = (0, 1, 2, 3, 4, 7)
        row_index = 0
        outcome = layer_row(
            decoder_in[row_index],
            partner_enc[row_index],
            segment_ids[row_index],
            cotangent[row_index],
            blocks,
            w_in,
            w_out,
            small_master,
        )
        result, grad_input, grad_ck, grad_cv, row_mats, grad_w_in, grad_w_out, vec_grad = outcome
        layer_out = result[None]
        input_grad = grad_input[None]
        key_grads = [grad_ck]
        value_grads = [grad_cv]
        for slot_index, slot_grad in zip(slots, row_mats):
            mat_grads[slot_index] = slot_grad
        returned = partner(jnp.stack([jnp.stack(key_grads), jnp.stack(value_grads)]), SIDE, 0)
        row_index = 0
        own_rows = encoder_out[row_index]
        mat_grads[5] = contract_rows(own_rows, returned[0, row_index])
        mat_grads[6] = contract_rows(own_rows, returned[1, row_index])
        enc_grads = [
            contract_cols(returned[0, row_index], blocks[5])
            + contract_cols(returned[1, row_index], blocks[6])
        ]
        encoder_grad = jnp.stack(enc_grads)
        attn_total = jnp.concatenate(mat_grads, 0)
        ffn_total = jnp.concatenate([grad_w_in, grad_w_out], 0)
        attn_grad, ffn_grad = (
            lax.psum_scatter(attn_total, (SIDE, DP), scatter_dimension=0, tiled=True),
            lax.psum_scatter(ffn_total, (SIDE, DP), scatter_dimension=0, tiled=True),
        )
        small_grad = lax.psum(vec_grad, (SIDE, DP))
    attn_new, attn_moment_new, attn_average_new = nesterov(
        attn_master, attn_moment, attn_average, attn_grad, rate_matrix
    )
    ffn_new, ffn_moment_new, ffn_average_new = nesterov(
        ffn_master, ffn_moment, ffn_average, ffn_grad, rate_matrix
    )
    small_new, small_moment_new, small_average_new = nesterov(
        small_master, small_moment, small_average, small_grad, rate_vector
    )
    return (
        layer_out,
        input_grad,
        encoder_grad,
        attn_grad,
        ffn_grad,
        small_grad,
        attn_new,
        ffn_new,
        small_new,
        attn_moment_new,
        ffn_moment_new,
        small_moment_new,
        attn_average_new,
        ffn_average_new,
        small_average_new,
    )


def solution(mesh):
    placed = (
        P((SIDE, DP), None, None),
        P((SIDE, DP), None, None),
        P((SIDE, DP), None),
        P((SIDE, DP), None, None),
        P((SIDE, DP), None),
        P((SIDE, DP), None),
        P(),
        P((SIDE, DP), None),
        P((SIDE, DP), None),
        P(),
        P((SIDE, DP), None),
        P((SIDE, DP), None),
        P(),
        P(),
        P(),
    )
    return jax.shard_map(
        local,
        mesh=mesh,
        in_specs=placed,
        out_specs=(
            P((SIDE, DP), None, None),
            P((SIDE, DP), None, None),
            P((SIDE, DP), None, None),
            P((SIDE, DP), None),
            P((SIDE, DP), None),
            P(),
            P((SIDE, DP), None),
            P((SIDE, DP), None),
            P(),
            P((SIDE, DP), None),
            P((SIDE, DP), None),
            P(),
            P((SIDE, DP), None),
            P((SIDE, DP), None),
            P(),
        ),
        check_vma=False,
    )
```

```python
import functools
import math
import types

import jax
import jax.numpy as jnp
from jax import lax
from jax.experimental import pallas as pl
from jax.experimental.pallas import tpu as pltpu
from jax.sharding import PartitionSpec as P

HEADS = 12
HEAD_DIM = 64


NEG_FILL = -1e30
EPSILON = 1e-05
MOMENTUM = 0.5
AVG_DECAY = 0.5


SIDE = "side"
DP = "dp"
ROUTE_A = "A"
ROUTE_B = "B"
UP = "up"
DOWN = "down"
L = "l"
CORE = "core"
F = "f"
FIRST = "first"
NEAR = "near"
ALONG = "along"
ACROSS = "across"
XA = "xa"
EA = "ea"
EB = "eb"
YB = "yb"
XC = "xc"
C = "c"
SLOT = "slot"
YA = "ya"
XB = "xb"
ZA = "za"
ZB = "zb"
START = "start"
CORES = "cores"
PLANES = "planes"
WAVE = "wave"
LAST = "last"
STEP = "step"
BEGIN = "begin"
SEG = "seg"
SEND = "send"
ATTN = "attn"
FFN = "ffn"
X = "x"
COT = "cot"
RECV = "recv"
WEIGHTS = "weights"
SELF = "self"
NORM1 = "norm1"
KEYS = "keys"
VALUES = "values"
CROSS = "cross"
NORM2 = "norm2"
FFN_DONE = "ffn_done"
NORM3 = "norm3"
LO = "lo"
DW2 = "dw2"
F1 = "f1"
DW1 = "dw1"
F0 = "f0"
NORM2_BACK = "norm2_back"
CROSS_BACK = "cross_back"
CR = "cr"
DCQ = "dcq"
DCK = "dck"
DCV = "dcv"
DWO = "dwo"
SELF_BACK = "self_back"
SL = "sl"
SR = "sr"
VEC = "vec"
SM = "sm"
DX = "dx"
IG = "ig"
LOADS = "loads"
ENC = "enc"
END = "end"
END2 = "end2"
END3 = "end3"
FFN_GRAD = "ffn_grad"
ATTN_GRAD = "attn_grad"
_MORE = "_more"
ENC_GRAD = "enc_grad"
QHD_KHD_HQK = "qhd,khd->hqk"
HQK_KHD_QHD = "hqk,khd->qhd"
HQK_QHD_KHD = "hqk,qhd->khd"

MESH_ID = pl.DeviceIdType.MESH
BF = jnp.bfloat16
F32 = jnp.float32
CUT = 128


def run_when(cond, body):
    @pl.when(cond)
    def _():
        body()


class Net:
    def __init__(self, send_sems, recv_sems):
        self.s = lax.axis_index(SIDE)
        self.d = lax.axis_index(DP)
        self.z, self.y, self.c = self.d // 4, (self.d // 2) % 2, self.d % 2
        self.depth = lax.axis_size(DP) // 4
        self.send_sems, self.recv_sems = send_sems, recv_sems
        self.sent, self.slots, self.conds = [], {}, []
        self.low = [self.z >= k for k in range(self.depth)]
        self.high = [self.z < self.depth - k for k in range(self.depth)]
        self.here = [self.z == k for k in range(self.depth)]
        self.away = [self.s != k for k in (0, 1)]
        self.away_y = [self.y != k for k in (0, 1)]
        self.home = [self.s == k for k in (0, 1)]

    def at(self, s=None, z=None, y=None, c=None):
        s, z, y, c = (own if got is None else got for got, own in ((s, self.s), (z, self.z), (y, self.y), (c, self.c)))
        return (s, (z * 2 + y) * 2 + c)

    def slot(self, key):
        return self.slots.setdefault(key, len(self.slots))

    def copy(self, src, dst, to, send_slot, recv_slot):
        return pltpu.make_async_remote_copy(
            src_ref=src,
            dst_ref=dst,
            send_sem=self.send_sems.at[send_slot],
            recv_sem=self.recv_sems.at[recv_slot],
            device_id=to,
            device_id_type=MESH_ID,
        )

    def send(self, src, dst, to, key, like, group=None):
        send_slot, recv_slot = len(self.sent), self.slot(key)
        self.copy(src, dst, to, send_slot, recv_slot).start()
        peer = (self.s, self.d)
        wait = lambda: self.copy(like(), like(), peer, send_slot, recv_slot).wait_send()
        self.sent.append((wait, tuple(self.conds), group))

    def recv(self, dst, key):
        self.copy(dst, dst, self.at(c=1 - self.c), 0, self.slot(key)).wait_recv()

    def when(self, cond, body):
        self.conds.append(cond)
        run_when(cond, body)
        self.conds.pop()

    def drain(self):
        assert max(len(self.sent), len(self.slots)) <= min(self.send_sems.shape[0], self.recv_sems.shape[0])
        for k, entry in enumerate(self.sent):
            if entry is not None:
                wait, conds, _ = entry
                for cond in conds:
                    wait = functools.partial(run_when, cond, wait)
                wait()
                self.sent[k] = None

    def drain_one(self, group):
        for k, entry in enumerate(self.sent):
            if entry is not None and entry[2] == group:
                entry[0]()
                self.sent[k] = None

    def greet(self, others=()):
        barrier = pltpu.get_barrier_semaphore()
        partners = [self.at(s=1 - self.s), self.at(y=1 - self.y), self.at(c=1 - self.c), *others]
        for to in partners:
            pl.semaphore_signal(barrier, inc=1, device_id=to, device_id_type=MESH_ID)
        low, high = self.low[1], self.high[1]

        def signal(to):
            pl.semaphore_signal(barrier, inc=1, device_id=to, device_id_type=MESH_ID)

        pl.when(low)(lambda: signal(self.at(z=self.z - 1)))
        pl.when(high)(lambda: signal(self.at(z=self.z + 1)))
        pl.semaphore_wait(barrier, len(partners) + low.astype(jnp.int32) + high.astype(jnp.int32))


def gather_ticks(net, full, tag):
    depth, rows = net.depth, full.shape[-2]
    span = {ROUTE_A: pl.ds(0, CUT), ROUTE_B: pl.ds(CUT, rows - CUT)}
    coord = {ROUTE_A: (net.s, net.y), ROUTE_B: (net.y, net.s)}
    other = {ROUTE_A: net.away, ROUTE_B: net.away_y}
    z, c = net.z, net.c

    def part(p, f, z_of, l, core):
        s, y = (f, l) if p == ROUTE_A else (l, f)
        return full.at[s, z_of, y, core, span[p], :]

    def dev(p, f, z_of, l, core):
        s, y = (f, l) if p == ROUTE_A else (l, f)
        return net.at(s, z_of, y, core)

    def like(p):
        return lambda: full.at[0, 0, 0, 0, span[p], :]

    def spread(p, f_of, rel, ways):
        f, l = coord[p]
        got = part(p, f_of, z + rel, l, c)
        if UP in ways and 1 - rel < depth:
            key = (tag, p, UP, 1 - rel, f_of)
            net.when(net.high[1], lambda: net.send(got, got, dev(p, f, z + 1, l, c), key, like(p)))
        if DOWN in ways and 1 + rel < depth:
            key = (tag, p, DOWN, 1 + rel, f_of)
            net.when(net.low[1], lambda: net.send(got, got, dev(p, f, z - 1, l, c), key, like(p)))
        net.send(got, got, dev(p, f, z, 1 - l, c), (tag, p, L, rel, f_of), like(p))

    def exists(rel, body):
        if rel == 0:
            body()
        else:
            net.when(net.low[-rel] if rel < 0 else net.high[rel], body)

    def to_core(p, rel, f_of, l_rel):
        f, l = coord[p]
        got = part(p, f_of, z + rel, l if l_rel == 0 else 1 - l, c)
        net.send(got, got, net.at(c=1 - c), (tag, p, CORE, rel, f_of, l_rel), like(p))

    def first(p):
        f, l = coord[p]
        got = part(p, f, z, l, c)
        net.send(got, got, dev(p, 1 - f, z, l, c), (tag, p, F), like(p))

    def near(p, f_of):
        f, l = coord[p]
        net.when(other[p][f_of], lambda: net.recv(part(p, f_of, z, l, c), (tag, p, F)))
        spread(p, f_of, 0, (UP, DOWN))
        to_core(p, 0, f_of, 0)

    def along(p, dist, f_of):
        f, l = coord[p]
        for way, rel in ((UP, -dist), (DOWN, dist)):

            def body(way=way, rel=rel):
                net.recv(part(p, f_of, z + rel, l, c), (tag, p, way, dist, f_of))
                spread(p, f_of, rel, (way,))
                to_core(p, rel, f_of, 0)

            exists(rel, body)

    def across(p, dist, f_of):
        f, l = coord[p]
        for rel in sorted({-dist, dist}):

            def body(rel=rel):
                net.recv(part(p, f_of, z + rel, 1 - l, c), (tag, p, L, rel, f_of))
                to_core(p, rel, f_of, 1)

            exists(rel, body)

    def from_core(p, f_of, side):
        f, l = coord[p]

        def body(l_rel):
            for rel in range(1 - depth, depth):
                got = lambda rel=rel: part(p, f_of, z + rel, l if l_rel == 0 else 1 - l, 1 - c)
                exists(rel, lambda rel=rel: net.recv(got(), (tag, p, CORE, rel, f_of, l_rel)))

        if p == ROUTE_A:
            body(0)
            body(1)
        else:
            net.when(net.home[side], lambda: body(0))
            net.when(net.away[side], lambda: body(1))

    ticks = {}
    for p in "AB":
        ticks[FIRST, p] = functools.partial(first, p)
        for f_of in (0, 1):
            ticks[NEAR, p, f_of] = functools.partial(near, p, f_of)
            for dist in range(1, depth):
                ticks[ALONG, p, dist, f_of] = functools.partial(along, p, dist, f_of)
            for dist in range(depth):
                ticks[ACROSS, p, dist, f_of] = functools.partial(across, p, dist, f_of)
            for side in (0, 1):
                if p == ROUTE_B or side == f_of:
                    ticks[CORE, p, f_of, side] = functools.partial(from_core, p, f_of, side)
    return ticks


def reduce_extra(rows, count):
    half = (rows - CUT) // 2
    return {XA: (CUT, count), EA: (CUT, count), EB: (2, half, count), YB: (half, count), XC: (half, count)}


def reduce_ticks(net, slots, own, room, extra, out, side, tag, columns):
    depth, rows = net.depth, room.shape[-2]
    cols = pl.ds(*columns)
    half = (rows - CUT) // 2
    s, z, y, c = net.s, net.z, net.y, net.c
    above = pl.ds(0, CUT)
    x_dev, y_dev, c_dev = net.at(s=1 - s), net.at(y=1 - y), net.at(c=1 - c)

    def part_of(which):
        return pl.ds(pl.multiple_of(CUT + which * half, half), half)

    mine, theirs = part_of(s), part_of(1 - s)
    rc = room.at[:, :, 0]
    ya = lambda z1: room.at[z1, 0, 1, above, cols]
    xb = lambda z1: room.at[z1, :, 1, pl.ds(CUT, half), cols]
    za = lambda place: room.at[place, 1, 1, above, cols] if place < depth else extra[EA]
    zb = lambda place: room.at[place, :, 1, pl.ds(CUT + half, half), cols] if place < depth else extra[EB]

    def start(z1, slot):
        like = lambda: rc.at[z1, :, :, cols]
        net.send(slots.at[slot, :, 1 - c, :, cols], like(), c_dev, (tag, C, z1), like, (SLOT, slot))

    def cores(z1):
        net.recv(rc.at[z1, :, :, cols], (tag, C, z1))
        for y1 in (0, 1):
            rc[z1, y1, :, cols] = rc[z1, y1, :, cols] + own[z1, y1, :, cols]
        net.send(rc.at[z1, 1 - y, above, cols], ya(z1), y_dev, (tag, YA, z1), lambda: ya(z1))
        net.send(rc.at[z1, :, theirs, cols], xb(z1), x_dev, (tag, XB, z1), lambda: xb(z1))

    def add_a(z1, ref):
        rc[z1, y, above, cols] = rc[z1, y, above, cols] + ref[...]

    def add_b(z1, ref):
        for y1 in (0, 1):
            rc[z1, y1, mine, cols] = rc[z1, y1, mine, cols] + ref[y1]

    def planes(z1):
        net.recv(ya(z1), (tag, YA, z1))
        add_a(z1, ya(z1))
        net.recv(xb(z1), (tag, XB, z1))
        add_b(z1, xb(z1))

    def wave(k, j):
        def go(way, z_here, z1):
            step = 1 if way == UP else -1
            place = z1 + 1 if way == UP else z1
            if k > 0:
                net.recv(za(place), (tag, ZA, place))
                add_a(z1, za(place))
                net.recv(zb(place), (tag, ZB, place))
                add_b(z1, zb(place))
            if z1 != z_here:
                to = net.at(z=z + step)
                net.send(rc.at[z1, y, above, cols], za(place), to, (tag, ZA, place), lambda: za(place))
                net.send(rc.at[z1, :, mine, cols], zb(place), to, (tag, ZB, place), lambda: zb(place))

        net.when(net.here[k], lambda: go(UP, k, depth - 1 - j))
        net.when(net.here[depth - 1 - k], lambda: go(DOWN, depth - 1 - k, j))

    def last_one():
        net.send(rc.at[z, 1 - y, mine, cols], extra[YB], y_dev, (tag, YB), lambda: extra[YB])
        net.when(
            net.away[side],
            lambda: net.send(rc.at[z, y, above, cols], extra[XA], x_dev, (tag, XA), lambda: extra[XA]),
        )

    def last_two():
        net.recv(extra[YB], (tag, YB))
        rc[z, y, mine, cols] = rc[z, y, mine, cols] + extra[YB][...]
        net.when(
            net.away[side],
            lambda: net.send(rc.at[z, y, mine, cols], extra[XC], x_dev, (tag, XC), lambda: extra[XC]),
        )

    def last_three():
        def body():
            net.recv(extra[XA], (tag, XA))
            total, more = out
            total[above, cols], more[above, cols] = rc[z, y, above, cols], extra[XA][...]
            total[mine, cols] = rc[z, y, mine, cols]
            net.recv(extra[XC], (tag, XC))
            total[theirs, cols] = extra[XC][...]
            more[pl.ds(CUT, rows - CUT), cols] = jnp.zeros((rows - CUT, columns[1]), BF)

        net.when(net.home[side], body)

    ticks = {}
    for z1 in range(depth):
        ticks[START, z1] = functools.partial(start, z1)
        ticks[CORES, z1] = functools.partial(cores, z1)
        ticks[PLANES, z1] = functools.partial(planes, z1)
        for j in range(depth - z1):
            ticks[WAVE, z1, j] = functools.partial(wave, z1, j)
    ticks[LAST, 1], ticks[LAST, 2], ticks[LAST, 3] = last_one, last_two, last_three
    return ticks


def flip_bit(index, bit):
    return index + bit * (1 - 2 * ((index // bit) % 2))


def total_partners(net):
    bits = [2**k for k in range(net_bits(lax.axis_size(DP)))]
    return [(net.s, flip_bit(net.d, bit)) for bit in bits] + [(1 - net.s, net.d)]


def net_bits(number):
    return number.bit_length() - 1


def total_ticks(net, sums, got, tag):
    partners = total_partners(net)

    def start(k):
        net.send(sums.at[k], got.at[k], partners[k], (tag, k), lambda: got.at[k])

    def finish(k):
        net.recv(got.at[k], (tag, k))
        sums[k + 1] = sums[k] + got[k]
        if k + 1 < len(partners):
            start(k + 1)

    ticks = {(START, 0): functools.partial(start, 0)}
    for k in range(len(partners)):
        ticks[STEP, k] = functools.partial(finish, k)
    return ticks


PAIR = 2 * HEAD_DIM


def dg(left, right, left_dim, right_dim):
    return lax.dot_general(
        left, right, (((left_dim,), (right_dim,)), ((), ())), preferred_element_type=F32
    )


def lane_ids(rows):
    return lax.broadcasted_iota(jnp.int32, (rows, PAIR), 1)


def head_lanes(h):
    lane = lane_ids(1)
    return jnp.where((lane >= h * HEAD_DIM) & (lane < (h + 1) * HEAD_DIM), 1.0, 0.0).astype(BF)


def spare_lanes(h):
    lane, first = lane_ids(1), (1 - h) * HEAD_DIM
    return jnp.where((lane >= first) & (lane < first + 3), 1.0, 0.0).astype(BF)


def with_constant(values, constant, h):
    high = constant.astype(BF).astype(F32)
    mid = (constant - high).astype(BF).astype(F32)
    low = constant - high - mid
    lane, first = lane_ids(values.shape[0]), (1 - h) * HEAD_DIM
    own = (lane >= h * HEAD_DIM) & (lane < (h + 1) * HEAD_DIM)
    out = jnp.where(own, values, 0.0)
    for k, term in enumerate((high, mid, low)):
        out = jnp.where(lane == first + k, term, out)
    return out.astype(BF)


def pair_lanes(p):
    return pl.ds(pl.multiple_of(p * PAIR, PAIR), PAIR)


def norm_rows(r, gain, shift):
    mean = jnp.mean(r, axis=-1, keepdims=True)
    centered = r - mean
    var = jnp.mean(centered * centered, axis=-1, keepdims=True)
    inv = lax.rsqrt(var + EPSILON)
    normed = centered * inv
    return normed * gain + shift, normed, inv


def norm_rows_back(grad, normed, inv, gain):
    dn = grad * gain
    out = inv * (
        dn
        - jnp.mean(dn, axis=-1, keepdims=True)
        - normed * jnp.mean(dn * normed, axis=-1, keepdims=True)
    )
    return out


def rowsum(values):
    return jnp.sum(values, axis=0, keepdims=True)


def by_rows(length, body, step=64):
    def go(k, carry):
        body(pl.ds(pl.multiple_of(k * step, step), step))
        return carry

    lax.fori_loop(0, length // step, go, 0)


def allowed_bias(bias, seg_row, seg_col):
    length = bias.shape[0]

    def body(span):
        shape = (span.size, length)
        query = lax.broadcasted_iota(jnp.int32, shape, 0) + span.start
        key = lax.broadcasted_iota(jnp.int32, shape, 1)
        ok = (key <= query) & (seg_col[span, 0:1] == seg_row[0:1, :].astype(F32))
        bias[span, :] = jnp.where(ok, 0.0, NEG_FILL)

    by_rows(length, body)


def attend_pair(p, q, k, v, q_aug, out, bias):
    lanes = pair_lanes(p)
    half = q.shape[0] // 2
    blocks = [(0, half, k.shape[0]), (half, half, k.shape[0])]
    if bias is not None:
        blocks = [(0, half, half), (half, half, 2 * half)]
    for first, rows, keys in blocks:
        span = pl.ds(first, rows)
        q_rows = q[span, lanes]
        k_rows, v_rows = k[pl.ds(0, keys), lanes], v[pl.ds(0, keys), lanes]
        outs = []
        for h in (0, 1):
            scores = dg(q_rows * head_lanes(h), k_rows, 1, 1)
            if bias is not None:
                scores = scores + bias[span, pl.ds(0, keys)]
            top = jnp.max(scores, axis=-1, keepdims=True)
            weight = jnp.exp(scores - top)
            total = jnp.sum(weight, axis=-1, keepdims=True)
            outs.append(dg(weight.astype(BF), v_rows, 1, 0) * (1.0 / total))
            q_aug[2 * p + h, span, :] = with_constant(q_rows.astype(F32), -(top + jnp.log(total)), h)
        out[span, lanes] = jnp.where(lane_ids(rows) < HEAD_DIM, outs[0], outs[1]).astype(BF)


def whole(ref):
    return ref[...].reshape(-1, ref.shape[-1])


class Local:
    def __init__(self, sems):
        self.sems, self.count, self.open = sems, 0, []

    def copy(self, src, dst):
        move = pltpu.make_async_copy(src, dst, self.sems.at[self.count])
        self.count += 1
        move.start()
        return move

    def save(self, src, dst):
        self.open.append(self.copy(src, dst))

    def drain(self):
        for move in self.open:
            move.wait()


def attend_pair_back(p, q_aug, k, v, a, da, dq, dk, dv, bias):
    lanes = pair_lanes(p)
    length, keys_all = da.shape[0], k.shape[0]
    part = dk[0].shape[0]
    half = length // 2
    blocks = [(half, half, keys_all), (0, half, keys_all)]
    if bias is not None:
        keys_all = length
        blocks = [(half, half, length), (0, half, half)]
    sums = None
    for first, rows, keys in blocks:
        span = pl.ds(first, rows)
        k_rows, v_rows = k[pl.ds(0, keys), lanes], v[pl.ds(0, keys), lanes]
        grad = da[span, lanes]
        grad_wide = grad.astype(F32)
        prod = grad_wide * a[span, lanes].astype(F32)
        q0, q1 = q_aug[2 * p, span, :], q_aug[2 * p + 1, span, :]
        q_t = (q0 * head_lanes(0) + q1 * head_lanes(1)).T
        grad_t = grad.T
        dqs, dks, dvs = [], [], []
        for h, q_h in ((0, q0), (1, q1)):
            lane = lane_ids(rows)
            own = (lane >= h * HEAD_DIM) & (lane < (h + 1) * HEAD_DIM)
            dot = jnp.sum(jnp.where(own, prod, 0.0), axis=-1, keepdims=True)
            spare = spare_lanes(h)
            keep = 1 - spare
            scores = dg(q_h, k_rows * keep + spare, 1, 1)
            if bias is not None:
                scores = scores + bias[span, pl.ds(0, keys)]
            prob = jnp.exp(scores)
            d_prob = dg(with_constant(grad_wide, -dot, h), v_rows * keep + spare, 1, 1)
            d_score = (prob * d_prob).astype(BF)
            own_rows = slice(h * HEAD_DIM, (h + 1) * HEAD_DIM)
            dqs.append(dg(d_score, k_rows, 1, 0))
            dvs.append(dg(grad_t[own_rows], prob.astype(BF), 1, 0))
            dks.append(dg(q_t[own_rows], d_score, 1, 0))
        d_q = jnp.where(lane_ids(rows) < HEAD_DIM, dqs[0], dqs[1]).astype(BF)
        dq[span, lanes] = (d_q.astype(F32) * (1.0 / math.sqrt(HEAD_DIM))).astype(BF)
        new = [jnp.concatenate(parts, 0) for parts in (dks, dvs)]
        if sums is None:
            sums = new
        else:
            sums = [
                old + term if keys == keys_all else jnp.concatenate([old[:, :keys] + term, old[:, keys:]], 1)
                for old, term in zip(sums, new)
            ]
    for refs, value in zip((dk, dv), sums):
        low = value.astype(BF)
        for j in range(keys_all // part):
            refs[j][:, lanes] = low[:, j * part : (j + 1) * part].T


PLAN = {
    BEGIN: (
        (SEG, SEND, 0), (ATTN, FIRST, ROUTE_A), (ATTN, FIRST, ROUTE_B), (ATTN, NEAR, ROUTE_B, 0),
        (FFN, FIRST, ROUTE_B), (FFN, NEAR, ROUTE_B, 0), (X, SEND, 1), (ATTN, NEAR, ROUTE_B, 1),
        (ATTN, NEAR, ROUTE_A, 0), (ATTN, ALONG, ROUTE_B, 1, 0), (ATTN, ALONG, ROUTE_A, 1, 0),
        (ATTN, ALONG, ROUTE_B, 2, 0), (ATTN, ALONG, ROUTE_A, 2, 0), (FFN, FIRST, ROUTE_A),
        (ATTN, ALONG, ROUTE_B, 3, 0),
    ),
    COT: (
        (SEG, RECV, 0), (X, SEND, 0), (ATTN, NEAR, ROUTE_A, 1), (ATTN, ACROSS, ROUTE_B, 1, 0),
        (ATTN, ACROSS, ROUTE_B, 2, 0), (ATTN, ALONG, ROUTE_A, 1, 1), (ATTN, ALONG, ROUTE_A, 3, 0),
        (ATTN, ACROSS, ROUTE_B, 3, 0), (ATTN, ACROSS, ROUTE_A, 0, 0), (ATTN, ACROSS, ROUTE_B, 0, 0),
        (ATTN, ACROSS, ROUTE_A, 2, 0), (ATTN, ALONG, ROUTE_B, 1, 1), (ATTN, ACROSS, ROUTE_A, 1, 0),
    ),
    WEIGHTS: (
        (X, RECV, 1), (FFN, NEAR, ROUTE_A, 1), (ATTN, ALONG, ROUTE_B, 2, 1), (FFN, NEAR, ROUTE_A, 0),
        (FFN, ALONG, ROUTE_B, 1, 0), (ATTN, ALONG, ROUTE_A, 2, 1), (ATTN, ACROSS, ROUTE_A, 3, 0), (X, RECV, 0),
        (ATTN, CORE, ROUTE_A, 0, 0), (ATTN, CORE, ROUTE_B, 0, 0), (ATTN, CORE, ROUTE_B, 0, 1),
        (ATTN, ALONG, ROUTE_B, 3, 1), (ATTN, ACROSS, ROUTE_B, 0, 1), (ATTN, ACROSS, ROUTE_B, 1, 1),
        (ATTN, ACROSS, ROUTE_B, 2, 1), (ATTN, ACROSS, ROUTE_B, 3, 1), (ATTN, CORE, ROUTE_B, 1, 0),
    ),
    (SELF, 0): (
        (FFN, NEAR, ROUTE_B, 1),
    ),
    (SELF, 1): (
        (FFN, ALONG, ROUTE_A, 1, 1),
    ),
    (SELF, 2): (
        (ATTN, ACROSS, ROUTE_A, 1, 1), (ATTN, ALONG, ROUTE_A, 3, 1),
    ),
    (SELF, 3): (
        (FFN, ACROSS, ROUTE_B, 0, 1), (COT, SEND, 0),
    ),
    (SELF, 4): (
        (ATTN, ACROSS, ROUTE_A, 0, 1), (FFN, ALONG, ROUTE_B, 1, 1),
    ),
    (SELF, 5): (
        (FFN, ACROSS, ROUTE_B, 0, 0), (FFN, ALONG, ROUTE_A, 2, 1),
    ),
    NORM1: (
        (ATTN, ACROSS, ROUTE_A, 2, 1), (ATTN, ACROSS, ROUTE_A, 3, 1), (ATTN, CORE, ROUTE_A, 1, 1),
        (ATTN, CORE, ROUTE_B, 1, 1),
    ),
    KEYS: (
        (FFN, ALONG, ROUTE_A, 1, 0),
    ),
    VALUES: (
        (FFN, ALONG, ROUTE_B, 2, 1), (FFN, ALONG, ROUTE_B, 2, 0),
    ),
    (CROSS, 0): (
        (FFN, ALONG, ROUTE_A, 3, 1),
    ),
    (CROSS, 1): (
        (FFN, ACROSS, ROUTE_B, 2, 1), (FFN, ACROSS, ROUTE_A, 1, 1),
    ),
    (CROSS, 2): (
        (FFN, ALONG, ROUTE_A, 2, 0), (FFN, ALONG, ROUTE_B, 3, 1), (FFN, ACROSS, ROUTE_A, 2, 1),
        (FFN, ALONG, ROUTE_B, 3, 0),
    ),
    (CROSS, 3): (
        (FFN, ALONG, ROUTE_A, 3, 0),
    ),
    (CROSS, 4): (
        (FFN, ACROSS, ROUTE_B, 1, 1), (FFN, ACROSS, ROUTE_B, 3, 1), (FFN, ACROSS, ROUTE_B, 3, 0),
        (FFN, ACROSS, ROUTE_A, 1, 0), (COT, SEND, 1), (FFN, ACROSS, ROUTE_A, 3, 1), (FFN, ACROSS, ROUTE_A, 0, 1),
        (FFN, ACROSS, ROUTE_B, 2, 0),
    ),
    (CROSS, 5): (
        (FFN, ACROSS, ROUTE_B, 1, 0), (FFN, ACROSS, ROUTE_A, 2, 0),
    ),
    NORM2: (
        (FFN, ACROSS, ROUTE_A, 3, 0), (FFN, ACROSS, ROUTE_A, 0, 0),
    ),
    (FFN, 0): (
        (FFN, CORE, ROUTE_B, 1, 1), (FFN, CORE, ROUTE_B, 1, 0), (FFN, CORE, ROUTE_A, 1, 1),
        (FFN, CORE, ROUTE_B, 0, 0), (FFN, CORE, ROUTE_B, 0, 1), (FFN, CORE, ROUTE_A, 0, 0),
    ),
    FFN_DONE: (
        (COT, RECV, 1), (COT, RECV, 0),
    ),
    NORM3: (
        (LO, SEND, 0), (LO, SEND, 1),
    ),
    (DW2, 1): (
        (F1, CORES, 0),
    ),
    (DW2, 3): (
        (F1, CORES, 1),
    ),
    (DW1, 1): (
        (F1, CORES, 2),
    ),
    (DW1, 2): (
        (F1, CORES, 3),
    ),
    (DW1, 3): (
        (F0, CORES, 1),
    ),
    NORM2_BACK: (
        (F0, CORES, 3),
    ),
    (CROSS_BACK, 0): (
        (F0, CORES, 2), (F1, PLANES, 2), (F1, PLANES, 1), (F1, WAVE, 0, 1),
    ),
    (CROSS_BACK, 1): (
        (F1, WAVE, 0, 2), (CR, CORES, 3), (F1, PLANES, 3),
    ),
    (CROSS_BACK, 2): (
        (F0, PLANES, 1), (F0, PLANES, 2), (F0, WAVE, 0, 1), (F1, PLANES, 0), (F1, WAVE, 0, 0),
    ),
    (CROSS_BACK, 4): (
        (F1, WAVE, 1, 1), (F0, CORES, 0),
    ),
    DCQ: (
        (F1, WAVE, 1, 2),
    ),
    DCK: (
        (CR, CORES, 0), (F0, WAVE, 0, 2),
    ),
    DCV: (
        (CR, PLANES, 3),
    ),
    DWO: (
        (CR, PLANES, 0), (CR, WAVE, 0, 0), (CR, CORES, 2),
    ),
    (SELF_BACK, 0): (
        (F0, PLANES, 3),
    ),
    (SELF_BACK, 1): (
        (F1, WAVE, 1, 0),
    ),
    (SL, 0): (
        (CR, CORES, 1),
    ),
    (SL, 1): (
        (F0, PLANES, 0), (F0, WAVE, 0, 0), (F1, WAVE, 2, 1),
    ),
    (SL, 2): (
        (F0, WAVE, 1, 1),
    ),
    (SELF_BACK, 3): (
        (SL, CORES, 0),
    ),
    (SELF_BACK, 5): (
        (SL, CORES, 3),
    ),
    (SR, 0): (
        (CR, PLANES, 2), (CR, PLANES, 1), (CR, WAVE, 0, 2), (SR, CORES, 3), (SR, CORES, 0),
        (SL, CORES, 1),
    ),
    (SR, 2): (
        (CR, WAVE, 1, 0),
    ),
    VEC: (
        (SM, START, 0), (SL, CORES, 2),
    ),
    (DX, 0): (
        (IG, SEND, 0), (F0, WAVE, 1, 0), (SR, PLANES, 3), (SR, PLANES, 0), (SR, WAVE, 0, 0),
        (SL, PLANES, 0), (SL, PLANES, 3), (SL, WAVE, 0, 3),
    ),
    (DX, 1): (
        (IG, SEND, 1), (F1, WAVE, 2, 0), (SR, CORES, 1), (SL, WAVE, 0, 0),
    ),
    LOADS: (
        (CR, WAVE, 1, 2),
    ),
    (ENC, 1): (
        (F0, WAVE, 2, 1),
    ),
    (ENC, 3): (
        (SM, STEP, 0), (SR, WAVE, 1, 0), (SL, PLANES, 1), (SL, PLANES, 2), (SL, WAVE, 0, 1),
    ),
    END: (
        (LO, RECV, 1), (IG, RECV, 0), (CR, WAVE, 2, 0), (F0, WAVE, 1, 2), (CR, WAVE, 0, 1),
        (LO, RECV, 0), (F1, WAVE, 3, 0),
    ),
    END2: (
        (SL, WAVE, 0, 2),
    ),
    END3: (
        (SL, WAVE, 1, 0), (CR, WAVE, 0, 3), (F0, WAVE, 2, 0), (SR, CORES, 2), (SL, WAVE, 1, 1),
        (SR, PLANES, 1), (SR, PLANES, 2), (SR, WAVE, 0, 1), (F0, WAVE, 0, 3), (SR, WAVE, 2, 0),
        (SL, WAVE, 2, 1), (SR, WAVE, 0, 2), (SR, WAVE, 0, 3), (SL, WAVE, 2, 0), (SM, STEP, 1),
        (CR, WAVE, 1, 1), (IG, RECV, 1), (F0, WAVE, 3, 0), (F0, LAST, 1), (F0, LAST, 2),
        (F1, WAVE, 0, 3), (F1, LAST, 1), (F1, LAST, 2), (SR, WAVE, 1, 1), (CR, WAVE, 2, 1),
        (CR, WAVE, 3, 0), (SL, WAVE, 1, 2), (SL, WAVE, 3, 0), (SR, WAVE, 1, 2), (SR, WAVE, 2, 1),
        (SR, WAVE, 3, 0), (CR, LAST, 1), (SL, LAST, 1), (SR, LAST, 1), (SM, STEP, 2),
        (CR, LAST, 2), (SL, LAST, 2), (SR, LAST, 2), (SM, STEP, 3), (F1, LAST, 3),
        (F0, LAST, 3), (CR, LAST, 3), (SL, LAST, 3), (SR, LAST, 3), (SM, STEP, 4),
    ),
}


def transfer_plan(depth):
    assert depth == 4
    return PLAN


def once(loop_index, at, body):
    run_when(loop_index == at, body)


SUMS = {
    F1: (0, FFN_GRAD, 1, (0, 768)),
    F0: (1, FFN_GRAD, 0, (0, 768)),
    CR: (3, ATTN_GRAD, 1, (0, 768)),
    SL: (2, ATTN_GRAD, 0, (0, 384)),
    SR: (2, ATTN_GRAD, 0, (384, 384)),
}


def mega_kernel(names, plan, *refs):
    r = types.SimpleNamespace(**dict(zip(names, refs)))
    net = Net(r.send_sems, r.recv_sems)
    s, z, y, c, depth = net.s, net.z, net.y, net.c, net.depth
    small, vec, attn_full, ffn_full = r.small, r.vec, r.attn_full, r.ffn_full
    local = Local(r.local_sems)
    scale = 1.0 / math.sqrt(HEAD_DIM)
    length, width = r.x.shape
    enc_length = r.enc.shape[0]
    pairs = width // PAIR
    partner_dev = net.at(s=1 - s)
    t, acc, bias = r.t, r.acc, r.t.at[:, pl.ds(0, length)]
    g, own, slots = r.g, r.own, r.slots

    ticks = {}
    for tag, full in ((ATTN, attn_full), (FFN, ffn_full)):
        ticks.update({(tag, *key): tick for key, tick in gather_ticks(net, full, tag).items()})
    for tag, (place, out, side, columns) in SUMS.items():
        extra = {name: getattr(r, name + tag) for name in reduce_extra(2, 1)}
        room = (attn_full, ffn_full)[place // 2].at[place % 2]
        terms = (getattr(r, out), getattr(r, out + _MORE))
        steps = reduce_ticks(net, slots, own, room, extra, terms, side, tag, columns)
        ticks.update({(tag, *key): step for key, step in steps.items()})

    def exchange(name, src, dst, parts):
        rows = src.shape[0] // parts

        def send(k):
            span = pl.ds(k * rows, rows)
            net.send(src.at[span], dst.at[span], partner_dev, (name, k), lambda: dst.at[span], name)

        def recv(k):
            net.recv(dst.at[pl.ds(k * rows, rows)], (name, k))

        for k in range(parts):
            ticks[name, SEND, k] = functools.partial(send, k)
            ticks[name, RECV, k] = functools.partial(recv, k)

    exchange(SEG, r.seg_mine, r.seg, 1)
    exchange(X, r.x_own, r.x, 2)
    exchange(COT, g.at[0], r.cot, 2)
    exchange(LO, r.cot, r.lo_got, 2)
    exchange(IG, r.h1, r.ig_got, 2)
    ticks.update({(SM, *key): step for key, step in total_ticks(net, r.sums, r.sum_got, SM).items()})
    done = set()

    def at(point, p=None, turns=range(pairs)):
        if p is None:
            for key in plan.get(point, ()):
                assert key not in done, key
                done.add(key)
                ticks[key]()
            return
        for k in turns:
            if plan.get((point, k)):
                once(p, k, lambda k=k: at((point, k)))

    def signal_room(sem):
        for to in neighbours:
            pl.semaphore_signal(sem, inc=1, device_id=to, device_id_type=MESH_ID)
        run_when(net.low[1], lambda: pl.semaphore_signal(sem, inc=1, device_id=net.at(z=z - 1), device_id_type=MESH_ID))
        run_when(net.high[1], lambda: pl.semaphore_signal(sem, inc=1, device_id=net.at(z=z + 1), device_id_type=MESH_ID))

    def wait_room(sem):
        pl.semaphore_wait(sem, len(neighbours) + net.low[1].astype(jnp.int32) + net.high[1].astype(jnp.int32))

    neighbours = [net.at(s=1 - s), net.at(y=1 - y), net.at(c=1 - c)]

    r.seg_mine[...] = jnp.broadcast_to(r.seg_own[...], r.seg_mine.shape)
    attn_full[s, z, y, c] = r.attn_own[...].astype(BF)
    ffn_full[s, z, y, c] = r.ffn_own[...].astype(BF)
    net.greet([to for to in total_partners(net)[2:-1]])
    at(BEGIN)
    enc_load = local.copy(r.enc_own, r.enc)
    local.copy(r.cot_own, acc).wait()

    def low_cot(span):
        g[0, span, :] = acc[span, :].astype(BF)

    by_rows(length, low_cot)
    at(COT)
    r.seg_col[...] = r.seg[...].astype(F32).T
    allowed_bias(bias, r.seg, r.seg_col)
    at(WEIGHTS)

    def block(k):
        return whole(attn_full.at[k // depth, k % depth])

    def into_heads(dst, left, right, shift, factor):
        half = left.shape[0] // 2
        for k in (0, 1):
            span = pl.ds(k * half, half)
            value = dg(left[span, :], right, 1, 0)
            if shift is not None:
                value = value + shift
            if factor is not None:
                value = value * factor
            dst[span, :] = value.astype(BF)

    into_heads(r.q, r.x, block(0), small[0:1], scale)
    into_heads(r.k, r.x, block(1), None, None)
    into_heads(r.v, r.x, block(2), small[1:2], None)
    at("qkv")

    def self_body(p, carry):
        attend_pair(p, r.q, r.k, r.v, r.qa, r.a, bias)
        at(SELF, p)
        return carry

    lax.fori_loop(0, pairs, self_body, 0)
    t[...] = dg(r.a[...], block(3), 1, 0)

    def norm_one(span):
        res = r.x[span, :].astype(F32) + t[span, :] + small[2:3]
        hidden, normed, inv = norm_rows(res, small[7:8], small[8:9])
        acc[span, :] = hidden
        r.h1[span, :] = hidden.astype(BF)
        r.n1[span, :] = normed
        r.inv[span, :] = jnp.broadcast_to(inv, (span.size, PAIR))

    by_rows(length, norm_one)
    at(NORM1)
    weights_saved = local.copy(attn_full, r.attn_out)

    into_heads(r.q, r.h1, block(4), small[3:4], scale)
    enc_load.wait()
    into_heads(r.k2, r.enc, block(5), None, None)
    at(KEYS)
    into_heads(r.v2, r.enc, block(6), small[4:5], None)
    at(VALUES)

    def cross_body(p, carry):
        attend_pair(p, r.q, r.k2, r.v2, r.qb, r.a2, None)
        at(CROSS, p)
        return carry

    lax.fori_loop(0, pairs, cross_body, 0)
    t[...] = dg(r.a2[...], block(7), 1, 0)

    def norm_two(span):
        res = acc[span, :] + t[span, :] + small[5:6]
        hidden, normed, inv = norm_rows(res, small[9:10], small[10:11])
        acc[span, :] = hidden
        r.h2[span, :] = hidden.astype(BF)
        r.n2[span, :] = normed
        r.inv[span, :] = jnp.where(lane_ids(span.size) < HEAD_DIM, r.inv[span, :], inv)

    by_rows(length, norm_two)
    at(NORM2)

    vec[...] = jnp.zeros_like(vec)
    root = math.sqrt(0.5)
    weights_saved.wait()
    net.drain_one(COT)
    for k in range(depth):
        at((FFN, k))
        t[...] = dg(r.h2[...], whole(ffn_full.at[0, k]), 1, 1)

        def gelu(span, k=k):
            u = t[span, :] + small[13 + k : 14 + k]
            below = 0.5 + 0.5 * lax.erf(u * root)
            g[k, span, :] = (u * below).astype(BF)
            r.gp[pl.ds(span.start + k * length, span.size), :] = (below + u * (jnp.exp(-0.5 * u * u) * (1.0 / math.sqrt(2.0 * math.pi)))).astype(BF)

        by_rows(length, gelu)
        acc[...] += dg(g[k], whole(ffn_full.at[1, k]), 1, 0)
    net.drain()
    signal_room(r.room_a)
    at(FFN_DONE)

    def norm_three(span):
        hidden, normed, inv = norm_rows(acc[span, :] + small[6:7], small[11:12], small[12:13])
        cot = r.cot[span, :].astype(F32)
        r.cot[span, :] = hidden.astype(BF)
        dr3 = norm_rows_back(cot, normed, inv, small[11:12])
        vec[11:12] += rowsum(cot * normed)
        vec[12:13] += rowsum(cot)
        acc[span, :] = dr3
        low = dr3.astype(BF)
        r.dy[span, :] = low
        vec[6:7] += rowsum(low.astype(F32))

    by_rows(length, norm_three)
    at(NORM3)

    used = [0]

    def put(left, right, tags, z1, first=0):
        cols = pl.ds(first, right.shape[-1])
        slot = used[0] % slots.shape[0]
        used[0] += 1
        if used[0] > slots.shape[0]:
            net.drain_one((SLOT, slot))
        slots[slot, :, :, :, cols] = dg(left, right, 0, 0).astype(BF).reshape(*slots.shape[1:4], -1)
        for y1 in (0, 1):
            own[z1, y1, :, cols] = slots[slot, y1, c, :, cols]
        for tag in tags:
            ticks[tag, START, z1](slot)

    wait_room(r.room_a)
    for k in range(depth):
        put(g[k], r.dy[...], (F1,), k)
        at((DW2, k))
        t[...] = dg(r.dy[...], whole(ffn_full.at[1, k]), 1, 1)

        def through(span, k=k):
            du = (t[span, :] * r.gp[pl.ds(span.start + k * length, span.size), :].astype(F32)).astype(BF)
            g[k, span, :] = du
            vec[13 + k : 14 + k] += rowsum(du.astype(F32))

        by_rows(length, through)
        at(("du", k))
    for k in range(depth):
        acc[...] += dg(g[k], whole(ffn_full.at[0, k]), 1, 0)
        at(("dh", k))
        put(g[k], r.h2[...], (F0,), k)
        at((DW1, k))
    signal_room(r.room_f)

    loads = {}

    def load_weight(k, slot):
        block_rows = attn_full.shape[-2]
        loads[k] = [
            local.copy(
                r.attn_out.at[k // depth, k % depth, j // 2, j % 2],
                r.gp.at[pl.ds(slot * width + j * block_rows, block_rows)],
            )
            for j in range(4)
        ]

    def weight(k, slot):
        for move in loads[k]:
            move.wait()
        return r.gp[pl.ds(slot * width, width), :]

    load_weight(7, 0)
    do, da, dq = r.dy, r.h2, r.q
    dk, dv = [g.at[0], g.at[1]], [g.at[2], g.at[3]]

    def norm_two_back(span):
        grad, normed = acc[span, :], r.n2[span, :]
        vec[9:10] += rowsum(grad * normed)
        vec[10:11] += rowsum(grad)
        grad = norm_rows_back(grad, normed, r.inv[span, HEAD_DIM : HEAD_DIM + 1], small[9:10])
        acc[span, :] = grad
        low = grad.astype(BF)
        do[span, :] = low
        vec[5:6] += rowsum(low.astype(F32))

    by_rows(length, norm_two_back)
    at(NORM2_BACK)

    def low_dot(dst, left, right):
        half = left.shape[0] // 2
        for k in (0, 1):
            span = pl.ds(k * half, half)
            dst[span, :] = dg(left[span, :], right, 1, 1).astype(BF)

    low_dot(da, do, weight(7, 0))
    load_weight(4, 0)
    wait_room(r.room_f)
    put(r.a2[...], do[...], (CR,), 3)
    at("dco")

    def cross_back(p, carry):
        attend_pair_back(p, r.qb, r.k2, r.v2, r.a2, da, dq, dk, dv, None)
        at(CROSS_BACK, p)
        return carry

    lax.fori_loop(0, pairs, cross_back, 0)
    put(r.h1[...], dq[...], (CR,), 0)
    at(DCQ)
    acc[...] += dg(dq[...], weight(4, 0), 1, 1)
    put(r.enc[...], g[0:2].reshape(enc_length, width), (CR,), 1)
    at(DCK)
    put(r.enc[...], g[2:4].reshape(enc_length, width), (CR,), 2)
    at(DCV)

    def colsum_into(row, ref):
        def body(span):
            vec[row : row + 1] += rowsum(ref[span, :].astype(F32))

        by_rows(ref.shape[0], body)

    colsum_into(3, dq)
    colsum_into(4, dv[0])
    colsum_into(4, dv[1])
    load_weight(3, 0)

    def norm_one_back(span):
        grad, normed = acc[span, :], r.n1[span, :]
        vec[7:8] += rowsum(grad * normed)
        vec[8:9] += rowsum(grad)
        grad = norm_rows_back(grad, normed, r.inv[span, 0:1], small[7:8])
        acc[span, :] = grad
        low = grad.astype(BF)
        do[span, :] = low
        vec[2:3] += rowsum(low.astype(F32))

    by_rows(length, norm_one_back)
    load_weight(0, 1)
    load_weight(1, 2)

    low_dot(da, do, weight(3, 0))
    load_weight(2, 0)
    put(r.a[...], do[...], (SL, SR), 3)
    at(DWO)
    allowed_bias(bias, r.seg, r.seg_col)
    ek, ev = r.k2.at[pl.ds(0, length)], r.v2.at[pl.ds(0, length)]
    edge = SUMS[SR][3][0]
    turns = edge // PAIR

    def self_back(some, p, carry):
        attend_pair_back(p, r.qa, r.k, r.v, r.a, da, dq, [ek], [ev], bias)
        at(SELF_BACK, p, some)
        return carry

    for tag, first, some in ((SL, 0, range(turns)), (SR, edge, range(turns, pairs))):
        lax.fori_loop(some.start, some.stop, functools.partial(self_back, some), 0)
        cols = pl.ds(first, len(some) * PAIR)
        for z1, ref in ((0, dq), (1, ek), (2, ev)):
            put(r.x[...], ref[:, cols], (tag,), z1, first)
            at((tag, z1))
    colsum_into(0, dq)
    colsum_into(1, ev)
    r.sums[0] = vec[...]
    at(VEC)
    from_q, from_k, from_v = weight(0, 1), weight(1, 2), weight(2, 0)
    half = length // 2
    for k in (0, 1):
        span = pl.ds(k * half, half)
        grad = acc[span, :] + dg(dq[span, :], from_q, 1, 1)
        grad = grad + dg(ek[span, :], from_k, 1, 1) + dg(ev[span, :], from_v, 1, 1)
        r.h1[span, :] = grad.astype(BF)
        at((DX, k))
    load_weight(5, 1)
    load_weight(6, 2)
    at(LOADS)
    from_keys, from_values = weight(5, 1), weight(6, 2)
    moves = [None, None]
    for k in range(4):
        span, rows = pl.ds((k % 2) * half, half), pl.ds((k % 2) * half, half)
        if moves[k % 2] is not None:
            moves[k % 2].wait()
        t[span, :] = dg(dk[k // 2][rows, :], from_keys, 1, 1) + dg(dv[k // 2][rows, :], from_values, 1, 1)
        moves[k % 2] = local.copy(t.at[span], r.enc_grad.at[pl.ds(k * half, half)])
        at((ENC, k))
    for move in moves:
        move.wait()
    at(END)

    at(END2)
    at(END3)
    r.small_grad[...] = r.sums[r.sums.shape[0] - 1]
    local.drain()
    net.drain()
    missing = [key for key in ticks if key not in done and key[1] != START]
    assert not missing, missing


def mega_call(x, enc, seg, cot, attn_own, ffn_own, small):
    rows, width = attn_own.shape
    depth = lax.axis_size(DP) // 4
    devices = lax.axis_size(DP) * 2
    length, enc_length = x.shape[0], enc.shape[0]
    heads = width // HEAD_DIM
    steps = net_bits(devices)
    act, enc_act, wide = ((length, width), BF), ((enc_length, width), BF), ((length, width), F32)
    aug, stack, col = ((heads, length, PAIR), BF), ((2, depth, 2, 2, rows, width), BF), ((length, PAIR), F32)
    many = ((depth, length, width), BF)
    vec = ((-(-small.shape[0] // 8) * 8, width), F32)
    own_rows = ((rows, width), BF)
    outs = dict(lo_got=act, ig_got=act, enc_grad=((enc_length, width), F32), attn_grad=own_rows, ffn_grad=own_rows, attn_grad_more=own_rows, ffn_grad_more=own_rows, small_grad=vec, attn_out=stack)
    inner = dict(
        attn_full=stack, ffn_full=stack, x=act, cot=act, enc=enc_act, seg=((8, length), jnp.int32), seg_mine=((8, length), jnp.int32), seg_col=((length, 8), F32),
        qa=aug, qb=aug, q=act, k=act, v=act, a=act, h1=act, k2=enc_act, v2=enc_act, a2=act, n1=wide, inv=col, acc=wide, t=wide,
        h2=act, n2=wide, g=many, gp=((max(depth * length, 3 * width), width), BF), dy=act, vec=vec,
        slots=((2, 2, 2, rows, width), BF), own=((depth, 2, rows, width), BF),
        sums=((steps + 1, *vec[0]), F32), sum_got=((steps, *vec[0]), F32),
    )
    for tag, (_, _, _, columns) in SUMS.items():
        inner.update({name + tag: (shape, BF) for name, shape in reduce_extra(rows, columns[1]).items()})
    inside, anywhere = pl.BlockSpec(memory_space=pltpu.VMEM), pl.BlockSpec(memory_space=pl.ANY)
    args = dict(x_own=x, enc_own=enc, seg_own=seg, cot_own=cot, attn_own=attn_own, ffn_own=ffn_own, small=small)
    names = (*args, *outs, *inner, "send_sems", "recv_sems", "local_sems", "room_a", "room_f")
    got = pl.pallas_call(
        functools.partial(mega_kernel, names, transfer_plan(depth)),
        out_shape=tuple(jax.ShapeDtypeStruct(*outs[name]) for name in outs),
        in_specs=[anywhere if name in ("x_own", "enc_own", "cot_own") else inside for name in args],
        out_specs=tuple(inside if "_grad" in name and name != ENC_GRAD else anywhere for name in outs),
        scratch_shapes=[
            *[pltpu.VMEM(*inner[name]) for name in inner],
            pltpu.SemaphoreType.DMA((440,)),
            pltpu.SemaphoreType.DMA((440,)),
            pltpu.SemaphoreType.DMA((64,)),
            pltpu.SemaphoreType.REGULAR,
            pltpu.SemaphoreType.REGULAR,
        ],
        compiler_params=pltpu.CompilerParams(collective_id=0, has_side_effects=True, vmem_limit_bytes=255 << 18),
        name="layer",
    )(*args.values())
    return dict(zip(outs, got))


def partner(value, axis, apart):
    mask = 2**apart
    pairs = [(source, source ^ mask) for source in range(lax.axis_size(axis))]
    return lax.ppermute(value, axis, pairs)


def matmul(left_op, right_op):
    return jnp.dot(left_op, right_op, preferred_element_type=jnp.float32)


def contract_rows(left_op, right_op):
    return lax.dot_general(
        left_op, right_op, (((0,), (0,)), ((), ())), preferred_element_type=jnp.float32
    )


def contract_cols(left_op, right_op):
    return lax.dot_general(
        left_op, right_op, (((1,), (1,)), ((), ())), preferred_element_type=jnp.float32
    )


def gelu_exact(pre_value):
    return jax.nn.gelu(pre_value, approximate=False)


def split_heads(matrix):
    return matrix.reshape(matrix.shape[0], HEADS, HEAD_DIM)


def merge_heads(tensor):
    return tensor.reshape(tensor.shape[0], HEADS * HEAD_DIM)


def column_sum(grad_low):
    return jnp.sum(grad_low.astype(jnp.float32), axis=0)


def norm_forward(residual, norm_gain, norm_shift):
    row_mean = jnp.mean(residual, axis=-1, keepdims=True)
    centered = residual - row_mean
    row_var = jnp.mean(centered * centered, axis=-1, keepdims=True)
    inv_std = lax.rsqrt(row_var + EPSILON)
    normed = centered * inv_std
    return (normed * norm_gain + norm_shift, normed, inv_std)


def norm_backward(grad_out, normed, inv_std, norm_gain):
    grad_norm = grad_out * norm_gain
    centered_grad = grad_norm - jnp.mean(grad_norm, axis=-1, keepdims=True)
    grad_res = inv_std * (
        centered_grad - normed * jnp.mean(grad_norm * normed, axis=-1, keepdims=True)
    )
    return (grad_res, jnp.sum(grad_out * normed, axis=0), jnp.sum(grad_out, axis=0))


def block_scores(q_block, keys_in, seg_row, first_row):
    scores = jnp.einsum(QHD_KHD_HQK, q_block, keys_in, preferred_element_type=jnp.float32)
    if seg_row is None:
        return scores
    block_len = q_block.shape[0]
    query_pos = first_row + jnp.arange(block_len)
    key_pos = jnp.arange(seg_row.shape[0])
    allowed = (key_pos[None, :] <= query_pos[:, None]) & (seg_row[:, None] == seg_row[None, :])
    return jnp.where(allowed[None], scores, NEG_FILL)


def attend_forward(queries, keys_in, values_in, seg_row):
    scores = block_scores(queries, keys_in, seg_row, 0)
    row_max = jnp.max(scores, axis=-1, keepdims=True)
    exp_scores = jnp.exp(scores - row_max)
    totals = jnp.sum(exp_scores, axis=-1, keepdims=True)
    attn_prob = (exp_scores / totals).astype(jnp.bfloat16)
    outputs = jnp.einsum(HQK_KHD_QHD, attn_prob, values_in, preferred_element_type=jnp.float32)
    lse_list = [row_max + jnp.log(totals)]
    return (outputs, lse_list)


def attend_backward(queries, keys_in, values_in, seg_row, lse_list, grad_mixed):
    query_len = queries.shape[0]
    block_len = min(512, query_len)
    grad_queries = []
    grad_keys = jnp.zeros(keys_in.shape, jnp.float32)
    grad_values = jnp.zeros(values_in.shape, jnp.float32)
    for block_index, first_row in enumerate(range(0, query_len, block_len)):
        scores = block_scores(queries, keys_in, seg_row, first_row)
        attn_prob = jnp.exp(scores - lse_list[block_index])
        grad_values = jnp.einsum(
            HQK_QHD_KHD,
            attn_prob.astype(jnp.bfloat16),
            grad_mixed,
            preferred_element_type=jnp.float32,
        )
        grad_prob = jnp.einsum(
            QHD_KHD_HQK, grad_mixed, values_in, preferred_element_type=jnp.float32
        )
        grad_scores = attn_prob * (
            grad_prob - jnp.sum(grad_prob * attn_prob, axis=-1, keepdims=True)
        )
        grad_low = grad_scores.astype(jnp.bfloat16)
        grad_queries.append(
            jnp.einsum(HQK_KHD_QHD, grad_low, keys_in, preferred_element_type=jnp.float32)
        )
        grad_keys = jnp.einsum(
            HQK_QHD_KHD, grad_low, queries, preferred_element_type=jnp.float32
        )
    grad_q_all = grad_queries[0].astype(jnp.bfloat16)
    return (grad_q_all, grad_keys.astype(jnp.bfloat16), grad_values.astype(jnp.bfloat16))


def layer_row(dec_row, enc_row, seg_row, cot_row, blocks, w_in, w_out, vectors):
    w_query, w_key, w_value, w_proj, c_query, c_key, c_value, c_proj = blocks
    scale = 1.0 / math.sqrt(HEAD_DIM)
    bias_in = vectors[13:].reshape(-1)
    dec_full = dec_row.astype(jnp.float32)
    queries = ((matmul(dec_row, w_query) + vectors[0]) * scale).astype(jnp.bfloat16)
    keys_self = matmul(dec_row, w_key).astype(jnp.bfloat16)
    vals_self = (matmul(dec_row, w_value) + vectors[1]).astype(jnp.bfloat16)
    mixed_self, lse_self = attend_forward(
        split_heads(queries), split_heads(keys_self), split_heads(vals_self), seg_row
    )
    self_flat = merge_heads(mixed_self).astype(jnp.bfloat16)
    self_out = matmul(self_flat, w_proj) + vectors[2]
    hidden_one, normed_one, inv_one = norm_forward(dec_full + self_out, vectors[7], vectors[8])
    hidden_one_low = hidden_one.astype(jnp.bfloat16)
    cross_q = ((matmul(hidden_one_low, c_query) + vectors[3]) * scale).astype(jnp.bfloat16)
    cross_k = matmul(enc_row, c_key).astype(jnp.bfloat16)
    cross_v = (matmul(enc_row, c_value) + vectors[4]).astype(jnp.bfloat16)
    mixed_cross, lse_cross = attend_forward(
        split_heads(cross_q), split_heads(cross_k), split_heads(cross_v), None
    )
    cross_flat = merge_heads(mixed_cross).astype(jnp.bfloat16)
    cross_out = matmul(cross_flat, c_proj) + vectors[5]
    hidden_two, normed_two, inv_two = norm_forward(hidden_one + cross_out, vectors[9], vectors[10])
    hidden_two_low = hidden_two.astype(jnp.bfloat16)
    pre_act = contract_cols(hidden_two_low, w_in) + bias_in
    act_full, act_pull = jax.vjp(gelu_exact, pre_act)
    act_low = act_full.astype(jnp.bfloat16)
    ffn_out = matmul(act_low, w_out) + vectors[6]
    result, normed_three, inv_three = norm_forward(hidden_two + ffn_out, vectors[11], vectors[12])
    grad_r3, grad_g3, grad_e3 = norm_backward(cot_row, normed_three, inv_three, vectors[11])
    grad_y = grad_r3.astype(jnp.bfloat16)
    grad_w_out = contract_rows(act_low, grad_y)
    grad_act = contract_cols(grad_y, w_out)
    grad_pre = act_pull(grad_act)[0].astype(jnp.bfloat16)
    grad_w_in = contract_rows(grad_pre, hidden_two_low)
    grad_h2 = grad_r3 + matmul(grad_pre, w_in)
    grad_r2, grad_g2, grad_e2 = norm_backward(grad_h2, normed_two, inv_two, vectors[9])
    grad_co = grad_r2.astype(jnp.bfloat16)
    grad_c_proj = contract_rows(cross_flat, grad_co)
    grad_mix_c = contract_cols(grad_co, c_proj).astype(jnp.bfloat16)
    grad_q_c, grad_k_c, grad_v_c = attend_backward(
        split_heads(cross_q),
        split_heads(cross_k),
        split_heads(cross_v),
        None,
        lse_cross,
        split_heads(grad_mix_c),
    )
    grad_cq = merge_heads(grad_q_c) * scale
    grad_ck = merge_heads(grad_k_c)
    grad_cv = merge_heads(grad_v_c)
    grad_c_query = contract_rows(hidden_one_low, grad_cq)
    grad_h1 = grad_r2 + contract_cols(grad_cq, c_query)
    grad_r1, grad_g1, grad_e1 = norm_backward(grad_h1, normed_one, inv_one, vectors[7])
    grad_so = grad_r1.astype(jnp.bfloat16)
    grad_w_proj = contract_rows(self_flat, grad_so)
    grad_mix_s = contract_cols(grad_so, w_proj).astype(jnp.bfloat16)
    grad_q_s, grad_k_s, grad_v_s = attend_backward(
        split_heads(queries),
        split_heads(keys_self),
        split_heads(vals_self),
        seg_row,
        lse_self,
        split_heads(grad_mix_s),
    )
    grad_sq = merge_heads(grad_q_s) * scale
    grad_sk = merge_heads(grad_k_s)
    grad_sv = merge_heads(grad_v_s)
    grad_w_query = contract_rows(dec_row, grad_sq)
    grad_w_key = contract_rows(dec_row, grad_sk)
    grad_w_value = contract_rows(dec_row, grad_sv)
    grad_input = (
        grad_r1
        + contract_cols(grad_sq, w_query)
        + contract_cols(grad_sk, w_key)
        + contract_cols(grad_sv, w_value)
    )
    vec_rows = jnp.stack(
        [
            column_sum(grad_sq),
            column_sum(grad_sv),
            column_sum(grad_so),
            column_sum(grad_cq),
            column_sum(grad_cv),
            column_sum(grad_co),
            column_sum(grad_y),
            grad_g1,
            grad_e1,
            grad_g2,
            grad_e2,
            grad_g3,
            grad_e3,
        ]
    )
    vec_grad = jnp.concatenate([vec_rows, column_sum(grad_pre).reshape(-1, vectors.shape[1])], 0)
    row_mats = (grad_w_query, grad_w_key, grad_w_value, grad_w_proj, grad_c_query, grad_c_proj)
    return (result, grad_input, grad_ck, grad_cv, row_mats, grad_w_in, grad_w_out, vec_grad)


def nesterov(master, moment, average, grad, rate):
    new_moment = MOMENTUM * moment + grad
    new_master = master - rate * (grad + MOMENTUM * new_moment)
    new_average = AVG_DECAY * average + (1.0 - AVG_DECAY) * new_master
    return (new_master, new_moment, new_average)


def local(
    decoder_in,
    encoder_out,
    segment_ids,
    cotangent,
    attn_master,
    ffn_master,
    small_master,
    attn_moment,
    ffn_moment,
    small_moment,
    attn_average,
    ffn_average,
    small_average,
    rate_matrix,
    rate_vector,
):
    if (
        lax.axis_size(DP) == 16
        and attn_master.shape[0] > CUT and attn_master.shape[0] % 32 == 0
        and decoder_in.shape[0] == 1
        and encoder_out.shape[1] == 2 * decoder_in.shape[1]
    ):
        got = mega_call(
            decoder_in[0], encoder_out[0], segment_ids, cotangent[0], attn_master, ffn_master, small_master
        )
        layer_out, input_grad = (got[name][None].astype(F32) for name in ("lo_got", "ig_got"))
        encoder_grad = got[ENC_GRAD][None]
        attn_grad, ffn_grad = (
            got[name].astype(F32) + got[name + _MORE].astype(F32) for name in (ATTN_GRAD, FFN_GRAD)
        )
        small_grad = got["small_grad"][: small_master.shape[0]]
    else:
        matrices, ffn_all = (
            lax.all_gather(attn_master.astype(jnp.bfloat16), (SIDE, DP), axis=0, tiled=True),
            lax.all_gather(ffn_master.astype(jnp.bfloat16), (SIDE, DP), axis=0, tiled=True),
        )
        model_width = matrices.shape[1]
        hidden_units = ffn_all.shape[0] // 2
        blocks = [
            matrices[block_index * model_width : (block_index + 1) * model_width]
            for block_index in range(8)
        ]
        w_in = ffn_all[:hidden_units]
        w_out = ffn_all[hidden_units:]
        partner_enc = partner(encoder_out, SIDE, 0)
        mat_grads = [jnp.zeros((model_width, model_width), jnp.float32) for block_index in range(8)]
        slots = (0, 1, 2, 3, 4, 7)
        row_index = 0
        outcome = layer_row(
            decoder_in[row_index],
            partner_enc[row_index],
            segment_ids[row_index],
            cotangent[row_index],
            blocks,
            w_in,
            w_out,
            small_master,
        )
        result, grad_input, grad_ck, grad_cv, row_mats, grad_w_in, grad_w_out, vec_grad = outcome
        layer_out = result[None]
        input_grad = grad_input[None]
        key_grads = [grad_ck]
        value_grads = [grad_cv]
        for slot_index, slot_grad in zip(slots, row_mats):
            mat_grads[slot_index] = slot_grad
        returned = partner(jnp.stack([jnp.stack(key_grads), jnp.stack(value_grads)]), SIDE, 0)
        row_index = 0
        own_rows = encoder_out[row_index]
        mat_grads[5] = contract_rows(own_rows, returned[0, row_index])
        mat_grads[6] = contract_rows(own_rows, returned[1, row_index])
        enc_grads = [
            contract_cols(returned[0, row_index], blocks[5])
            + contract_cols(returned[1, row_index], blocks[6])
        ]
        encoder_grad = jnp.stack(enc_grads)
        attn_total = jnp.concatenate(mat_grads, 0)
        ffn_total = jnp.concatenate([grad_w_in, grad_w_out], 0)
        attn_grad, ffn_grad = (
            lax.psum_scatter(attn_total, (SIDE, DP), scatter_dimension=0, tiled=True),
            lax.psum_scatter(ffn_total, (SIDE, DP), scatter_dimension=0, tiled=True),
        )
        small_grad = lax.psum(vec_grad, (SIDE, DP))
    attn_new, attn_moment_new, attn_average_new = nesterov(
        attn_master, attn_moment, attn_average, attn_grad, rate_matrix
    )
    ffn_new, ffn_moment_new, ffn_average_new = nesterov(
        ffn_master, ffn_moment, ffn_average, ffn_grad, rate_matrix
    )
    small_new, small_moment_new, small_average_new = nesterov(
        small_master, small_moment, small_average, small_grad, rate_vector
    )
    return (
        layer_out,
        input_grad,
        encoder_grad,
        attn_grad,
        ffn_grad,
        small_grad,
        attn_new,
        ffn_new,
        small_new,
        attn_moment_new,
        ffn_moment_new,
        small_moment_new,
        attn_average_new,
        ffn_average_new,
        small_average_new,
    )


def solution(mesh):
    placed = (
        P((SIDE, DP), None, None),
        P((SIDE, DP), None, None),
        P((SIDE, DP), None),
        P((SIDE, DP), None, None),
        P((SIDE, DP), None),
        P((SIDE, DP), None),
        P(),
        P((SIDE, DP), None),
        P((SIDE, DP), None),
        P(),
        P((SIDE, DP), None),
        P((SIDE, DP), None),
        P(),
        P(),
        P(),
    )
    return jax.shard_map(
        local,
        mesh=mesh,
        in_specs=placed,
        out_specs=(
            P((SIDE, DP), None, None),
            P((SIDE, DP), None, None),
            P((SIDE, DP), None, None),
            P((SIDE, DP), None),
            P((SIDE, DP), None),
            P(),
            P((SIDE, DP), None),
            P((SIDE, DP), None),
            P(),
            P((SIDE, DP), None),
            P((SIDE, DP), None),
            P(),
            P((SIDE, DP), None),
            P((SIDE, DP), None),
            P(),
        ),
        check_vma=False,
    )
```
